256 devices in a mesh: grp: 4 (over y), gz: 64 (over x, z, core).
Axes of the slice: x: 4, y: 4, z: 8, core: 2. Of those that a mesh axis runs over, the one named last changes fastest.
Arguments:
- features: bfloat16 [32768, 256], P(('grp', 'gz')), may hold values from -6 to 6
- hilbert_rank: int32 [32768], P(('grp', 'gz')), may hold values from 0 to 8191, as said below
- neighbours: int32 [32768, 27], P(('grp', 'gz')), may hold values from -1 to 159, as said below
- halo_rows: int32 [256, 32], P(('grp', 'gz')), may hold values from 0 to 127, as said below
- cotangent: bfloat16 [32768, 256], P(('grp', 'gz')), may hold values from -6 to 6
- conv_weight: bfloat16 [6912, 256], replicated, may hold values from -0.078125 to 0.078125
- qkv_weight: bfloat16 [256, 768], replicated, may hold values from -0.375 to 0.375
- proj_weight: bfloat16 [256, 256], replicated, may hold values from -0.375 to 0.375
- norm_gain: float32 [256], replicated, may hold values from 0.25 to 1.75
Outputs:
- block_out: bfloat16 [32768, 256], P(('grp', 'gz'))
- grad_features: bfloat16 [32768, 256], P(('grp', 'gz'))
- grad_conv: float32 [6912, 256], P('gz')
- grad_qkv: float32 [256, 768], replicated
- grad_proj: float32 [256, 256], replicated
- grad_gain: float32 [256], replicated
The draws below stay inside these ranges and needn't reach their ends.
Inputs may be any that keep to these rules, and one draw needn't show every extreme that they name: `hilbert_rank`: within each group the 8192 ranks are a permutation. Ranks k * 128 to (k + 1) * 128 - 1 are held in Hilbert order by index k of gz, and indices 2i and 2i + 1 hold patch i. At most 4 points of one device have ranks in one such range, and every device has exactly 4 in some range. `neighbours`: -1 marks an absent neighbour. Otherwise the entry indexes the device's extended rows: its 128 own rows, then 16 rows from the previous index of gz, then 16 from the next; entries of the last two kinds occur only where that device exists. Offset 13 is the point itself. `halo_rows`: row indices of the device's own points: the first 16 entries go to the previous index of gz, the last 16 to the next; repeats may occur.
All inputs are finite; a program needn't handle non-finite values.
Results may differ from the reference program's by a relative error of at most 0.014.
Values may be sent and summed in bfloat16 or wider, within the bound.
No kernel may reach another device: no remote copies, remote signals or barrier semaphores. Data moves between devices by JAX's collectives and lax.ppermute only.
A program may use at most 64 MiB of HBM per device.

```python
import math
import jax
import jax.numpy as jnp
from jax import lax

D = 256
HEADS = 16
OFFSETS = 27
P_DEV = 128
SHARDS = 64
GROUPS = 4
HALO = 16
TOKENS = 32768


def pair_counts(key):
    unit = P_DEV // SHARDS
    half = SHARDS // 2
    shifts = jax.random.randint(key, (half - 1,), -unit, unit + 1).astype(jnp.int32)
    pattern = jnp.concatenate([jnp.zeros((1,), jnp.int32), unit + shifts, jnp.full((1,), 2 * unit, jnp.int32), unit - shifts[::-1]])
    lag_table = (jnp.arange(SHARDS)[None, :] - jnp.arange(SHARDS)[:, None]) % SHARDS
    return pattern[lag_table]


def group_ranks(key):
    counts = pair_counts(jax.random.fold_in(key, 1))
    row_end = jnp.cumsum(counts, 1)
    row_start = row_end - counts
    col_start = jnp.cumsum(counts, 0) - counts
    source_keys = jax.random.split(jax.random.fold_in(key, 2), SHARDS)
    send_order = jax.vmap(lambda sub_key: jax.random.permutation(sub_key, P_DEV))(source_keys)
    owner_index = jnp.sum(row_end[:, None, :] <= send_order[:, :, None], 2)
    source_index = jnp.broadcast_to(jnp.arange(SHARDS)[:, None], (SHARDS, P_DEV))
    slot_index = send_order - row_start[source_index, owner_index]
    arrival = col_start[source_index, owner_index] + slot_index
    owner_keys = jax.random.split(jax.random.fold_in(key, 3), SHARDS)
    final_order = jax.vmap(lambda sub_key: jax.random.permutation(sub_key, P_DEV))(owner_keys)
    local_rank = final_order[owner_index, arrival]
    return (owner_index * P_DEV + local_rank).reshape(-1)


def draw_hilbert_rank(key, part):
    key = jax.random.fold_in(key, 5)
    ranks = jax.vmap(lambda group_id: group_ranks(jax.random.fold_in(key, group_id)))(jnp.arange(GROUPS))
    return ranks.reshape(-1).astype(jnp.int32)


def draw_halo_rows(key, part):
    key = jax.random.fold_in(key, 11)

    def one_device(sub_key):
        key_down, key_up = jax.random.split(sub_key)
        down_list = jax.random.permutation(key_down, P_DEV // 4)[:HALO].at[0].set(0)
        up_list = P_DEV - 1 - jax.random.permutation(key_up, P_DEV // 4)[:HALO].at[0].set(0)
        return jnp.concatenate([down_list, up_list])
    return jax.vmap(one_device)(jax.random.split(key, GROUPS * SHARDS)).astype(jnp.int32)


def draw_neighbours(key, part):
    key = jax.random.fold_in(key, 7)
    key_near, key_kind, key_rim = jax.random.split(key, 3)
    point_id = jnp.arange(TOKENS)
    row_index = point_id % P_DEV
    shard_index = point_id // P_DEV % SHARDS
    nearby = jnp.clip(row_index[:, None] + jax.random.randint(key_near, (TOKENS, OFFSETS), -32, 33), 0, P_DEV - 1)
    kind_draw = jax.random.randint(key_kind, (TOKENS, OFFSETS), 0, 10)
    rim_pick = jax.random.randint(key_rim, (TOKENS, OFFSETS), 0, HALO)
    low_side = ((row_index < HALO) & (shard_index > 0))[:, None]
    high_side = ((row_index >= P_DEV - HALO) & (shard_index < SHARDS - 1))[:, None]
    table = jnp.where(kind_draw < 3, -1, nearby)
    table = jnp.where((kind_draw >= 7) & low_side, P_DEV + rim_pick, table)
    table = jnp.where((kind_draw >= 7) & high_side, P_DEV + HALO + rim_pick, table)
    table = table.at[:, 13].set(row_index)
    table = table.at[:, 0].set(jnp.where(high_side[:, 0] & (row_index == P_DEV - 1), P_DEV + 2 * HALO - 1, table[:, 0]))
    table = table.at[:, 1].set(jnp.where(row_index == 0, -1, table[:, 1]))
    return table.astype(jnp.int32)


def block_scale(key, extent, cuts, least, largest):
    loudness = 1.0
    for axis_at, parts in cuts:
        draws = jax.random.uniform(jax.random.fold_in(jax.random.fold_in(key, 6), axis_at), (parts,), jnp.float32, least / len(cuts), largest / len(cuts))
        loudness = loudness * jnp.repeat(jnp.exp(draws), extent[axis_at] // parts).reshape((-1,) + (1,) * (len(extent) - 1 - axis_at))
    return loudness


def gaussian(stream_key, dims, deviation, reach, cuts=(), held_as=jnp.bfloat16):
    values = jax.random.normal(stream_key, dims, jnp.float32) * deviation
    if len(cuts) > 0:
        values = block_scale(stream_key, dims, cuts, -0.22, 0.18) * values
    return jnp.clip(values, min=-reach, max=reach).astype(held_as)


def setup_inputs(seed: int = 0) -> dict:
    key_list = jax.random.split(jax.random.key(seed), 10)
    features = gaussian(key_list[0], (TOKENS, D), 1.0, 6.0, ((0, 256),))
    hilbert_rank = draw_hilbert_rank(jax.random.fold_in(key_list[9], 71), 0)
    neighbours = draw_neighbours(jax.random.fold_in(key_list[9], 71), 0)
    halo_rows = draw_halo_rows(jax.random.fold_in(key_list[9], 71), 0)
    cotangent = gaussian(key_list[4], (TOKENS, D), 1.0, 6.0, ((0, 256),))
    conv_weight = gaussian(key_list[5], (OFFSETS * D, D), (OFFSETS * D) ** -0.5, 0.078125)
    qkv_weight = gaussian(key_list[6], (D, 3 * D), D ** -0.5, 0.375)
    proj_weight = gaussian(key_list[7], (D, D), D ** -0.5, 0.375)
    norm_gain = jnp.clip(1.0 + 0.15 * jax.random.normal(key_list[8], (D,), jnp.float32), 0.25, 1.75)
    return dict(features=features, hilbert_rank=hilbert_rank, neighbours=neighbours, halo_rows=halo_rows, cotangent=cotangent, conv_weight=conv_weight, qkv_weight=qkv_weight, proj_weight=proj_weight, norm_gain=norm_gain)


norm_eps = 1e-05

def neighbour_rows(extended, neighbours):
    present = neighbours >= 0
    picked = extended[jnp.where(present, neighbours, 0)]
    picked = jnp.where(present[:, :, None], picked, jnp.zeros((), extended.dtype))
    return picked.reshape(neighbours.shape[0], -1)

def contract_rows(left_side, right_side):
    return lax.dot_general(left_side, right_side, (((0,), (0,)), ((), ())), preferred_element_type=jnp.float32)

def contract_cols(left_side, right_side):
    return lax.dot_general(left_side, right_side, (((1,), (1,)), ((), ())), preferred_element_type=jnp.float32)

def rounded(values):
    return lax.optimization_barrier(values.astype(jnp.bfloat16)).astype(jnp.float32)

def pair_work(mixed_pair, cot_pair, norm_gain, qkv_weight, proj_weight):
    point_count = mixed_pair.shape[1]
    feat_width = mixed_pair.shape[2]
    head_dim = feat_width // HEADS
    score_scale = head_dim ** (-0.5)
    hidden = mixed_pair.astype(jnp.float32)
    centred = hidden - lax.optimization_barrier(jnp.mean(hidden, -1, keepdims=True))
    inverse = lax.rsqrt(lax.optimization_barrier(jnp.mean(centred * centred, -1, keepdims=True)) + norm_eps)
    normed = centred * inverse
    scaled = (normed * norm_gain).astype(jnp.bfloat16).reshape(2 * point_count, feat_width)
    projected = jnp.dot(scaled, qkv_weight, preferred_element_type=jnp.float32).astype(jnp.bfloat16)
    query_heads = projected[:, :feat_width].reshape(2, point_count, HEADS, head_dim).astype(jnp.float32)
    key_heads = projected[:, feat_width:2 * feat_width].reshape(2 * point_count, HEADS, head_dim).astype(jnp.float32)
    value_heads = projected[:, 2 * feat_width:].reshape(2 * point_count, HEADS, head_dim).astype(jnp.float32)
    scores = jnp.einsum('sqhd,khd->shqk', query_heads, key_heads) * score_scale
    exp_scores = jnp.exp(scores)
    attn_probs = rounded(exp_scores / lax.optimization_barrier(jnp.sum(exp_scores, -1, keepdims=True)))
    attended = jnp.einsum('shqk,khd->sqhd', attn_probs, value_heads).reshape(2 * point_count, feat_width).astype(jnp.bfloat16)
    cot_flat = cot_pair.reshape(2 * point_count, feat_width)
    result = (hidden.reshape(2 * point_count, feat_width) + jnp.dot(attended, proj_weight, preferred_element_type=jnp.float32)).astype(jnp.bfloat16)
    grad_proj = contract_rows(attended, cot_flat)
    grad_attended = rounded(contract_cols(cot_flat, proj_weight)).reshape(2, point_count, HEADS, head_dim)
    grad_probs = jnp.einsum('sqhd,khd->shqk', grad_attended, value_heads)
    row_delta = lax.optimization_barrier(jnp.sum(attn_probs * grad_probs, -1, keepdims=True))
    grad_scores = rounded(attn_probs * (grad_probs - row_delta) * score_scale)
    grad_query = jnp.einsum('shqk,khd->sqhd', grad_scores, key_heads).reshape(2 * point_count, feat_width).astype(jnp.bfloat16)
    grad_keys = jnp.einsum('shqk,sqhd->skhd', grad_scores, query_heads).reshape(2, 2 * point_count, feat_width).astype(jnp.bfloat16)
    grad_values = jnp.einsum('shqk,sqhd->skhd', attn_probs, grad_attended).reshape(2, 2 * point_count, feat_width).astype(jnp.bfloat16)
    grad_keyval = jnp.concatenate([grad_keys, grad_values], -1)
    w_query = qkv_weight[:, :feat_width]
    w_keyval = qkv_weight[:, feat_width:]
    grad_qkv = jnp.concatenate([contract_rows(scaled, grad_query), contract_rows(scaled, grad_keyval[0]) + contract_rows(scaled, grad_keyval[1])], 1)
    grad_scaled = contract_cols(grad_query, w_query) + contract_cols(grad_keyval[0], w_keyval) + contract_cols(grad_keyval[1], w_keyval)
    grad_scaled = grad_scaled.reshape(2, point_count, feat_width)
    grad_gain = lax.optimization_barrier(jnp.sum(grad_scaled * normed, (0, 1)))
    grad_normed = grad_scaled * norm_gain
    grad_hidden = (grad_normed - lax.optimization_barrier(jnp.mean(grad_normed, -1, keepdims=True)) - normed * lax.optimization_barrier(jnp.mean(grad_normed * normed, -1, keepdims=True))) * inverse
    grad_mixed = (cot_pair.astype(jnp.float32) + grad_hidden).astype(jnp.bfloat16)
    return (result.reshape(2, point_count, feat_width), grad_mixed, grad_proj, grad_qkv, grad_gain)

def reference(features, hilbert_rank, neighbours, halo_rows, cotangent, conv_weight, qkv_weight, proj_weight, norm_gain):
    devices = GROUPS * SHARDS
    points = features.reshape(devices, P_DEV, D)
    sent_rows = jax.vmap(lambda block_rows, pick_rows: block_rows[pick_rows])(points, halo_rows).reshape(GROUPS, SHARDS, 2 * HALO, D)
    empty_rim = jnp.zeros((GROUPS, 1, HALO, D), jnp.bfloat16)
    from_prev = jnp.concatenate([empty_rim, sent_rows[:, :-1, HALO:]], 1)
    from_next = jnp.concatenate([sent_rows[:, 1:, :HALO], empty_rim], 1)
    extended = jnp.concatenate([points.reshape(GROUPS, SHARDS, P_DEV, D), from_prev, from_next], 2).reshape(devices, P_DEV + 2 * HALO, D)
    tables = neighbours.reshape(devices, P_DEV, OFFSETS)

    def conv_forward(inputs):
        ext_block, table_rows, block_rows = inputs
        flat_rows = neighbour_rows(ext_block, table_rows)
        return (block_rows.astype(jnp.float32) + jnp.dot(flat_rows, conv_weight, preferred_element_type=jnp.float32)).astype(jnp.bfloat16)
    mixed_rows = lax.map(conv_forward, (extended, tables, points))
    rank_table = hilbert_rank.reshape(GROUPS, SHARDS * P_DEV)

    def to_hilbert(values):
        grouped = values.reshape(GROUPS, SHARDS * P_DEV, D)
        placed = jax.vmap(lambda block_rows, rank_order: jnp.zeros_like(block_rows).at[rank_order].set(block_rows))(grouped, rank_table)
        return placed.reshape(GROUPS * SHARDS // 2, 2, P_DEV, D)

    def from_hilbert(values):
        grouped = values.reshape(GROUPS, SHARDS * P_DEV, D)
        return jax.vmap(lambda block_rows, rank_order: block_rows[rank_order])(grouped, rank_table).reshape(devices, P_DEV, D)

    def pair_step(inputs):
        return pair_work(inputs[0], inputs[1], norm_gain, qkv_weight, proj_weight)
    results, grad_mixed, grad_proj, grad_qkv, grad_gain = lax.map(pair_step, (to_hilbert(mixed_rows), to_hilbert(cotangent)))
    block_out = from_hilbert(results)
    grad_mixed_z = from_hilbert(grad_mixed)

    def conv_backward(running_sum, inputs):
        ext_block, table_rows, grad_block = inputs
        flat_rows = neighbour_rows(ext_block, table_rows)
        running_sum = running_sum + contract_rows(flat_rows, grad_block)
        present = table_rows >= 0
        grad_flat = contract_cols(grad_block, conv_weight).reshape(P_DEV, OFFSETS, D)
        grad_flat = jnp.where(present[:, :, None], grad_flat, jnp.zeros((), jnp.float32))
        spread = jnp.zeros((P_DEV + 2 * HALO, D), jnp.float32).at[jnp.where(present, table_rows, 0)].add(grad_flat)
        return (running_sum, spread)
    grad_conv, spread = lax.scan(conv_backward, jnp.zeros((OFFSETS * D, D), jnp.float32), (extended, tables, grad_mixed_z))
    spread = spread.reshape(GROUPS, SHARDS, P_DEV + 2 * HALO, D)
    zero_rim = jnp.zeros((GROUPS, 1, HALO, D), jnp.float32)
    got_up = jnp.concatenate([spread[:, 1:, P_DEV:P_DEV + HALO], zero_rim], 1).reshape(devices, HALO, D)
    got_down = jnp.concatenate([zero_rim, spread[:, :-1, P_DEV + HALO:]], 1).reshape(devices, HALO, D)
    own_part = spread[:, :, :P_DEV].reshape(devices, P_DEV, D)

    def add_rims(block_rows, pick_rows, down_part, up_part):
        return block_rows.at[pick_rows[:HALO]].add(down_part).at[pick_rows[HALO:]].add(up_part)
    own_part = jax.vmap(add_rims)(own_part, halo_rows, got_down, got_up)
    grad_features = (grad_mixed_z.astype(jnp.float32) + own_part).astype(jnp.bfloat16)
    factor = 1.0 / math.sqrt(TOKENS)
    return (block_out.reshape(TOKENS, D), grad_features.reshape(TOKENS, D), grad_conv * factor, lax.optimization_barrier(jnp.sum(grad_qkv, 0)) * factor, lax.optimization_barrier(jnp.sum(grad_proj, 0)) * factor, lax.optimization_barrier(jnp.sum(grad_gain, 0)) * factor)
```

```python
import math

import jax
import jax.numpy as jnp
from jax import lax
from jax.experimental import pallas as pl
from jax.experimental.pallas import tpu as pltpu
from jax.sharding import PartitionSpec as P

HEADS = 16
NORM_EPS = 1e-05
BF = jnp.bfloat16
F32 = jnp.float32
I32 = jnp.int32

PTS = 128
FEAT = 256
OFFS = 27
RIM = 16
EXT = PTS + 2 * RIM
SLOTS = 512
PAY = 304
VMEM_LIMIT = 48 * 1024 * 1024

NX, NZ, NC = 4, 8, 2
Z_GROUPS = [[x * 16 + z * 2 + c for z in range(NZ)] for x in range(NX) for c in range(NC)]
XC_GROUPS = [[x * 16 + z * 2 + c for x in range(NX) for c in range(NC)] for z in range(NZ)]
SWAP = [(i, i ^ 1) for i in range(NX * NZ * NC)]
UP = [(i, i + 1) for i in range(NX * NZ * NC - 1)]
DOWN = [(i + 1, i) for i in range(NX * NZ * NC - 1)]


def mm(a, b):
    return jnp.dot(a, b, preferred_element_type=F32)


def mm_t(a, b):
    return lax.dot_general(a, b, (((1,), (1,)), ((), ())), preferred_element_type=F32)


def t_mm(a, b):
    return lax.dot_general(a, b, (((0,), (0,)), ((), ())), preferred_element_type=F32)


def one_hot(cond):
    return jnp.where(cond, 1.0, 0.0).astype(BF)


def iota(shape, dim):
    return lax.broadcasted_iota(I32, shape, dim)


def call(body, out_shape, *args, scratch=(), flops=1 << 26, nbytes=1 << 20, smem=0):
    specs = [pl.BlockSpec(memory_space=pltpu.SMEM)] * smem
    specs += [pl.BlockSpec(memory_space=pltpu.VMEM)] * (len(args) - smem)
    single = not isinstance(out_shape, (list, tuple))
    outs = [out_shape] if single else list(out_shape)
    got = pl.pallas_call(
        body,
        out_shape=outs,
        in_specs=specs,
        out_specs=[pl.BlockSpec(memory_space=pltpu.VMEM)] * len(outs),
        scratch_shapes=list(scratch),
        compiler_params=pltpu.CompilerParams(vmem_limit_bytes=VMEM_LIMIT),
        cost_estimate=pl.CostEstimate(flops=flops, bytes_accessed=nbytes, transcendentals=0),
    )(*args)
    return got[0] if single else got


def sds(shape, dtype=BF):
    return jax.ShapeDtypeStruct(shape, dtype)


def pick_body(pick_ref, feat_ref, down_ref, up_ref):
    rows = jnp.broadcast_to(pick_ref[...], (PTS, 2 * RIM))
    hit = one_hot(rows == iota((PTS, 2 * RIM), 0))
    got = t_mm(hit, feat_ref[...]).astype(BF)
    down_ref[...] = got[:RIM]
    up_ref[...] = got[RIM:]


def slot_hits(rank_row):
    owner = lax.shift_right_logical(rank_row, 7)
    wide = jnp.broadcast_to(owner, (PTS, PTS))
    tall = jnp.transpose(wide)
    earlier = (wide == tall) & (iota((PTS, PTS), 0) < iota((PTS, PTS), 1))
    slot = jnp.sum(jnp.where(earlier, 1, 0), axis=0, keepdims=True)
    target = owner * 8 + slot
    rows = iota((SLOTS, PTS), 0)
    return one_hot(rows == target), one_hot(rows == target + 4)


def conv_body(feat_ref, prev_ref, next_ref, nbr_ref, rank_ref, cot_ref, weight_ref, send_ref, ext, wide):
    ext[:PTS] = feat_ref[...]
    ext[PTS : PTS + RIM] = prev_ref[...]
    ext[PTS + RIM : EXT] = next_ref[...]
    ext[EXT:] = jnp.zeros((FEAT - EXT, FEAT), BF)
    rows = ext[...]
    lanes = iota((PTS, FEAT), 1)
    for k in range(OFFS):
        hit = one_hot(nbr_ref[:, k : k + 1] == lanes)
        wide[:, k * FEAT : (k + 1) * FEAT] = mm(hit, rows).astype(BF)
    mixed = (feat_ref[...].astype(F32) + mm(wide[...], weight_ref[...])).astype(BF)
    rank_row = rank_ref[...]
    first, second = slot_hits(rank_row)
    place = jnp.transpose(jnp.broadcast_to(rank_row & (PTS - 1), (PTS, PTS))).astype(F32)
    send_ref[:, :FEAT] = (mm(first, mixed) + mm(second, cot_ref[...])).astype(BF)
    marks = mm(first, (place + 1.0).astype(BF)) + mm(second, (place + (PTS + 1.0)).astype(BF))
    send_ref[:, FEAT:] = marks.astype(BF)


def place_hits(marks):
    marks = marks.astype(F32)
    lanes = iota((SLOTS, PTS), 1).astype(F32)
    return one_hot(marks == lanes + 1.0), one_hot(marks == lanes + (PTS + 1.0))


def layer_norm(hidden):
    centred = hidden - jnp.mean(hidden, -1, keepdims=True)
    inverse = lax.rsqrt(jnp.mean(centred * centred, -1, keepdims=True) + NORM_EPS)
    return centred * inverse, inverse


def keyval_body(got_ref, qkv_ref, gain_ref, local_ref, kv_ref):
    first, second = place_hits(got_ref[:, FEAT:])
    rows = got_ref[:, :FEAT]
    hidden = t_mm(first, rows)
    local_ref[:PTS] = hidden.astype(BF)
    local_ref[PTS:] = t_mm(second, rows).astype(BF)
    normed, _ = layer_norm(hidden)
    scaled = (normed * gain_ref[...]).astype(BF)
    kv_ref[...] = mm(scaled, qkv_ref[:, FEAT:]).astype(BF)


def attend_body(
    local_ref, own_ref, far_ref, qkv_ref, proj_ref, gain_ref,
    out_ref, far_grad_ref, own_grad_ref, gq_ref, gp_ref,
    qm, am, pr, ds,
):
    head_dim = FEAT // HEADS
    hidden = local_ref[:PTS].astype(F32)
    cot = local_ref[PTS:]
    normed, _ = layer_norm(hidden)
    scaled = (normed * gain_ref[...]).astype(BF)
    query = mm(scaled, qkv_ref[:, :FEAT]).astype(BF)
    grad_att = mm_t(cot, proj_ref[...]).astype(BF)
    keys = jnp.concatenate([own_ref[:, :FEAT], far_ref[:, :FEAT]], 0)
    values = jnp.concatenate([own_ref[:, FEAT:], far_ref[:, FEAT:]], 0)
    head_of = iota((PTS, FEAT), 1) // head_dim
    zero = jnp.zeros((PTS, FEAT), BF)
    att = jnp.zeros((PTS, FEAT), F32)
    gq = jnp.zeros((PTS, FEAT), F32)
    scale = head_dim ** (-0.5)
    for h in range(HEADS):
        mine = head_of == h
        span = slice(h * PTS, (h + 1) * PTS)
        q_h = jnp.where(mine, query, zero)
        a_h = jnp.where(mine, grad_att, zero)
        qm[span] = q_h
        am[span] = a_h
        e = jnp.exp(mm_t(q_h, keys) * scale)
        probs = (e * (1.0 / jnp.sum(e, -1, keepdims=True))).astype(BF)
        pr[span] = probs
        att = jnp.where(mine, mm(probs, values), att)
        grad_probs = mm_t(a_h, values)
        wide = probs.astype(F32)
        delta = jnp.sum(wide * grad_probs, -1, keepdims=True)
        grad_scores = (wide * (grad_probs - delta) * scale).astype(BF)
        ds[span] = grad_scores
        gq = jnp.where(mine, mm(grad_scores, keys), gq)
    grad_key = t_mm(ds[...], qm[...]).astype(BF)
    grad_value = t_mm(pr[...], am[...]).astype(BF)
    own_grad_ref[:, :FEAT] = grad_key[:PTS]
    own_grad_ref[:, FEAT:] = grad_value[:PTS]
    far_grad_ref[:, :FEAT] = grad_key[PTS:]
    far_grad_ref[:, FEAT:] = grad_value[PTS:]
    attended = att.astype(BF)
    out_ref[...] = (hidden + mm(attended, proj_ref[...])).astype(BF)
    gq_ref[...] = gq.astype(BF)
    gp_ref[...] = t_mm(attended, cot).astype(BF)


def norm_body(
    got_ref, local_ref, out_ref, gq_ref, own_ref, near_ref, gp_ref, qkv_ref, gain_ref,
    back_ref, dense_ref, gg_ref,
):
    hidden = local_ref[:PTS].astype(F32)
    cot = local_ref[PTS:].astype(F32)
    gain = gain_ref[...]
    normed, inverse = layer_norm(hidden)
    scaled = (normed * gain).astype(BF)
    gq, own, near = gq_ref[...], own_ref[...], near_ref[...]
    w_query, w_keyval = qkv_ref[:, :FEAT], qkv_ref[:, FEAT:]
    grad_scaled = mm_t(gq, w_query) + mm_t(own, w_keyval) + mm_t(near, w_keyval)
    grad_kv = t_mm(scaled, own) + t_mm(scaled, near)
    dense_ref[:FEAT] = t_mm(scaled, gq).astype(BF)
    dense_ref[FEAT : 2 * FEAT] = grad_kv[:, :FEAT].astype(BF)
    dense_ref[2 * FEAT : 3 * FEAT] = grad_kv[:, FEAT:].astype(BF)
    dense_ref[3 * FEAT :] = gp_ref[...]
    gg_ref[...] = jnp.sum(grad_scaled * normed, 0, keepdims=True)
    grad_normed = grad_scaled * gain
    grad_hidden = (
        grad_normed
        - jnp.mean(grad_normed, -1, keepdims=True)
        - normed * jnp.mean(grad_normed * normed, -1, keepdims=True)
    ) * inverse
    grad_local = (cot + grad_hidden).astype(BF)
    first, second = place_hits(got_ref[:, FEAT:])
    back_ref[...] = (mm(first, out_ref[...]) + mm(second, grad_local)).astype(BF)


def spread_body(
    back_ref, rank_ref, feat_ref, prev_ref, next_ref, nbr_ref, gg_ref, weight_ref,
    block_ref, pay_ref, own_ref, down_ref, up_ref,
    acc,
):
    first, second = slot_hits(rank_ref[...])
    rows = back_ref[...]
    block_ref[...] = t_mm(first, rows).astype(BF)
    grad_f32 = t_mm(second, rows)
    grad = grad_f32.astype(BF)
    eye = one_hot(iota((PTS, PTS), 0) == iota((PTS, PTS), 1))
    table = t_mm(nbr_ref[...].astype(F32).astype(BF), eye)
    points = iota((EXT, PTS), 0).astype(F32)
    acc[...] = jnp.zeros((EXT, FEAT), F32)
    for k in range(OFFS):
        hit = one_hot(points == table[k : k + 1])
        term = mm(hit, grad).astype(BF)
        acc[...] += mm_t(term, weight_ref[k * FEAT : (k + 1) * FEAT])
    own_ref[...] = acc[:PTS] + grad_f32
    down_ref[...] = acc[PTS : PTS + RIM].astype(BF)
    up_ref[...] = acc[PTS + RIM :].astype(BF)
    pay_ref[:PTS] = grad
    pay_ref[PTS : 2 * PTS] = feat_ref[...]
    pay_ref[2 * PTS : 2 * PTS + RIM] = prev_ref[...]
    pay_ref[2 * PTS + RIM : 2 * PTS + 2 * RIM] = next_ref[...]
    gg = gg_ref[...]
    pay_ref[PTS + EXT :, :PTS] = table[:16].astype(BF)
    low = jnp.concatenate([table[16:27], jnp.zeros((5, PTS), F32)], 0)
    at = iota((16, PTS), 0)
    low = jnp.where(at == 12, gg[:, :PTS], jnp.where(at == 14, gg[:, PTS:], low))
    pay_ref[PTS + EXT :, PTS:] = low.astype(BF)


def rim_body(own_ref, down_ref, up_ref, pick_ref, out_ref):
    rows = jnp.broadcast_to(pick_ref[...], (PTS, 2 * RIM))
    hit = one_hot(rows == iota((PTS, 2 * RIM), 0))
    rims = jnp.concatenate([down_ref[...], up_ref[...]], 0)
    out_ref[...] = (own_ref[...] + mm(hit, rims)).astype(BF)


def kernel_grad_body(where_ref, all_ref, dense_ref, out_ref, tab, terms, total):
    first_offset = where_ref[0]
    first_row = where_ref[1]
    odd = where_ref[2]
    sources = NX * NC
    gain = jnp.zeros((1, FEAT), F32)
    exts = []
    for s in range(sources):
        at = s * PAY
        rows = all_ref[at + PTS + EXT : at + PAY].astype(F32)
        tab[s * 32 : s * 32 + 16] = rows[:, :PTS]
        tab[s * 32 + 16 : s * 32 + 32] = rows[:, PTS:]
        gain += jnp.concatenate([rows[12:13, PTS:], rows[14:15, PTS:]], 1)
        exts.append(all_ref[at + PTS : at + PTS + EXT])
    ext_t = jnp.transpose(jnp.concatenate(exts, 0))
    points = iota((EXT, PTS), 0).astype(F32)
    for k in range(8):
        for s in range(sources):
            hit = one_hot(points == tab[pl.ds(first_offset + (s * 32 + k), 1), :])
            terms[s * EXT : (s + 1) * EXT] = mm(hit, all_ref[s * PAY : s * PAY + PTS]).astype(BF)
        total[k * FEAT : (k + 1) * FEAT] = mm(ext_t, terms[...])
    total[8 * FEAT :] = jnp.zeros((16, FEAT), F32)
    dense = jnp.zeros((PTS, FEAT), F32)
    for s in range(sources):
        dense += dense_ref[s].astype(F32)
    at = iota((112, FEAT), 0)
    for z in range(NZ):
        wide = total[pl.ds(pl.multiple_of(first_row + z * 216, 8), 120), :]
        rows = jnp.where(odd == 1, wide[4:116], wide[:112])
        rows = jnp.where(at < 108, rows, jnp.where(at == 108, gain, 0.0))
        out_ref[z, :112] = rows.astype(BF)
        out_ref[z, 112:] = dense[z * 16 : (z + 1) * 16].astype(BF)


def sum_body(got_ref, out_ref):
    total = got_ref[0].astype(F32)
    for i in range(1, got_ref.shape[0]):
        total += got_ref[i].astype(F32)
    out_ref[...] = total.astype(BF)


def group_sum_body(factor, got_ref, conv_ref, gain_ref, dense_ref):
    total = got_ref[0].astype(F32)
    for i in range(1, got_ref.shape[0]):
        total += got_ref[i].astype(F32)
    conv_ref[...] = total[:108] * factor
    gain_ref[...] = total[108:109] * factor
    dense_ref[...] = total[112:]


def unfold_body(factor, got_ref, qkv_ref, proj_ref):
    for x in range(NX):
        for c in range(NC):
            for z in range(NZ):
                row = (x * 2 + c) * 128 + z * 16
                block = got_ref[pl.ds((x * 16 + z * 2 + c) * 16, 16), :] * factor
                part, at = row // FEAT, row % FEAT
                if part < 3:
                    qkv_ref[at : at + 16, part * FEAT : (part + 1) * FEAT] = block
                else:
                    proj_ref[at : at + 16] = block


def shards(
    features,
    hilbert_rank,
    neighbours,
    halo_rows,
    cotangent,
    conv_weight,
    qkv_weight,
    proj_weight,
    norm_gain,
):
    factor = 1.0 / math.sqrt(PTS * NX * NZ * NC * lax.axis_size("grp"))
    rank_row = hilbert_rank.reshape(1, PTS)
    gain_row = norm_gain.reshape(1, FEAT)
    to_prev, to_next = call(pick_body, [sds((RIM, FEAT))] * 2, halo_rows, features)
    from_prev = lax.ppermute(to_next, "gz", UP)
    from_next = lax.ppermute(to_prev, "gz", DOWN)
    send = call(
        conv_body,
        sds((SLOTS, FEAT + PTS)),
        features, from_prev, from_next, neighbours, rank_row, cotangent, conv_weight,
        scratch=[pltpu.VMEM((FEAT, FEAT), BF), pltpu.VMEM((PTS, OFFS * FEAT), BF)],
    )
    got = lax.all_to_all(
        send.reshape(64, 8, FEAT + PTS), "gz", split_axis=0, concat_axis=0, tiled=True
    ).reshape(SLOTS, FEAT + PTS)
    local, own_kv = call(
        keyval_body, [sds((2 * PTS, FEAT)), sds((PTS, 2 * FEAT))], got, qkv_weight, gain_row
    )
    far_kv = lax.ppermute(own_kv, "gz", SWAP)
    out_local, far_grad, own_grad, grad_query, grad_proj = call(
        attend_body,
        [sds((PTS, FEAT)), sds((PTS, 2 * FEAT)), sds((PTS, 2 * FEAT)), sds((PTS, FEAT)), sds((FEAT, FEAT))],
        local, own_kv, far_kv, qkv_weight, proj_weight, gain_row,
        scratch=[pltpu.VMEM((HEADS * PTS, FEAT), BF)] * 4,
    )
    near_grad = lax.ppermute(far_grad, "gz", SWAP)
    back, dense, grad_gain = call(
        norm_body,
        [sds((SLOTS, FEAT)), sds((4 * FEAT, FEAT)), sds((1, FEAT), F32)],
        got, local, out_local, grad_query, own_grad, near_grad, grad_proj, qkv_weight, gain_row,
    )
    returned = lax.all_to_all(
        back.reshape(64, 8, FEAT), "gz", split_axis=0, concat_axis=0, tiled=True
    ).reshape(SLOTS, FEAT)
    dense_parts = lax.all_to_all(
        dense.reshape(8, PTS, FEAT), "gz", split_axis=0, concat_axis=0,
        axis_index_groups=XC_GROUPS, tiled=True,
    )
    block_out, payload, own_part, rim_down, rim_up = call(
        spread_body,
        [sds((PTS, FEAT)), sds((PAY, FEAT)), sds((PTS, FEAT), F32), sds((RIM, FEAT)), sds((RIM, FEAT))],
        returned, rank_row, features, from_prev, from_next, neighbours, grad_gain, conv_weight,
        scratch=[pltpu.VMEM((EXT, FEAT), F32)],
    )
    got_down = lax.ppermute(rim_down, "gz", DOWN)
    got_up = lax.ppermute(rim_up, "gz", UP)
    grad_features = call(rim_body, sds((PTS, FEAT)), own_part, got_up, got_down, halo_rows)
    everyone = lax.all_gather(payload, "gz", axis_index_groups=XC_GROUPS, tiled=True)
    me = lax.axis_index("gz")
    odd = me % 2
    base = (me // 16) * 1728 + odd * 108
    first_offset = jnp.minimum(base // FEAT, OFFS - 8)
    where = jnp.stack([first_offset, base - first_offset * FEAT - odd * 4, odd]).astype(I32)
    parts = call(
        kernel_grad_body,
        sds((NZ, 128, FEAT)),
        where, everyone, dense_parts,
        scratch=[
            pltpu.VMEM((NX * NC * 32, PTS), F32),
            pltpu.VMEM((NX * NC * EXT, FEAT), BF),
            pltpu.VMEM((8 * FEAT + 16, FEAT), F32),
        ],
        smem=1,
    )
    z_parts = lax.all_to_all(
        parts, "gz", split_axis=0, concat_axis=0, axis_index_groups=Z_GROUPS, tiled=True
    )
    mine = call(sum_body, sds((128, FEAT)), z_parts)
    groups = lax.all_gather(mine, "grp")
    grad_conv, gain_sum, dense_rows = call(
        lambda *refs: group_sum_body(factor, *refs),
        [sds((108, FEAT), F32), sds((1, FEAT), F32), sds((16, FEAT), F32)],
        groups,
    )
    dense_all = lax.all_gather(dense_rows, "gz", tiled=True)
    grad_qkv, grad_proj_sum = call(
        lambda *refs: unfold_body(factor, *refs),
        [sds((FEAT, 3 * FEAT), F32), sds((FEAT, FEAT), F32)],
        dense_all,
    )
    return (
        block_out,
        grad_features,
        grad_conv,
        grad_qkv,
        grad_proj_sum,
        gain_sum.reshape(FEAT),
    )


def solution(mesh):
    return jax.shard_map(
        shards,
        mesh=mesh,
        in_specs=(
            P(("grp", "gz"), None),
            P(("grp", "gz")),
            P(("grp", "gz"), None),
            P(("grp", "gz"), None),
            P(("grp", "gz"), None),
            P(),
            P(),
            P(),
            P(),
        ),
        out_specs=(P(("grp", "gz"), None), P(("grp", "gz"), None), P("gz", None), P(), P(), P()),
        check_vma=False,
    )
```

```python
import math

import jax
import jax.numpy as jnp
from jax import lax
from jax.experimental import pallas as pl
from jax.experimental.pallas import tpu as pltpu
from jax.sharding import PartitionSpec as P

HEADS = 16
NORM_EPS = 1e-05
BF = jnp.bfloat16
F32 = jnp.float32
I32 = jnp.int32

PTS = 128
FEAT = 256
OFFS = 27
RIM = 16
EXT = PTS + 2 * RIM
SLOTS = 512
PAY = 256
VMEM_LIMIT = 48 * 1024 * 1024

NX, NZ, NC = 4, 8, 2
Z_GROUPS = [[x * 16 + z * 2 + c for z in range(NZ)] for x in range(NX) for c in range(NC)]
XC_GROUPS = [[x * 16 + z * 2 + c for x in range(NX) for c in range(NC)] for z in range(NZ)]
SWAP = [(i, i ^ 1) for i in range(NX * NZ * NC)]
UP = [(i, i + 1) for i in range(NX * NZ * NC - 1)]
DOWN = [(i + 1, i) for i in range(NX * NZ * NC - 1)]


def along_x(value, d):
    n = NX * NZ * NC
    return lax.ppermute(value, "gz", [(i, (i + 16 * d) % n) for i in range(n)])


def over_chips(value):
    near = [value] + [along_x(value, d) for d in range(1, NX)]
    return near + [lax.ppermute(v, "gz", SWAP) for v in near]


def mm(a, b):
    return jnp.dot(a, b, preferred_element_type=F32)


def mm_t(a, b):
    return lax.dot_general(a, b, (((1,), (1,)), ((), ())), preferred_element_type=F32)


def t_mm(a, b):
    return lax.dot_general(a, b, (((0,), (0,)), ((), ())), preferred_element_type=F32)


def one_hot(cond):
    return jnp.where(cond, 1.0, 0.0).astype(BF)


def iota(shape, dim):
    return lax.broadcasted_iota(I32, shape, dim)


def call(body, out_shape, *args, scratch=(), flops=1 << 26, nbytes=1 << 20, smem=0, fetched=(), late=()):
    fetched = tuple(fetched) + tuple(late)
    specs = []
    for i in range(len(args)):
        space = pltpu.SMEM if i < smem else pl.ANY if i in fetched else pltpu.VMEM
        specs.append(pl.BlockSpec(memory_space=space))
    single = not isinstance(out_shape, (list, tuple))
    outs = [out_shape] if single else list(out_shape)
    held = [pltpu.VMEM(args[i].shape, args[i].dtype) for i in fetched]
    held += [pltpu.SemaphoreType.DMA] * len(fetched)

    def outer(*refs):
        base = len(args) + len(outs) + len(scratch)
        views = list(refs[: len(args)])
        copies = {}
        for n, i in enumerate(fetched):
            copies[i] = pltpu.make_async_copy(refs[i], refs[base + n], refs[base + len(fetched) + n])
            copies[i].start()
            views[i] = refs[base + n]
        for i in fetched:
            if i in late:
                views[i] = (views[i], copies[i].wait)
            else:
                copies[i].wait()
        body(*views, *refs[len(args) : base])

    got = pl.pallas_call(
        outer,
        out_shape=outs,
        in_specs=specs,
        out_specs=[pl.BlockSpec(memory_space=pltpu.VMEM)] * len(outs),
        scratch_shapes=list(scratch) + held,
        compiler_params=pltpu.CompilerParams(vmem_limit_bytes=VMEM_LIMIT),
        cost_estimate=pl.CostEstimate(flops=flops, bytes_accessed=nbytes, transcendentals=0),
    )(*args)
    return got[0] if single else got


def sds(shape, dtype=BF):
    return jax.ShapeDtypeStruct(shape, dtype)


def pick_body(pick_ref, feat_ref, down_ref, up_ref):
    rows = jnp.broadcast_to(pick_ref[...], (PTS, 2 * RIM))
    hit = one_hot(rows == iota((PTS, 2 * RIM), 0))
    got = t_mm(hit, feat_ref[...]).astype(BF)
    down_ref[...] = got[:RIM]
    up_ref[...] = got[RIM:]


def slot_hits(rank_row):
    owner = lax.shift_right_logical(rank_row, 7)
    wide = jnp.broadcast_to(owner, (PTS, PTS))
    tall = jnp.transpose(wide)
    earlier = (wide == tall) & (iota((PTS, PTS), 0) < iota((PTS, PTS), 1))
    slot = jnp.sum(jnp.where(earlier, 1, 0), axis=0, keepdims=True)
    target = owner * 8 + slot
    rows = iota((SLOTS, PTS), 0)
    return one_hot(rows == target), one_hot(rows == target + 4)


def conv_body(feat_ref, prev_ref, next_ref, nbr_ref, rank_ref, cot_ref, weight, send_ref, ext, tab, wide):
    weight_ref, weight_here = weight
    ext[:PTS] = feat_ref[...]
    ext[PTS : PTS + RIM] = prev_ref[...]
    ext[PTS + RIM : EXT] = next_ref[...]
    ext[EXT:] = jnp.zeros((FEAT - EXT, FEAT), BF)
    rows = ext[...]
    tab[:OFFS] = nbr_ref[...].astype(F32)
    tab[OFFS:] = jnp.zeros((PTS - OFFS, PTS), F32)
    table = jnp.transpose(tab[...])
    lanes = iota((PTS, FEAT), 1).astype(F32)
    for k in range(OFFS):
        hit = one_hot(table[:, k : k + 1] == lanes)
        wide[:, k * FEAT : (k + 1) * FEAT] = mm(hit, rows).astype(BF)
    weight_here()
    mixed = (feat_ref[...].astype(F32) + mm(wide[...], weight_ref[...])).astype(BF)
    rank_row = rank_ref[...]
    first, second = slot_hits(rank_row)
    place = jnp.transpose(jnp.broadcast_to(rank_row & (PTS - 1), (PTS, PTS))).astype(F32)
    send_ref[:, :FEAT] = (mm(first, mixed) + mm(second, cot_ref[...])).astype(BF)
    marks = mm(first, (place + 1.0).astype(BF)) + mm(second, (place + (PTS + 1.0)).astype(BF))
    send_ref[:, FEAT:] = marks.astype(BF)


def place_hits(marks):
    marks = marks.astype(F32)
    lanes = iota((SLOTS, PTS), 1).astype(F32)
    return one_hot(marks == lanes + 1.0), one_hot(marks == lanes + (PTS + 1.0))


def layer_norm(hidden):
    centred = hidden - jnp.mean(hidden, -1, keepdims=True)
    inverse = lax.rsqrt(jnp.mean(centred * centred, -1, keepdims=True) + NORM_EPS)
    return centred * inverse, inverse


def keyval_body(got_ref, qkv_ref, gain_ref, local_ref, kv_ref):
    first, second = place_hits(got_ref[:, FEAT:])
    rows = got_ref[:, :FEAT]
    hidden = t_mm(first, rows)
    local_ref[:PTS] = hidden.astype(BF)
    local_ref[PTS:] = t_mm(second, rows).astype(BF)
    normed, _ = layer_norm(hidden)
    scaled = (normed * gain_ref[...]).astype(BF)
    kv_ref[...] = mm(scaled, qkv_ref[:, FEAT:]).astype(BF)


def attend_body(
    local_ref, own_ref, far_ref, qkv_ref, proj_ref, gain_ref,
    out_ref, far_grad_ref, own_grad_ref, gq_ref, gp_ref,
    qm, am, pr, ds, sc, gs,
):
    head_dim = FEAT // HEADS
    scale = head_dim ** (-0.5)
    hidden = local_ref[:PTS].astype(F32)
    cot = local_ref[PTS:]
    normed, _ = layer_norm(hidden)
    scaled = (normed * gain_ref[...]).astype(BF)
    query = mm(scaled, qkv_ref[:, :FEAT]).astype(BF)
    grad_att = mm_t(cot, proj_ref[...]).astype(BF)
    keys = jnp.concatenate([own_ref[:, :FEAT], far_ref[:, :FEAT]], 0)
    values = jnp.concatenate([own_ref[:, FEAT:], far_ref[:, FEAT:]], 0)
    head_of = iota((PTS, FEAT), 1) // head_dim
    zero = jnp.zeros((PTS, FEAT), BF)
    spans = [slice(h * PTS, (h + 1) * PTS) for h in range(HEADS)]
    for h in range(HEADS):
        qm[spans[h]] = jnp.where(head_of == h, query, zero)
        am[spans[h]] = jnp.where(head_of == h, grad_att, zero)
    sc[...] = mm_t(qm[...], keys)
    gs[...] = mm_t(am[...], values)
    for h in range(HEADS):
        e = jnp.exp(sc[spans[h]] * scale)
        probs = (e * (1.0 / jnp.sum(e, -1, keepdims=True))).astype(BF)
        pr[spans[h]] = probs
        wide = probs.astype(F32)
        grad_probs = gs[spans[h]]
        delta = jnp.sum(wide * grad_probs, -1, keepdims=True)
        ds[spans[h]] = (wide * (grad_probs - delta) * scale).astype(BF)
    sc[...] = mm(pr[...], values)
    gs[...] = mm(ds[...], keys)
    att = sc[spans[0]]
    gq = gs[spans[0]]
    for h in range(1, HEADS):
        att = jnp.where(head_of == h, sc[spans[h]], att)
        gq = jnp.where(head_of == h, gs[spans[h]], gq)
    grad_key = t_mm(ds[...], qm[...]).astype(BF)
    grad_value = t_mm(pr[...], am[...]).astype(BF)
    own_grad_ref[:, :FEAT] = grad_key[:PTS]
    own_grad_ref[:, FEAT:] = grad_value[:PTS]
    far_grad_ref[:, :FEAT] = grad_key[PTS:]
    far_grad_ref[:, FEAT:] = grad_value[PTS:]
    attended = att.astype(BF)
    out_ref[...] = (hidden + mm(attended, proj_ref[...])).astype(BF)
    gq_ref[...] = gq.astype(BF)
    gp_ref[...] = t_mm(attended, cot).astype(BF)


def attend(*args):
    return call(
        attend_body,
        [sds((PTS, FEAT)), sds((PTS, 2 * FEAT)), sds((PTS, 2 * FEAT)), sds((PTS, FEAT)), sds((FEAT, FEAT))],
        *args,
        scratch=[pltpu.VMEM((HEADS * PTS, FEAT), BF)] * 4 + [pltpu.VMEM((HEADS * PTS, FEAT), F32)] * 2,
    )


def norm_body(
    got_ref, local_ref, out_ref, gq_ref, own_ref, near_ref, gp_ref, qkv_ref, gain_ref,
    back_ref, dense_ref, gg_ref,
):
    hidden = local_ref[:PTS].astype(F32)
    cot = local_ref[PTS:].astype(F32)
    gain = gain_ref[...]
    normed, inverse = layer_norm(hidden)
    scaled = (normed * gain).astype(BF)
    gq, own, near = gq_ref[...], own_ref[...], near_ref[...]
    w_query, w_keyval = qkv_ref[:, :FEAT], qkv_ref[:, FEAT:]
    grad_scaled = mm_t(gq, w_query) + mm_t(own, w_keyval) + mm_t(near, w_keyval)
    grad_kv = t_mm(scaled, own) + t_mm(scaled, near)
    dense_ref[:FEAT] = t_mm(scaled, gq).astype(BF)
    dense_ref[FEAT : 2 * FEAT] = grad_kv[:, :FEAT].astype(BF)
    dense_ref[2 * FEAT : 3 * FEAT] = grad_kv[:, FEAT:].astype(BF)
    dense_ref[3 * FEAT :] = gp_ref[...]
    gg_ref[...] = jnp.sum(grad_scaled * normed, 0, keepdims=True)
    grad_normed = grad_scaled * gain
    grad_hidden = (
        grad_normed
        - jnp.mean(grad_normed, -1, keepdims=True)
        - normed * jnp.mean(grad_normed * normed, -1, keepdims=True)
    ) * inverse
    grad_local = (cot + grad_hidden).astype(BF)
    first, second = place_hits(got_ref[:, FEAT:])
    back_ref[...] = (mm(first, out_ref[...]) + mm(second, grad_local)).astype(BF)


def table_body(feat_ref, prev_ref, next_ref, nbr_ref, pay_ref):
    pay_ref[:PTS] = feat_ref[...]
    pay_ref[PTS : PTS + RIM] = prev_ref[...]
    pay_ref[PTS + RIM : EXT] = next_ref[...]
    table = nbr_ref[...].astype(F32)
    pay_ref[EXT : EXT + 16, :PTS] = table[:16].astype(BF)
    pay_ref[EXT : EXT + 16, PTS:] = jnp.concatenate([table[16:], jnp.zeros((5, PTS), F32)], 0).astype(BF)
    pay_ref[EXT + 16 :] = jnp.zeros((PAY - EXT - 16, FEAT), BF)


def unpack_body(back_ref, rank_ref, gg_ref, block_ref, grad_ref):
    first, second = slot_hits(rank_ref[...])
    rows = back_ref[...]
    grad_ref[:PTS] = t_mm(second, rows).astype(BF)
    grad_ref[PTS:] = jnp.broadcast_to(gg_ref[...], (16, FEAT)).astype(BF)
    block_ref[...] = t_mm(first, rows).astype(BF)


def spread_body(grad_ref, nbr_ref, weight_ref, own_ref, down_ref, up_ref, acc):
    grad = grad_ref[:PTS]
    table = nbr_ref[...].astype(F32)
    points = iota((EXT, PTS), 0).astype(F32)
    acc[...] = jnp.zeros((EXT, FEAT), F32)
    for k in range(OFFS):
        hit = one_hot(points == table[k : k + 1])
        term = mm(hit, grad).astype(BF)
        acc[...] += mm_t(term, weight_ref[k * FEAT : (k + 1) * FEAT])
    own_ref[...] = acc[:PTS] + grad.astype(F32)
    down_ref[...] = acc[PTS : PTS + RIM].astype(BF)
    up_ref[...] = acc[PTS + RIM :].astype(BF)


def rim_body(own_ref, down_ref, up_ref, pick_ref, out_ref):
    rows = jnp.broadcast_to(pick_ref[...], (PTS, 2 * RIM))
    hit = one_hot(rows == iota((PTS, 2 * RIM), 0))
    rims = jnp.concatenate([down_ref[...], up_ref[...]], 0)
    out_ref[...] = (own_ref[...] + mm(hit, rims)).astype(BF)


def kernel_grad_body(where_ref, all_ref, dense_ref, *refs):
    grads, (out_ref, tab, exts, terms, total) = refs[: NX * NC], refs[NX * NC :]
    first_offset = where_ref[0]
    first_row = where_ref[1]
    core = where_ref[2]
    x = where_ref[3]
    gain = jnp.zeros((1, FEAT), F32)
    for s in range(NX * NC):
        source = ((x + NX - s % NX) & (NX - 1)) * NC + (core if s < NX else 1 - core)
        rows = all_ref[source, EXT : EXT + 16].astype(F32)
        tab[s * 32 : s * 32 + 16] = rows[:, :PTS]
        tab[s * 32 + 16 : s * 32 + 32] = rows[:, PTS:]
        exts[s * EXT : (s + 1) * EXT] = all_ref[source, :EXT]
        gain += grads[s][PTS : PTS + 1].astype(F32)
    ext_t = jnp.transpose(exts[...])
    points = iota((EXT, PTS), 0).astype(F32)
    for k in range(8):
        for s in range(NX * NC):
            hit = one_hot(points == tab[pl.ds(first_offset + (s * 32 + k), 1), :])
            terms[s * EXT : (s + 1) * EXT] = mm(hit, grads[s][:PTS]).astype(BF)
        total[k * FEAT : (k + 1) * FEAT] = mm(ext_t, terms[...])
    total[8 * FEAT :] = jnp.zeros((16, FEAT), F32)
    at = iota((112, FEAT), 0)
    for z in range(NZ):
        wide = total[pl.ds(pl.multiple_of(first_row + z * 216, 8), 120), :]
        rows = jnp.where(core == 1, wide[4:116], wide[:112])
        rows = jnp.where(at < 108, rows, jnp.where(at == 108, gain, 0.0))
        out_ref[z, :112] = rows.astype(BF)
        out_ref[z, 112:] = dense_ref[...]


def sum_body(got_ref, out_ref):
    total = got_ref[0].astype(F32)
    for i in range(1, got_ref.shape[0]):
        total += got_ref[i].astype(F32)
    out_ref[...] = total.astype(BF)


def group_sum_body(factor, *refs):
    parts, (conv_ref, gain_ref, dense_ref) = refs[:4], refs[4:]
    total = parts[0][...].astype(F32)
    for part in parts[1:]:
        total += part[...].astype(F32)
    dense_ref[...] = total[112:].astype(BF)
    conv_ref[...] = total[:108] * factor
    gain_ref[...] = total[108:109] * factor


def unfold_body(factor, where_ref, *refs):
    parts, (qkv_ref, proj_ref, rows) = refs[: NX * NC], refs[NX * NC :]
    core = where_ref[2]
    x = where_ref[3]
    for s in range(NX * NC):
        source = ((x + NX - s % NX) & (NX - 1)) * NC + (core if s < NX else 1 - core)
        rows[source] = parts[s][...].astype(F32) * factor
    for b in range(NX * NC):
        part, at = b // 2, b % 2 * PTS
        if part < 3:
            qkv_ref[at : at + PTS, part * FEAT : (part + 1) * FEAT] = rows[b]
        else:
            proj_ref[at : at + PTS] = rows[b]


def shards(
    features,
    hilbert_rank,
    neighbours,
    halo_rows,
    cotangent,
    conv_weight,
    qkv_weight,
    proj_weight,
    norm_gain,
):
    factor = 1.0 / math.sqrt(PTS * NX * NZ * NC * lax.axis_size("grp"))
    rank_row = hilbert_rank.reshape(1, PTS)
    gain_row = norm_gain.reshape(1, FEAT)
    table = neighbours.T
    to_prev, to_next = call(
        pick_body, [sds((RIM, FEAT))] * 2, halo_rows, features, fetched=(0, 1)
    )
    from_prev = lax.ppermute(to_next, "gz", UP)
    from_next = lax.ppermute(to_prev, "gz", DOWN)
    me = lax.axis_index("gz")
    core = me % 2
    base = (me // 16) * 1728 + core * 108
    first_offset = jnp.minimum(base // FEAT, OFFS - 8)
    where = jnp.stack([first_offset, base - first_offset * FEAT - core * 4, core, me // 16]).astype(I32)
    payload = call(table_body, sds((PAY, FEAT)), features, from_prev, from_next, table)
    everyone = lax.all_gather(payload, "gz", axis_index_groups=XC_GROUPS)
    send = call(
        conv_body,
        sds((SLOTS, FEAT + PTS)),
        features, from_prev, from_next, table, rank_row, cotangent, conv_weight,
        scratch=[pltpu.VMEM((FEAT, FEAT), BF), pltpu.VMEM((PTS, PTS), F32), pltpu.VMEM((PTS, OFFS * FEAT), BF)],
        fetched=(0, 3, 4, 5), late=(6,),
    )
    got = lax.all_to_all(
        send.reshape(64, 8, FEAT + PTS), "gz", split_axis=0, concat_axis=0, tiled=True
    ).reshape(SLOTS, FEAT + PTS)
    local, own_kv = call(
        keyval_body, [sds((2 * PTS, FEAT)), sds((PTS, 2 * FEAT))], got, qkv_weight, gain_row
    )
    far_kv = lax.ppermute(own_kv, "gz", SWAP)
    out_local, far_grad, own_grad, grad_query, grad_proj = attend(
        local, own_kv, far_kv, qkv_weight, proj_weight, gain_row
    )
    near_grad = lax.ppermute(far_grad, "gz", SWAP)
    back, dense, grad_gain = call(
        norm_body,
        [sds((SLOTS, FEAT)), sds((4 * FEAT, FEAT)), sds((1, FEAT), F32)],
        got, local, out_local, grad_query, own_grad, near_grad, grad_proj, qkv_weight, gain_row,
    )
    dense_part = lax.psum_scatter(
        dense, "gz", scatter_dimension=0, axis_index_groups=XC_GROUPS, tiled=True
    )
    returned = lax.all_to_all(
        back.reshape(64, 8, FEAT), "gz", split_axis=0, concat_axis=0, tiled=True
    ).reshape(SLOTS, FEAT)
    block_out, grad = call(
        unpack_body, [sds((PTS, FEAT)), sds((PTS + 16, FEAT))], returned, rank_row, grad_gain
    )
    grads = over_chips(grad)
    own_part, rim_down, rim_up = call(
        spread_body,
        [sds((PTS, FEAT), F32), sds((RIM, FEAT)), sds((RIM, FEAT))],
        grad, table, conv_weight,
        scratch=[pltpu.VMEM((EXT, FEAT), F32)],
    )
    got_down = lax.ppermute(rim_down, "gz", DOWN)
    got_up = lax.ppermute(rim_up, "gz", UP)
    grad_features = call(rim_body, sds((PTS, FEAT)), own_part, got_up, got_down, halo_rows)
    parts = call(
        kernel_grad_body,
        sds((NZ, 240, FEAT)),
        where, everyone, dense_part, *grads,
        scratch=[
            pltpu.VMEM((NX * NC * 32, PTS), F32),
            pltpu.VMEM((NX * NC * EXT, FEAT), BF),
            pltpu.VMEM((NX * NC * EXT, FEAT), BF),
            pltpu.VMEM((8 * FEAT + 16, FEAT), F32),
        ],
        smem=1,
    )
    z_parts = lax.all_to_all(
        parts, "gz", split_axis=0, concat_axis=0, axis_index_groups=Z_GROUPS, tiled=True
    )
    mine = call(sum_body, sds((240, FEAT)), z_parts)
    groups = [mine] + [
        lax.ppermute(mine, "grp", [(i, (i + d) % 4) for i in range(4)]) for d in range(1, 4)
    ]
    grad_conv, gain_sum, dense_rows = call(
        lambda *refs: group_sum_body(factor, *refs),
        [sds((108, FEAT), F32), sds((1, FEAT), F32), sds((PTS, FEAT))],
        *groups,
    )
    grad_qkv, grad_proj_sum = call(
        lambda *refs: unfold_body(factor, *refs),
        [sds((FEAT, 3 * FEAT), F32), sds((FEAT, FEAT), F32)],
        where, *over_chips(dense_rows),
        scratch=[pltpu.VMEM((NX * NC, PTS, FEAT), F32)],
        smem=1,
    )
    return (
        block_out,
        grad_features,
        grad_conv,
        grad_qkv,
        grad_proj_sum,
        gain_sum.reshape(FEAT),
    )


def solution(mesh):
    return jax.shard_map(
        shards,
        mesh=mesh,
        in_specs=(
            P(("grp", "gz"), None),
            P(("grp", "gz")),
            P(("grp", "gz"), None),
            P(("grp", "gz"), None),
            P(("grp", "gz"), None),
            P(),
            P(),
            P(),
            P(),
        ),
        out_specs=(P(("grp", "gz"), None), P(("grp", "gz"), None), P("gz", None), P(), P(), P()),
        check_vma=False,
    )
```

```python
import math

import jax
import jax.numpy as jnp
from jax import lax
from jax.experimental import pallas as pl
from jax.experimental.pallas import tpu as pltpu
from jax.sharding import PartitionSpec as P

HEADS = 16
NORM_EPS = 1e-05
BF = jnp.bfloat16
F32 = jnp.float32
I32 = jnp.int32

PTS = 128
FEAT = 256
OFFS = 27
RIM = 16
EXT = PTS + 2 * RIM
SLOTS = 512
PAY = 256
MIB = 1024 * 1024

NX, NZ, NC = 4, 8, 2
Z_GROUPS = [[x * 16 + z * 2 + c for z in range(NZ)] for x in range(NX) for c in range(NC)]
XC_GROUPS = [[x * 16 + z * 2 + c for x in range(NX) for c in range(NC)] for z in range(NZ)]
XZ_GROUPS = [[x * 16 + z * 2 + c for x in range(NX) for z in range(NZ)] for c in range(NC)]
SWAP = [(i, i ^ 1) for i in range(NX * NZ * NC)]
UP = [(i, i + 1) for i in range(NX * NZ * NC - 1)]
DOWN = [(i + 1, i) for i in range(NX * NZ * NC - 1)]


def along_x(value, d):
    n = NX * NZ * NC
    return lax.ppermute(value, "gz", [(i, (i + 16 * d) % n) for i in range(n)])


def over_chips(value):
    near = [value] + [along_x(value, d) for d in range(1, NX)]
    return near + [lax.ppermute(v, "gz", SWAP) for v in near]


def over_groups(value):
    n = lax.axis_size("grp")
    return [value] + [lax.ppermute(value, "grp", [(i, (i + d) % n) for i in range(n)]) for d in range(1, n)]


def mm(a, b):
    return jnp.dot(a, b, preferred_element_type=F32)


def mm_t(a, b):
    return lax.dot_general(a, b, (((1,), (1,)), ((), ())), preferred_element_type=F32)


def t_mm(a, b):
    return lax.dot_general(a, b, (((0,), (0,)), ((), ())), preferred_element_type=F32)


def one_hot(cond):
    return jnp.where(cond, 1.0, 0.0).astype(BF)


def iota(shape, dim):
    return lax.broadcasted_iota(I32, shape, dim)


def call(body, out_shape, *args, scratch=(), flops=1 << 26, nbytes=1 << 20, smem=0, fetched=(), late=(), idle=(), limit=16):
    fetched = tuple(fetched) + tuple(late)
    specs = []
    for i in range(len(args)):
        space = pltpu.SMEM if i < smem else pltpu.HBM if i in fetched else pl.ANY if i in idle else pltpu.VMEM
        specs.append(pl.BlockSpec(memory_space=space))
    single = not isinstance(out_shape, (list, tuple))
    outs = [out_shape] if single else list(out_shape)
    held = [pltpu.VMEM(args[i].shape, args[i].dtype) for i in fetched]
    held += [pltpu.SemaphoreType.DMA] * len(fetched)

    def outer(*refs):
        base = len(args) + len(outs) + len(scratch)
        views = list(refs[: len(args)])
        copies = {}
        for n, i in enumerate(fetched):
            copies[i] = pltpu.make_async_copy(refs[i], refs[base + n], refs[base + len(fetched) + n])
            copies[i].start()
            views[i] = refs[base + n]
        for i in fetched:
            if i in late:
                views[i] = (views[i], copies[i].wait)
            else:
                copies[i].wait()
        body(*[v for i, v in enumerate(views) if i not in idle], *refs[len(args) : base])

    got = pl.pallas_call(
        outer,
        out_shape=outs,
        in_specs=specs,
        out_specs=[pl.BlockSpec(memory_space=pltpu.VMEM)] * len(outs),
        scratch_shapes=list(scratch) + held,
        compiler_params=pltpu.CompilerParams(vmem_limit_bytes=limit * MIB),
        cost_estimate=pl.CostEstimate(flops=flops, bytes_accessed=nbytes, transcendentals=0),
    )(*args)
    return got[0] if single else got


def sds(shape, dtype=BF):
    return jax.ShapeDtypeStruct(shape, dtype)


def position():
    me = lax.axis_index("gz")
    return lax.shift_right_logical(me, 4), me & 1


def pick_body(pick_ref, feat_ref, down_ref, up_ref):
    rows = jnp.broadcast_to(pick_ref[...], (PTS, 2 * RIM))
    hit = one_hot(rows == iota((PTS, 2 * RIM), 0))
    got = t_mm(hit, feat_ref[...]).astype(BF)
    down_ref[...] = got[:RIM]
    up_ref[...] = got[RIM:]


def slot_hits(rank_row):
    owner = lax.shift_right_logical(rank_row, 7)
    wide = jnp.broadcast_to(owner, (PTS, PTS))
    tall = jnp.transpose(wide)
    earlier = (wide == tall) & (iota((PTS, PTS), 0) < iota((PTS, PTS), 1))
    slot = jnp.sum(jnp.where(earlier, 1, 0), axis=0, keepdims=True)
    target = owner * 8 + slot
    rows = iota((SLOTS, PTS), 0)
    return one_hot(rows == target), one_hot(rows == target + 4)


def conv_body(feat_ref, prev_ref, next_ref, nbr_ref, rank_ref, cot_ref, weight, send_ref, ext, tab, wide):
    weight_ref, weight_here = weight
    ext[:PTS] = feat_ref[...]
    ext[PTS : PTS + RIM] = prev_ref[...]
    ext[PTS + RIM : EXT] = next_ref[...]
    ext[EXT:] = jnp.zeros((FEAT - EXT, FEAT), BF)
    rows = ext[...]
    tab[:OFFS] = nbr_ref[...].astype(F32)
    tab[OFFS:] = jnp.zeros((PTS - OFFS, PTS), F32)
    table = jnp.transpose(tab[...])
    lanes = iota((PTS, FEAT), 1).astype(F32)
    for k in range(OFFS):
        hit = one_hot(table[:, k : k + 1] == lanes)
        wide[:, k * FEAT : (k + 1) * FEAT] = mm(hit, rows).astype(BF)
    weight_here()
    mixed = (feat_ref[...].astype(F32) + mm(wide[...], weight_ref[...])).astype(BF)
    rank_row = rank_ref[...]
    first, second = slot_hits(rank_row)
    place = jnp.transpose(jnp.broadcast_to(rank_row & (PTS - 1), (PTS, PTS))).astype(F32)
    send_ref[:, :FEAT] = (mm(first, mixed) + mm(second, cot_ref[...])).astype(BF)
    marks = mm(first, (place + 1.0).astype(BF)) + mm(second, (place + (PTS + 1.0)).astype(BF))
    send_ref[:, FEAT:] = marks.astype(BF)


def patch_hits(marks):
    upper = lax.shift_right_logical(iota((SLOTS, PTS), 0), 3) & 1
    marks = marks.astype(F32) + jnp.where(upper == 1, 512.0, 0.0)
    lanes = iota((SLOTS, PTS), 1).astype(F32)
    return jnp.concatenate([one_hot(marks == lanes + (b + 1.0)) for b in (0, 512, 128, 640)], 1)


def layer_norm(hidden):
    centred = hidden - jnp.mean(hidden, -1, keepdims=True)
    inverse = lax.rsqrt(jnp.mean(centred * centred, -1, keepdims=True) + NORM_EPS)
    return centred * inverse, inverse


def patch_body(
    a_ref, b_ref, qkv_ref, proj_ref, gain_ref,
    back_ref, d0_ref, d1_ref, d2_ref, d3_ref, gg_ref,
    hits, qm, am, pr, ds, sc, gs, dense,
):
    x, core = position()
    whole = 2 * PTS
    head_dim = FEAT // HEADS
    scale = head_dim ** (-0.5)
    hits[...] = patch_hits(a_ref[:, FEAT:])
    rows = t_mm(hits[...], a_ref[:, :FEAT]) + t_mm(patch_hits(b_ref[:, FEAT:]), b_ref[:, :FEAT])
    hidden = rows[:whole]
    cot = rows[whole:].astype(BF)
    gain = gain_ref[...]
    normed, inverse = layer_norm(hidden)
    scaled = (normed * gain).astype(BF)
    projected = mm(scaled, qkv_ref[...]).astype(BF)
    query, keys, values = (projected[:, i * FEAT : (i + 1) * FEAT] for i in range(3))
    grad_att = mm_t(cot, proj_ref[...]).astype(BF)
    head_of = iota((PTS, FEAT), 1) // head_dim
    zero = jnp.zeros((PTS, FEAT), BF)
    halves = [slice(0, PTS), slice(PTS, whole)]
    spans = [[slice((s * HEADS + h) * PTS, (s * HEADS + h + 1) * PTS) for h in range(HEADS)] for s in range(2)]
    for s in range(2):
        for h in range(HEADS):
            qm[spans[s][h]] = jnp.where(head_of == h, query[halves[s]], zero)
            am[spans[s][h]] = jnp.where(head_of == h, grad_att[halves[s]], zero)
    sc[...] = mm_t(qm[...], keys)
    gs[...] = mm_t(am[...], values)
    for span in spans[0] + spans[1]:
        e = jnp.exp(sc[span] * scale)
        probs = (e * (1.0 / jnp.sum(e, -1, keepdims=True))).astype(BF)
        pr[span] = probs
        wide = probs.astype(F32)
        grad_probs = gs[span]
        delta = jnp.sum(wide * grad_probs, -1, keepdims=True)
        ds[span] = (wide * (grad_probs - delta) * scale).astype(BF)
    sc[...] = mm(pr[...], values)
    gs[...] = mm(ds[...], keys)
    att_parts, gq_parts, parts = [], [], []
    for s in range(2):
        att, gq = sc[spans[s][0]], gs[spans[s][0]]
        for h in range(1, HEADS):
            att = jnp.where(head_of == h, sc[spans[s][h]], att)
            gq = jnp.where(head_of == h, gs[spans[s][h]], gq)
        att_parts.append(att.astype(BF))
        gq_parts.append(gq.astype(BF))
        half = slice(s * HEADS * PTS, (s + 1) * HEADS * PTS)
        parts.append((t_mm(ds[half], qm[half]).astype(BF), t_mm(pr[half], am[half]).astype(BF)))
    attended = jnp.concatenate(att_parts, 0)
    gq = jnp.concatenate(gq_parts, 0)
    out = (hidden + mm(attended, proj_ref[...])).astype(BF)
    w_query, w_key, w_value = (qkv_ref[:, i * FEAT : (i + 1) * FEAT] for i in range(3))
    grad_scaled = mm_t(gq, w_query)
    for grad_key, grad_value in parts:
        grad_scaled += mm_t(grad_key, w_key) + mm_t(grad_value, w_value)

    @pl.when(core == 0)
    def _():
        dense[:FEAT] = t_mm(scaled, gq).astype(BF)
        dense[FEAT:] = (t_mm(scaled, parts[0][0]) + t_mm(scaled, parts[1][0])).astype(BF)

    @pl.when(core == 1)
    def _():
        dense[:FEAT] = (t_mm(scaled, parts[0][1]) + t_mm(scaled, parts[1][1])).astype(BF)
        dense[FEAT:] = t_mm(attended, cot).astype(BF)

    for d, ref in enumerate((d0_ref, d1_ref, d2_ref, d3_ref)):
        ref[...] = dense[pl.ds(pl.multiple_of(((x + d) & (NX - 1)) * PTS, PTS), PTS), :]
    gain_terms = grad_scaled * normed
    gg_ref[...] = jnp.sum(jnp.where(core == 0, gain_terms[:PTS], gain_terms[PTS:]), 0, keepdims=True)
    grad_normed = grad_scaled * gain
    grad_hidden = (
        grad_normed
        - jnp.mean(grad_normed, -1, keepdims=True)
        - normed * jnp.mean(grad_normed * normed, -1, keepdims=True)
    ) * inverse
    grad_local = (cot.astype(F32) + grad_hidden).astype(BF)
    back_ref[...] = mm(hits[...], jnp.concatenate([out, grad_local], 0)).astype(BF)


def table_body(feat_ref, prev_ref, next_ref, nbr_ref, pay_ref):
    pay_ref[:PTS] = feat_ref[...]
    pay_ref[PTS : PTS + RIM] = prev_ref[...]
    pay_ref[PTS + RIM : EXT] = next_ref[...]
    table = nbr_ref[...].astype(F32)
    pay_ref[EXT : EXT + 16, :PTS] = table[:16].astype(BF)
    pay_ref[EXT : EXT + 16, PTS:] = jnp.concatenate([table[16:], jnp.zeros((5, PTS), F32)], 0).astype(BF)
    pay_ref[EXT + 16 :] = jnp.zeros((PAY - EXT - 16, FEAT), BF)


def unpack_body(back_ref, rank_ref, gg_ref, d0_ref, d1_ref, d2_ref, d3_ref, block_ref, grad_ref, dense_ref):
    first, second = slot_hits(rank_ref[...])
    rows = back_ref[...]
    grad_ref[:PTS] = t_mm(second, rows).astype(BF)
    grad_ref[PTS:] = jnp.broadcast_to(gg_ref[...], (16, FEAT)).astype(BF)
    dense = d0_ref[...].astype(F32) + d1_ref[...].astype(F32) + d2_ref[...].astype(F32) + d3_ref[...].astype(F32)
    dense_ref[...] = dense.astype(BF)
    block_ref[...] = t_mm(first, rows).astype(BF)


def spread_body(grad_ref, nbr_ref, weight_ref, own_ref, down_ref, up_ref, acc):
    grad = grad_ref[:PTS]
    table = nbr_ref[...].astype(F32)
    points = iota((EXT, PTS), 0).astype(F32)
    acc[...] = jnp.zeros((EXT, FEAT), F32)
    for k in range(OFFS):
        hit = one_hot(points == table[k : k + 1])
        term = mm(hit, grad).astype(BF)
        acc[...] += mm_t(term, weight_ref[k * FEAT : (k + 1) * FEAT])
    own_ref[...] = acc[:PTS] + grad.astype(F32)
    down_ref[...] = acc[PTS : PTS + RIM].astype(BF)
    up_ref[...] = acc[PTS + RIM :].astype(BF)


def rim_body(own_ref, down_ref, up_ref, pick_ref, out_ref):
    rows = jnp.broadcast_to(pick_ref[...], (PTS, 2 * RIM))
    hit = one_hot(rows == iota((PTS, 2 * RIM), 0))
    rims = jnp.concatenate([down_ref[...], up_ref[...]], 0)
    out_ref[...] = (own_ref[...] + mm(hit, rims)).astype(BF)


def kernel_grad_body(all_ref, p0_ref, p1_ref, p2_ref, p3_ref, *refs):
    grads, (out_ref, tab, exts, terms, total) = refs[: NX * NC], refs[NX * NC :]
    x, core = position()
    base = x * 1728 + core * 108
    first_offset = jnp.minimum(lax.shift_right_logical(base, 8), OFFS - 8)
    first_row = base - first_offset * FEAT - core * 4
    dense = p0_ref[...].astype(F32) + p1_ref[...].astype(F32) + p2_ref[...].astype(F32) + p3_ref[...].astype(F32)
    dense = dense.astype(BF)
    gain = jnp.zeros((1, FEAT), F32)
    for s in range(NX * NC):
        source = ((x + NX - s % NX) & (NX - 1)) * NC + (core if s < NX else 1 - core)
        rows = all_ref[source, EXT : EXT + 16].astype(F32)
        tab[s * 32 : s * 32 + 16] = rows[:, :PTS]
        tab[s * 32 + 16 : s * 32 + 32] = rows[:, PTS:]
        exts[s * EXT : (s + 1) * EXT] = all_ref[source, :EXT]
        gain += grads[s][PTS : PTS + 1].astype(F32)
    ext_t = jnp.transpose(exts[...])
    points = iota((EXT, PTS), 0).astype(F32)
    for k in range(8):
        for s in range(NX * NC):
            hit = one_hot(points == tab[pl.ds(first_offset + (s * 32 + k), 1), :])
            terms[s * EXT : (s + 1) * EXT] = mm(hit, grads[s][:PTS]).astype(BF)
        total[k * FEAT : (k + 1) * FEAT] = mm(ext_t, terms[...])
    total[8 * FEAT :] = jnp.zeros((16, FEAT), F32)
    at = iota((112, FEAT), 0)
    for z in range(NZ):
        wide = total[pl.ds(pl.multiple_of(first_row + z * 216, 8), 120), :]
        rows = jnp.where(core == 1, wide[4:116], wide[:112])
        rows = jnp.where(at < 108, rows, jnp.where(at == 108, gain, 0.0))
        out_ref[z, :112] = rows.astype(BF)
        out_ref[z, 112:] = dense


def sum_body(got_ref, conv_ref, dense_ref):
    total = got_ref[0].astype(F32)
    for i in range(1, NZ):
        total += got_ref[i].astype(F32)
    conv_ref[...] = total[:112].astype(BF)
    dense_ref[...] = total[112:].astype(BF)


def last_body(factor, *refs):
    groups, parts = refs[:4], refs[4 : 4 + NX * NC]
    conv_ref, gain_ref, qkv_ref, proj_ref, rows = refs[4 + NX * NC :]
    total = groups[0][...].astype(F32)
    for group in groups[1:]:
        total += group[...].astype(F32)
    conv_ref[...] = total[:108] * factor
    gain_ref[...] = total[108:109] * factor
    x, core = position()
    for s in range(NX * NC):
        source = ((x + NX - s % NX) & (NX - 1)) + NX * (core if s < NX else 1 - core)
        rows[source] = parts[s][...].astype(F32) * factor
    for b in range(NX * NC):
        part, at = b // 2, b % 2 * PTS
        if part < 3:
            qkv_ref[at : at + PTS, part * FEAT : (part + 1) * FEAT] = rows[b]
        else:
            proj_ref[at : at + PTS] = rows[b]


def shards(
    features,
    hilbert_rank,
    neighbours,
    halo_rows,
    cotangent,
    conv_weight,
    qkv_weight,
    proj_weight,
    norm_gain,
):
    factor = 1.0 / math.sqrt(PTS * NX * NZ * NC * lax.axis_size("grp"))
    rank_row = hilbert_rank.reshape(1, PTS)
    gain_row = norm_gain.reshape(1, FEAT)
    table = neighbours.T
    to_prev, to_next = call(
        pick_body, [sds((RIM, FEAT))] * 2, halo_rows, features, fetched=(0, 1), limit=8
    )
    from_prev = lax.ppermute(to_next, "gz", UP)
    from_next = lax.ppermute(to_prev, "gz", DOWN)
    payload = call(
        table_body, sds((PAY, FEAT)), features, from_prev, from_next, table, fetched=(0, 3), limit=8
    )
    everyone = lax.all_gather(payload, "gz", axis_index_groups=XC_GROUPS)
    send = call(
        conv_body,
        sds((SLOTS, FEAT + PTS)),
        features, from_prev, from_next, table, rank_row, cotangent, conv_weight, payload,
        scratch=[pltpu.VMEM((FEAT, FEAT), BF), pltpu.VMEM((PTS, PTS), F32), pltpu.VMEM((PTS, OFFS * FEAT), BF)],
        fetched=(0, 3, 4, 5), late=(6,), idle=(7,), limit=16,
    )
    got = lax.all_to_all(
        send.reshape(32, 16, FEAT + PTS), "gz", split_axis=0, concat_axis=0,
        axis_index_groups=XZ_GROUPS, tiled=True,
    ).reshape(SLOTS, FEAT + PTS)
    other = lax.ppermute(got, "gz", SWAP)
    rows = 2 * HEADS * PTS
    back, d0, d1, d2, d3, grad_gain = call(
        patch_body,
        [sds((SLOTS, FEAT))] + [sds((PTS, FEAT))] * 4 + [sds((1, FEAT), F32)],
        got, other, qkv_weight, proj_weight, gain_row,
        scratch=[pltpu.VMEM((SLOTS, SLOTS), BF)]
        + [pltpu.VMEM((rows, FEAT), BF)] * 4
        + [pltpu.VMEM((rows, FEAT), F32)] * 2
        + [pltpu.VMEM((2 * FEAT, FEAT), BF)],
        limit=32,
    )
    dense_parts = [d0] + [along_x(v, d) for d, v in ((1, d1), (2, d2), (3, d3))]
    returned = lax.all_to_all(
        back.reshape(32, 16, FEAT), "gz", split_axis=0, concat_axis=0,
        axis_index_groups=XZ_GROUPS, tiled=True,
    ).reshape(SLOTS, FEAT)
    block_out, grad, dense = call(
        unpack_body,
        [sds((PTS, FEAT)), sds((PTS + 16, FEAT)), sds((PTS, FEAT))],
        returned, rank_row, grad_gain, *dense_parts,
        fetched=(1,), limit=8,
    )
    grads = over_chips(grad)
    dense_groups = over_groups(dense)
    own_part, rim_down, rim_up = call(
        spread_body,
        [sds((PTS, FEAT), F32), sds((RIM, FEAT)), sds((RIM, FEAT))],
        grad, table, conv_weight,
        scratch=[pltpu.VMEM((EXT, FEAT), F32)],
        limit=8,
    )
    got_down = lax.ppermute(rim_down, "gz", DOWN)
    got_up = lax.ppermute(rim_up, "gz", UP)
    parts = call(
        kernel_grad_body,
        sds((NZ, 240, FEAT)),
        everyone, *dense_groups, *grads, own_part,
        scratch=[
            pltpu.VMEM((NX * NC * 32, PTS), F32),
            pltpu.VMEM((NX * NC * EXT, FEAT), BF),
            pltpu.VMEM((NX * NC * EXT, FEAT), BF),
            pltpu.VMEM((8 * FEAT + 16, FEAT), F32),
        ],
        idle=(13,),
    )
    grad_features = call(rim_body, sds((PTS, FEAT)), own_part, got_up, got_down, halo_rows, limit=8)
    z_parts = lax.all_to_all(
        parts, "gz", split_axis=0, concat_axis=0, axis_index_groups=Z_GROUPS, tiled=True
    )
    conv_part, dense_sum = call(
        sum_body, [sds((112, FEAT)), sds((PTS, FEAT))], z_parts, grad_features, idle=(1,), limit=8
    )
    grad_conv, gain_sum, grad_qkv, grad_proj = call(
        lambda *refs: last_body(factor, *refs),
        [sds((108, FEAT), F32), sds((1, FEAT), F32), sds((FEAT, 3 * FEAT), F32), sds((FEAT, FEAT), F32)],
        *over_groups(conv_part), *over_chips(dense_sum),
        scratch=[pltpu.VMEM((NX * NC, PTS, FEAT), F32)],
        limit=8,
    )
    return (block_out, grad_features, grad_conv, grad_qkv, grad_proj, gain_sum.reshape(FEAT))


def solution(mesh):
    return jax.shard_map(
        shards,
        mesh=mesh,
        in_specs=(
            P(("grp", "gz"), None),
            P(("grp", "gz")),
            P(("grp", "gz"), None),
            P(("grp", "gz"), None),
            P(("grp", "gz"), None),
            P(),
            P(),
            P(),
            P(),
        ),
        out_specs=(P(("grp", "gz"), None), P(("grp", "gz"), None), P("gz", None), P(), P(), P()),
        check_vma=False,
    )
```

```python
import math

import jax
import jax.numpy as jnp
from jax import lax
from jax.experimental import pallas as pl
from jax.experimental.pallas import tpu as pltpu
from jax.sharding import PartitionSpec as P

HEADS = 16
NORM_EPS = 1e-05
BF = jnp.bfloat16
F32 = jnp.float32
I32 = jnp.int32

PTS = 128
FEAT = 256
OFFS = 27
RIM = 16
EXT = PTS + 2 * RIM
SLOTS = 512
PAY = 256
MIB = 1024 * 1024

NX, NZ, NC = 4, 8, 2
Z_GROUPS = [[x * 16 + z * 2 + c for z in range(NZ)] for x in range(NX) for c in range(NC)]
XC_GROUPS = [[x * 16 + z * 2 + c for x in range(NX) for c in range(NC)] for z in range(NZ)]
XZ_GROUPS = [[x * 16 + z * 2 + c for x in range(NX) for z in range(NZ)] for c in range(NC)]
SWAP = [(i, i ^ 1) for i in range(NX * NZ * NC)]
UP = [(i, i + 1) for i in range(NX * NZ * NC - 1)]
DOWN = [(i + 1, i) for i in range(NX * NZ * NC - 1)]


def along_x(value, d):
    n = NX * NZ * NC
    return lax.ppermute(value, "gz", [(i, (i + 16 * d) % n) for i in range(n)])


def over_chips(value):
    near = [value] + [along_x(value, d) for d in range(1, NX)]
    return near + [lax.ppermute(v, "gz", SWAP) for v in near]


def over_groups(value):
    n = lax.axis_size("grp")
    return [value] + [lax.ppermute(value, "grp", [(i, (i + d) % n) for i in range(n)]) for d in range(1, n)]


def mm(a, b):
    return jnp.dot(a, b, preferred_element_type=F32)


def mm_t(a, b):
    return lax.dot_general(a, b, (((1,), (1,)), ((), ())), preferred_element_type=F32)


def t_mm(a, b):
    return lax.dot_general(a, b, (((0,), (0,)), ((), ())), preferred_element_type=F32)


def one_hot(cond):
    return jnp.where(cond, 1.0, 0.0).astype(BF)


def iota(shape, dim):
    return lax.broadcasted_iota(I32, shape, dim)


def call(body, out_shape, *args, scratch=(), us=1.0, fetched=(), late=(), idle=(), pinned=(), limit=16):
    fetched = tuple(fetched) + tuple(late)
    args = [pltpu.with_memory_space_constraint(a, pltpu.HBM) if i in fetched else a for i, a in enumerate(args)]
    specs = []
    for i in range(len(args)):
        space = pltpu.HBM if i in fetched else pl.ANY if i in idle else pltpu.VMEM
        specs.append(pl.BlockSpec(memory_space=space))
    single = not isinstance(out_shape, (list, tuple))
    outs = [out_shape] if single else list(out_shape)
    held = [pltpu.VMEM(args[i].shape, args[i].dtype) for i in fetched]
    held += [pltpu.VMEM(outs[i].shape, outs[i].dtype) for i in pinned]
    held += [pltpu.SemaphoreType.DMA] * (len(fetched) + len(pinned))
    shapes = [pltpu.HBM(o.shape, o.dtype) if i in pinned else o for i, o in enumerate(outs)]

    def outer(*refs):
        ins = list(refs[: len(args)])
        results = list(refs[len(args) : len(args) + len(outs)])
        first = len(args) + len(outs)
        extra = refs[first : first + len(scratch)]
        rest = refs[first + len(scratch) :]
        moved = len(fetched) + len(pinned)
        buffers, sems = rest[:moved], rest[moved:]
        copies = {}
        for n, i in enumerate(fetched):
            copies[i] = pltpu.make_async_copy(ins[i], buffers[n], sems[n])
            copies[i].start()
            ins[i] = buffers[n]
        for i in fetched:
            if i in late:
                ins[i] = (ins[i], copies[i].wait)
            else:
                copies[i].wait()
        leaving = []
        for n, i in enumerate(pinned):
            n += len(fetched)
            leaving.append(pltpu.make_async_copy(buffers[n], results[i], sems[n]))
            results[i] = buffers[n]
        body(*[v for i, v in enumerate(ins) if i not in idle], *results, *extra)
        for copy in leaving:
            copy.start()
        for copy in leaving:
            copy.wait()

    got = pl.pallas_call(
        outer,
        out_shape=shapes,
        in_specs=specs,
        out_specs=[pl.BlockSpec(memory_space=pltpu.HBM if i in pinned else pltpu.VMEM) for i in range(len(outs))],
        scratch_shapes=list(scratch) + held,
        compiler_params=pltpu.CompilerParams(vmem_limit_bytes=limit * MIB),
        cost_estimate=pl.CostEstimate(flops=int(us * 1.1e9), bytes_accessed=1 << 18, transcendentals=0),
    )(*args)
    return got[0] if single else got


def sds(shape, dtype=BF):
    return jax.ShapeDtypeStruct(shape, dtype)


def position():
    me = lax.axis_index("gz")
    return lax.shift_right_logical(me, 4), me & 1


def pick_body(pick_ref, feat_ref, down_ref, up_ref):
    rows = jnp.broadcast_to(pick_ref[...], (PTS, 2 * RIM))
    hit = one_hot(rows == iota((PTS, 2 * RIM), 0))
    got = t_mm(hit, feat_ref[...]).astype(BF)
    down_ref[...] = got[:RIM]
    up_ref[...] = got[RIM:]


def slot_hits(rank_row):
    owner = lax.shift_right_logical(rank_row, 7)
    wide = jnp.broadcast_to(owner, (PTS, PTS))
    tall = jnp.transpose(wide)
    earlier = (wide == tall) & (iota((PTS, PTS), 0) < iota((PTS, PTS), 1))
    slot = jnp.sum(jnp.where(earlier, 1, 0), axis=0, keepdims=True)
    target = owner * 8 + slot
    rows = iota((SLOTS, PTS), 0)
    return one_hot(rows == target), one_hot(rows == target + 4)


def conv_body(feat_ref, prev_ref, next_ref, nbr_ref, rank_ref, cot_ref, weight, send_ref, pay_ref, ext, tab, wide):
    weight_ref, weight_here = weight
    ext[:PTS] = feat_ref[...]
    ext[PTS : PTS + RIM] = prev_ref[...]
    ext[PTS + RIM : EXT] = next_ref[...]
    ext[EXT:] = jnp.zeros((FEAT - EXT, FEAT), BF)
    rows = ext[...]
    tab[:OFFS] = nbr_ref[...].astype(F32)
    tab[OFFS:] = jnp.zeros((PTS - OFFS, PTS), F32)
    pay_ref[:EXT] = rows[:EXT]
    pay_ref[EXT : EXT + 16, :PTS] = tab[:16].astype(BF)
    pay_ref[EXT : EXT + 16, PTS:] = tab[16:32].astype(BF)
    pay_ref[EXT + 16 :] = jnp.zeros((PAY - EXT - 16, FEAT), BF)
    table = jnp.transpose(tab[...])
    lanes = iota((PTS, FEAT), 1).astype(F32)
    for k in range(OFFS):
        hit = one_hot(table[:, k : k + 1] == lanes)
        wide[:, k * FEAT : (k + 1) * FEAT] = mm(hit, rows).astype(BF)
    weight_here()
    mixed = (feat_ref[...].astype(F32) + mm(wide[...], weight_ref[...])).astype(BF)
    rank_row = rank_ref[...]
    first, second = slot_hits(rank_row)
    place = jnp.transpose(jnp.broadcast_to(rank_row & (PTS - 1), (PTS, PTS))).astype(F32)
    send_ref[:, :FEAT] = (mm(first, mixed) + mm(second, cot_ref[...])).astype(BF)
    marks = mm(first, (place + 1.0).astype(BF)) + mm(second, (place + (PTS + 1.0)).astype(BF))
    send_ref[:, FEAT:] = marks.astype(BF)


def patch_hits(marks):
    upper = lax.shift_right_logical(iota((SLOTS, PTS), 0), 3) & 1
    marks = marks.astype(F32) + jnp.where(upper == 1, 512.0, 0.0)
    lanes = iota((SLOTS, PTS), 1).astype(F32)
    return jnp.concatenate([one_hot(marks == lanes + (b + 1.0)) for b in (0, 512, 128, 640)], 1)


def layer_norm(hidden):
    centred = hidden - jnp.mean(hidden, -1, keepdims=True)
    inverse = lax.rsqrt(jnp.mean(centred * centred, -1, keepdims=True) + NORM_EPS)
    return centred * inverse, inverse


def patch_body(
    a_ref, b_ref, qkv_ref, proj_ref, gain_ref,
    back_ref, gg_ref,
    hits, qm, am, pr, ds, sc, gs, dense,
):
    x, core = position()
    whole = 2 * PTS
    head_dim = FEAT // HEADS
    scale = head_dim ** (-0.5)
    hits[...] = patch_hits(a_ref[:, FEAT:])
    rows = t_mm(hits[...], a_ref[:, :FEAT]) + t_mm(patch_hits(b_ref[:, FEAT:]), b_ref[:, :FEAT])
    hidden = rows[:whole]
    cot = rows[whole:].astype(BF)
    gain = gain_ref[...]
    normed, inverse = layer_norm(hidden)
    scaled = (normed * gain).astype(BF)
    projected = mm(scaled, qkv_ref[...]).astype(BF)
    query, keys, values = (projected[:, i * FEAT : (i + 1) * FEAT] for i in range(3))
    grad_att = mm_t(cot, proj_ref[...]).astype(BF)
    head_of = iota((PTS, FEAT), 1) // head_dim
    zero = jnp.zeros((PTS, FEAT), BF)
    halves = [slice(0, PTS), slice(PTS, whole)]
    spans = [[slice((s * HEADS + h) * PTS, (s * HEADS + h + 1) * PTS) for h in range(HEADS)] for s in range(2)]
    for s in range(2):
        for h in range(HEADS):
            qm[spans[s][h]] = jnp.where(head_of == h, query[halves[s]], zero)
            am[spans[s][h]] = jnp.where(head_of == h, grad_att[halves[s]], zero)
    sc[...] = mm_t(qm[...], keys)
    gs[...] = mm_t(am[...], values)
    for span in spans[0] + spans[1]:
        e = jnp.exp(sc[span] * scale)
        probs = (e * (1.0 / jnp.sum(e, -1, keepdims=True))).astype(BF)
        pr[span] = probs
        wide = probs.astype(F32)
        grad_probs = gs[span]
        delta = jnp.sum(wide * grad_probs, -1, keepdims=True)
        ds[span] = (wide * (grad_probs - delta) * scale).astype(BF)
    sc[...] = mm(pr[...], values)
    gs[...] = mm(ds[...], keys)
    att_parts, gq_parts, parts = [], [], []
    for s in range(2):
        att, gq = sc[spans[s][0]], gs[spans[s][0]]
        for h in range(1, HEADS):
            att = jnp.where(head_of == h, sc[spans[s][h]], att)
            gq = jnp.where(head_of == h, gs[spans[s][h]], gq)
        att_parts.append(att.astype(BF))
        gq_parts.append(gq.astype(BF))
        half = slice(s * HEADS * PTS, (s + 1) * HEADS * PTS)
        parts.append((t_mm(ds[half], qm[half]).astype(BF), t_mm(pr[half], am[half]).astype(BF)))
    attended = jnp.concatenate(att_parts, 0)
    gq = jnp.concatenate(gq_parts, 0)
    out = (hidden + mm(attended, proj_ref[...])).astype(BF)
    w_query, w_key, w_value = (qkv_ref[:, i * FEAT : (i + 1) * FEAT] for i in range(3))
    grad_scaled = mm_t(gq, w_query)
    for grad_key, grad_value in parts:
        grad_scaled += mm_t(grad_key, w_key) + mm_t(grad_value, w_value)

    @pl.when(core == 0)
    def _():
        dense[:FEAT] = t_mm(scaled, gq).astype(BF)
        dense[FEAT:] = (t_mm(scaled, parts[0][0]) + t_mm(scaled, parts[1][0])).astype(BF)

    @pl.when(core == 1)
    def _():
        dense[:FEAT] = (t_mm(scaled, parts[0][1]) + t_mm(scaled, parts[1][1])).astype(BF)
        dense[FEAT:] = t_mm(attended, cot).astype(BF)

    back_ref[:, 16:] = dense[...].reshape(32, 16, FEAT)
    gain_terms = grad_scaled * normed
    gg_ref[...] = jnp.sum(jnp.where(core == 0, gain_terms[:PTS], gain_terms[PTS:]), 0, keepdims=True)
    grad_normed = grad_scaled * gain
    grad_hidden = (
        grad_normed
        - jnp.mean(grad_normed, -1, keepdims=True)
        - normed * jnp.mean(grad_normed * normed, -1, keepdims=True)
    ) * inverse
    grad_local = (cot.astype(F32) + grad_hidden).astype(BF)
    back = mm(hits[...], jnp.concatenate([out, grad_local], 0)).astype(BF)
    back_ref[:, :16] = back.reshape(32, 16, FEAT)


def unpack_body(back_ref, rank_ref, gg_ref, block_ref, grad_ref, dense_ref):
    first, second = slot_hits(rank_ref[...])
    rows = back_ref[:, :16].reshape(SLOTS, FEAT)
    grad_ref[:PTS] = t_mm(second, rows).astype(BF)
    grad_ref[PTS:] = jnp.broadcast_to(gg_ref[...], (16, FEAT)).astype(BF)
    dense_ref[...] = jnp.sum(back_ref[:, 16:].astype(F32), 0).astype(BF)
    block_ref[...] = t_mm(first, rows).astype(BF)


def spread_body(grad_ref, nbr_ref, weight, own_ref, down_ref, up_ref, terms, acc):
    weight_ref, weight_here = weight
    grad = grad_ref[:PTS]
    table = nbr_ref[...].astype(F32)
    points = iota((EXT, PTS), 0).astype(F32)
    for k in range(OFFS):
        hit = one_hot(points == table[k : k + 1])
        terms[k * EXT : (k + 1) * EXT] = mm(hit, grad).astype(BF)
    weight_here()
    acc[...] = jnp.zeros((EXT, FEAT), F32)
    for k in range(OFFS):
        acc[...] += mm_t(terms[k * EXT : (k + 1) * EXT], weight_ref[k * FEAT : (k + 1) * FEAT])
    own_ref[...] = acc[:PTS] + grad.astype(F32)
    down_ref[...] = acc[PTS : PTS + RIM].astype(BF)
    up_ref[...] = acc[PTS + RIM :].astype(BF)


def rim_body(own_ref, down_ref, up_ref, pick_ref, out_ref):
    rows = jnp.broadcast_to(pick_ref[...], (PTS, 2 * RIM))
    hit = one_hot(rows == iota((PTS, 2 * RIM), 0))
    rims = jnp.concatenate([down_ref[...], up_ref[...]], 0)
    out_ref[...] = (own_ref[...] + mm(hit, rims)).astype(BF)


def kernel_grad_body(all_ref, p0_ref, p1_ref, p2_ref, p3_ref, *refs):
    grads, (out_ref, tab, exts, terms, total) = refs[: NX * NC], refs[NX * NC :]
    x, core = position()
    base = x * 1728 + core * 108
    first_offset = jnp.minimum(lax.shift_right_logical(base, 8), OFFS - 8)
    first_row = base - first_offset * FEAT - core * 4
    dense = p0_ref[...].astype(F32) + p1_ref[...].astype(F32) + p2_ref[...].astype(F32) + p3_ref[...].astype(F32)
    dense = dense.astype(BF)
    gain = jnp.zeros((1, FEAT), F32)
    for s in range(NX * NC):
        source = ((x + NX - s % NX) & (NX - 1)) * NC + (core if s < NX else 1 - core)
        rows = all_ref[source, EXT : EXT + 16].astype(F32)
        tab[s * 32 : s * 32 + 16] = rows[:, :PTS]
        tab[s * 32 + 16 : s * 32 + 32] = rows[:, PTS:]
        exts[s * EXT : (s + 1) * EXT] = all_ref[source, :EXT]
        gain += grads[s][PTS : PTS + 1].astype(F32)
    ext_t = jnp.transpose(exts[...])
    points = iota((EXT, PTS), 0).astype(F32)
    for k in range(8):
        for s in range(NX * NC):
            hit = one_hot(points == tab[pl.ds(first_offset + (s * 32 + k), 1), :])
            terms[s * EXT : (s + 1) * EXT] = mm(hit, grads[s][:PTS]).astype(BF)
        total[k * FEAT : (k + 1) * FEAT] = mm(ext_t, terms[...])
    total[8 * FEAT :] = jnp.zeros((16, FEAT), F32)
    at = iota((112, FEAT), 0)
    for z in range(NZ):
        wide = total[pl.ds(pl.multiple_of(first_row + z * 216, 8), 120), :]
        rows = jnp.where(core == 1, wide[4:116], wide[:112])
        rows = jnp.where(at < 108, rows, jnp.where(at == 108, gain, 0.0))
        out_ref[z, :112] = rows.astype(BF)
        out_ref[z, 112:] = dense


def sum_body(got_ref, conv_ref, dense_ref):
    total = got_ref[0].astype(F32)
    for i in range(1, NZ):
        total += got_ref[i].astype(F32)
    conv_ref[...] = total[:112].astype(BF)
    for i in range(NZ):
        dense_ref[i * 16 : (i + 1) * 16] = got_ref[i, 112:]


def last_body(factor, *refs):
    groups, parts = refs[:4], refs[4 : 4 + NX * NC]
    conv_ref, gain_ref, qkv_ref, proj_ref, rows = refs[4 + NX * NC :]
    total = groups[0][...].astype(F32)
    for group in groups[1:]:
        total += group[...].astype(F32)
    conv_ref[...] = total[:108] * factor
    gain_ref[...] = total[108:109] * factor
    x, core = position()
    for s in range(NX * NC):
        source = ((x + NX - s % NX) & (NX - 1)) + NX * (core if s < NX else 1 - core)
        rows[source] = parts[s][...].astype(F32) * factor
    for b in range(NX * NC):
        part, at = b // 2, b % 2 * PTS
        if part < 3:
            qkv_ref[at : at + PTS, part * FEAT : (part + 1) * FEAT] = rows[b]
        else:
            proj_ref[at : at + PTS] = rows[b]


def shards(
    features,
    hilbert_rank,
    neighbours,
    halo_rows,
    cotangent,
    conv_weight,
    qkv_weight,
    proj_weight,
    norm_gain,
):
    factor = 1.0 / math.sqrt(PTS * NX * NZ * NC * lax.axis_size("grp"))
    rank_row = hilbert_rank.reshape(1, PTS)
    gain_row = norm_gain.reshape(1, FEAT)
    table = neighbours.T
    to_prev, to_next = call(
        pick_body, [sds((RIM, FEAT))] * 2, halo_rows, features, fetched=(0, 1), us=0.5, limit=8
    )
    from_prev = lax.ppermute(to_next, "gz", UP)
    from_next = lax.ppermute(to_prev, "gz", DOWN)
    send, payload = call(
        conv_body,
        [sds((SLOTS, FEAT + PTS)), sds((PAY, FEAT))],
        features, from_prev, from_next, table, rank_row, cotangent, conv_weight,
        scratch=[pltpu.VMEM((FEAT, FEAT), BF), pltpu.VMEM((PTS, PTS), F32), pltpu.VMEM((PTS, OFFS * FEAT), BF)],
        fetched=(0, 3, 4, 5), late=(6,), pinned=(0, 1), us=3.0,
    )
    everyone = lax.all_gather(payload, "gz", axis_index_groups=XC_GROUPS)
    got = lax.all_to_all(
        send.reshape(32, 16, FEAT + PTS), "gz", split_axis=0, concat_axis=0,
        axis_index_groups=XZ_GROUPS, tiled=True,
    ).reshape(SLOTS, FEAT + PTS)
    other = lax.ppermute(got, "gz", SWAP)
    rows = 2 * HEADS * PTS
    back, grad_gain = call(
        patch_body,
        [sds((32, 32, FEAT)), sds((1, FEAT), F32)],
        got, other, qkv_weight, proj_weight, gain_row,
        scratch=[pltpu.VMEM((SLOTS, SLOTS), BF)]
        + [pltpu.VMEM((rows, FEAT), BF)] * 4
        + [pltpu.VMEM((rows, FEAT), F32)] * 2
        + [pltpu.VMEM((2 * FEAT, FEAT), BF)],
        pinned=(0, 1), us=6.0, limit=32,
    )
    returned = lax.all_to_all(
        back, "gz", split_axis=0, concat_axis=0, axis_index_groups=XZ_GROUPS, tiled=True
    )
    block_out, grad, dense = call(
        unpack_body,
        [sds((PTS, FEAT)), sds((PTS + 16, FEAT)), sds((16, FEAT))],
        returned, rank_row, grad_gain,
        fetched=(0, 1, 2), pinned=(1, 2), us=1.5, limit=8,
    )
    grads = over_chips(grad)
    dense_groups = over_groups(dense)
    own_part, rim_down, rim_up = call(
        spread_body,
        [sds((PTS, FEAT), F32), sds((RIM, FEAT)), sds((RIM, FEAT))],
        grad, table, conv_weight,
        scratch=[pltpu.VMEM((OFFS * EXT, FEAT), BF), pltpu.VMEM((EXT, FEAT), F32)],
        fetched=(0, 1), late=(2,), pinned=(0, 1, 2), us=4.0,
    )
    got_down = lax.ppermute(rim_down, "gz", DOWN)
    got_up = lax.ppermute(rim_up, "gz", UP)
    parts = call(
        kernel_grad_body,
        sds((NZ, 128, FEAT)),
        everyone, *dense_groups, *grads, own_part,
        scratch=[
            pltpu.VMEM((NX * NC * 32, PTS), F32),
            pltpu.VMEM((NX * NC * EXT, FEAT), BF),
            pltpu.VMEM((NX * NC * EXT, FEAT), BF),
            pltpu.VMEM((8 * FEAT + 16, FEAT), F32),
        ],
        fetched=tuple(range(13)), idle=(13,), pinned=(0,), us=5.0,
    )
    grad_features = call(
        rim_body, sds((PTS, FEAT)), own_part, got_up, got_down, halo_rows,
        fetched=(0, 1, 2, 3), us=1.0, limit=8,
    )
    z_parts = lax.all_to_all(
        parts, "gz", split_axis=0, concat_axis=0, axis_index_groups=Z_GROUPS, tiled=True
    )
    conv_part, dense_sum = call(
        sum_body, [sds((112, FEAT)), sds((PTS, FEAT))], z_parts, grad_features,
        fetched=(0,), idle=(1,), us=1.0, limit=8,
    )
    grad_conv, gain_sum, grad_qkv, grad_proj = call(
        lambda *refs: last_body(factor, *refs),
        [sds((108, FEAT), F32), sds((1, FEAT), F32), sds((FEAT, 3 * FEAT), F32), sds((FEAT, FEAT), F32)],
        *over_groups(conv_part), *over_chips(dense_sum),
        scratch=[pltpu.VMEM((NX * NC, PTS, FEAT), F32)],
        limit=8,
    )
    return (block_out, grad_features, grad_conv, grad_qkv, grad_proj, gain_sum.reshape(FEAT))


def solution(mesh):
    return jax.shard_map(
        shards,
        mesh=mesh,
        in_specs=(
            P(("grp", "gz"), None),
            P(("grp", "gz")),
            P(("grp", "gz"), None),
            P(("grp", "gz"), None),
            P(("grp", "gz"), None),
            P(),
            P(),
            P(),
            P(),
        ),
        out_specs=(P(("grp", "gz"), None), P(("grp", "gz"), None), P("gz", None), P(), P(), P()),
        check_vma=False,
    )
```

```python
import math

import jax
import jax.numpy as jnp
from jax import lax
from jax.experimental import pallas as pl
from jax.experimental.pallas import tpu as pltpu
from jax.sharding import PartitionSpec as P

HEADS = 16
NORM_EPS = 1e-05
BF = jnp.bfloat16
F32 = jnp.float32
I32 = jnp.int32

PTS = 128
FEAT = 256
OFFS = 27
RIM = 16
EXT = PTS + 2 * RIM
SLOTS = 512
AT_GAIN, AT_EXT, AT_TAB, PAY = 128, 144, 304, 320
MIB = 1024 * 1024

NX, NZ, NC = 4, 8, 2
Z_GROUPS = [[x * 16 + z * 2 + c for z in range(NZ)] for x in range(NX) for c in range(NC)]
X_GROUPS = [[x * 16 + z * 2 + c for x in range(NX)] for z in range(NZ) for c in range(NC)]
XZ_GROUPS = [[x * 16 + z * 2 + c for x in range(NX) for z in range(NZ)] for c in range(NC)]
SWAP = [(i, i ^ 1) for i in range(NX * NZ * NC)]
UP = [(i, i + 1) for i in range(NX * NZ * NC - 1)]
DOWN = [(i + 1, i) for i in range(NX * NZ * NC - 1)]


def by_chips(copies):
    near = lax.all_to_all(copies, "gz", split_axis=0, concat_axis=0, axis_index_groups=X_GROUPS, tiled=True)
    return near, lax.ppermute(near, "gz", SWAP)


def along_x(value, d):
    n = NX * NZ * NC
    return lax.ppermute(value, "gz", [(i, (i + 16 * d) % n) for i in range(n)])


def over_chips(value):
    near = [value] + [along_x(value, d) for d in range(1, NX)]
    return near + [lax.ppermute(v, "gz", SWAP) for v in near]


def over_groups(value):
    n = lax.axis_size("grp")
    return [value] + [lax.ppermute(value, "grp", [(i, (i + d) % n) for i in range(n)]) for d in range(1, n)]


def mm(a, b):
    return jnp.dot(a, b, preferred_element_type=F32)


def mm_t(a, b):
    return lax.dot_general(a, b, (((1,), (1,)), ((), ())), preferred_element_type=F32)


def t_mm(a, b):
    return lax.dot_general(a, b, (((0,), (0,)), ((), ())), preferred_element_type=F32)


def one_hot(cond):
    return jnp.where(cond, 1.0, 0.0).astype(BF)


def iota(shape, dim):
    return lax.broadcasted_iota(I32, shape, dim)


def call(body, out_shape, *args, scratch=(), us=1.0, fetched=(), late=(), idle=(), pinned=(), limit=16):
    fetched = tuple(fetched) + tuple(late)
    args = [pltpu.with_memory_space_constraint(a, pltpu.HBM) if i in fetched + tuple(idle) else a for i, a in enumerate(args)]
    specs = []
    for i in range(len(args)):
        space = pltpu.HBM if i in fetched + tuple(idle) else pltpu.VMEM
        specs.append(pl.BlockSpec(memory_space=space))
    single = not isinstance(out_shape, (list, tuple))
    outs = [out_shape] if single else list(out_shape)
    held = [pltpu.VMEM(args[i].shape, args[i].dtype) for i in fetched]
    held += [pltpu.VMEM(outs[i].shape, outs[i].dtype) for i in pinned]
    held += [pltpu.SemaphoreType.DMA] * (len(fetched) + len(pinned))
    shapes = [pltpu.HBM(o.shape, o.dtype) if i in pinned else o for i, o in enumerate(outs)]

    def outer(*refs):
        ins = list(refs[: len(args)])
        results = list(refs[len(args) : len(args) + len(outs)])
        first = len(args) + len(outs)
        extra = refs[first : first + len(scratch)]
        rest = refs[first + len(scratch) :]
        moved = len(fetched) + len(pinned)
        buffers, sems = rest[:moved], rest[moved:]
        copies = {}
        for n, i in enumerate(fetched):
            copies[i] = pltpu.make_async_copy(ins[i], buffers[n], sems[n])
            copies[i].start()
            ins[i] = buffers[n]
        for i in fetched:
            if i in late:
                ins[i] = (ins[i], copies[i].wait)
            else:
                copies[i].wait()
        leaving = []
        for n, i in enumerate(pinned):
            n += len(fetched)
            leaving.append(pltpu.make_async_copy(buffers[n], results[i], sems[n]))
            results[i] = buffers[n]
        body(*[v for i, v in enumerate(ins) if i not in idle], *results, *extra)
        for copy in leaving:
            copy.start()
        for copy in leaving:
            copy.wait()

    got = pl.pallas_call(
        outer,
        out_shape=shapes,
        in_specs=specs,
        out_specs=[pl.BlockSpec(memory_space=pltpu.HBM if i in pinned else pltpu.VMEM) for i in range(len(outs))],
        scratch_shapes=list(scratch) + held,
        compiler_params=pltpu.CompilerParams(vmem_limit_bytes=limit * MIB),
        cost_estimate=pl.CostEstimate(flops=int(us * 1.1e9), bytes_accessed=1 << 18, transcendentals=0),
    )(*args)
    return got[0] if single else got


def sds(shape, dtype=BF):
    return jax.ShapeDtypeStruct(shape, dtype)


def position():
    me = lax.axis_index("gz")
    return lax.shift_right_logical(me, 4), me & 1


def pick_body(pick_ref, feat_ref, down_ref, up_ref):
    rows = jnp.broadcast_to(pick_ref[...], (PTS, 2 * RIM))
    hit = one_hot(rows == iota((PTS, 2 * RIM), 0))
    got = t_mm(hit, feat_ref[...]).astype(BF)
    down_ref[...] = got[:RIM]
    up_ref[...] = got[RIM:]


def slot_hits(rank_row):
    owner = lax.shift_right_logical(rank_row, 7)
    wide = jnp.broadcast_to(owner, (PTS, PTS))
    tall = jnp.transpose(wide)
    earlier = (wide == tall) & (iota((PTS, PTS), 0) < iota((PTS, PTS), 1))
    slot = jnp.sum(jnp.where(earlier, 1, 0), axis=0, keepdims=True)
    target = owner * 8 + slot
    rows = iota((SLOTS, PTS), 0)
    return one_hot(rows == target), one_hot(rows == target + 4)


def conv_body(feat_ref, prev_ref, next_ref, nbr_ref, rank_ref, cot_ref, weight, send_ref, ext, tab, wide):
    weight_ref, weight_here = weight
    ext[:PTS] = feat_ref[...]
    ext[PTS : PTS + RIM] = prev_ref[...]
    ext[PTS + RIM : EXT] = next_ref[...]
    ext[EXT:] = jnp.zeros((FEAT - EXT, FEAT), BF)
    rows = ext[...]
    tab[:OFFS] = nbr_ref[...].astype(F32)
    tab[OFFS:] = jnp.zeros((PTS - OFFS, PTS), F32)
    table = jnp.transpose(tab[...])
    lanes = iota((PTS, FEAT), 1).astype(F32)
    for k in range(OFFS):
        hit = one_hot(table[:, k : k + 1] == lanes)
        wide[:, k * FEAT : (k + 1) * FEAT] = mm(hit, rows).astype(BF)
    weight_here()
    mixed = (feat_ref[...].astype(F32) + mm(wide[...], weight_ref[...])).astype(BF)
    rank_row = rank_ref[...]
    first, second = slot_hits(rank_row)
    place = jnp.transpose(jnp.broadcast_to(rank_row & (PTS - 1), (PTS, PTS))).astype(F32)
    send_ref[:, :FEAT] = (mm(first, mixed) + mm(second, cot_ref[...])).astype(BF)
    marks = mm(first, (place + 1.0).astype(BF)) + mm(second, (place + (PTS + 1.0)).astype(BF))
    send_ref[:, FEAT:] = marks.astype(BF)


def patch_hits(marks):
    upper = lax.shift_right_logical(iota((SLOTS, PTS), 0), 3) & 1
    marks = marks.astype(F32) + jnp.where(upper == 1, 512.0, 0.0)
    lanes = iota((SLOTS, PTS), 1).astype(F32)
    return jnp.concatenate([one_hot(marks == lanes + (b + 1.0)) for b in (0, 512, 128, 640)], 1)


def layer_norm(hidden):
    centred = hidden - jnp.mean(hidden, -1, keepdims=True)
    inverse = lax.rsqrt(jnp.mean(centred * centred, -1, keepdims=True) + NORM_EPS)
    return centred * inverse, inverse


def patch_body(
    a_ref, b_ref, qkv_ref, proj_ref, gain_ref,
    back_ref, gg_ref,
    hits, qm, am, pr, ds, sc, gs, dense,
):
    x, core = position()
    whole = 2 * PTS
    head_dim = FEAT // HEADS
    scale = head_dim ** (-0.5)
    hits[...] = patch_hits(a_ref[:, FEAT:])
    rows = t_mm(hits[...], a_ref[:, :FEAT]) + t_mm(patch_hits(b_ref[:, FEAT:]), b_ref[:, :FEAT])
    hidden = rows[:whole]
    cot = rows[whole:].astype(BF)
    gain = gain_ref[...]
    normed, inverse = layer_norm(hidden)
    scaled = (normed * gain).astype(BF)
    projected = mm(scaled, qkv_ref[...]).astype(BF)
    query, keys, values = (projected[:, i * FEAT : (i + 1) * FEAT] for i in range(3))
    grad_att = mm_t(cot, proj_ref[...]).astype(BF)
    head_of = iota((PTS, FEAT), 1) // head_dim
    zero = jnp.zeros((PTS, FEAT), BF)
    halves = [slice(0, PTS), slice(PTS, whole)]
    spans = [[slice((s * HEADS + h) * PTS, (s * HEADS + h + 1) * PTS) for h in range(HEADS)] for s in range(2)]
    for s in range(2):
        for h in range(HEADS):
            qm[spans[s][h]] = jnp.where(head_of == h, query[halves[s]], zero)
            am[spans[s][h]] = jnp.where(head_of == h, grad_att[halves[s]], zero)
    sc[...] = mm_t(qm[...], keys)
    gs[...] = mm_t(am[...], values)
    for span in spans[0] + spans[1]:
        e = jnp.exp(sc[span] * scale)
        probs = (e * (1.0 / jnp.sum(e, -1, keepdims=True))).astype(BF)
        pr[span] = probs
        wide = probs.astype(F32)
        grad_probs = gs[span]
        delta = jnp.sum(wide * grad_probs, -1, keepdims=True)
        ds[span] = (wide * (grad_probs - delta) * scale).astype(BF)
    sc[...] = mm(pr[...], values)
    gs[...] = mm(ds[...], keys)
    att_parts, gq_parts, parts = [], [], []
    for s in range(2):
        att, gq = sc[spans[s][0]], gs[spans[s][0]]
        for h in range(1, HEADS):
            att = jnp.where(head_of == h, sc[spans[s][h]], att)
            gq = jnp.where(head_of == h, gs[spans[s][h]], gq)
        att_parts.append(att.astype(BF))
        gq_parts.append(gq.astype(BF))
        half = slice(s * HEADS * PTS, (s + 1) * HEADS * PTS)
        parts.append((t_mm(ds[half], qm[half]).astype(BF), t_mm(pr[half], am[half]).astype(BF)))
    attended = jnp.concatenate(att_parts, 0)
    gq = jnp.concatenate(gq_parts, 0)
    out = (hidden + mm(attended, proj_ref[...])).astype(BF)
    w_query, w_key, w_value = (qkv_ref[:, i * FEAT : (i + 1) * FEAT] for i in range(3))
    grad_scaled = mm_t(gq, w_query)
    for grad_key, grad_value in parts:
        grad_scaled += mm_t(grad_key, w_key) + mm_t(grad_value, w_value)

    @pl.when(core == 0)
    def _():
        dense[:FEAT] = t_mm(scaled, gq).astype(BF)
        dense[FEAT:] = (t_mm(scaled, parts[0][0]) + t_mm(scaled, parts[1][0])).astype(BF)

    @pl.when(core == 1)
    def _():
        dense[:FEAT] = (t_mm(scaled, parts[0][1]) + t_mm(scaled, parts[1][1])).astype(BF)
        dense[FEAT:] = t_mm(attended, cot).astype(BF)

    back_ref[:, 16:] = dense[...].reshape(32, 16, FEAT)
    gain_terms = grad_scaled * normed
    gg_ref[...] = jnp.sum(jnp.where(core == 0, gain_terms[:PTS], gain_terms[PTS:]), 0, keepdims=True)
    grad_normed = grad_scaled * gain
    grad_hidden = (
        grad_normed
        - jnp.mean(grad_normed, -1, keepdims=True)
        - normed * jnp.mean(grad_normed * normed, -1, keepdims=True)
    ) * inverse
    grad_local = (cot.astype(F32) + grad_hidden).astype(BF)
    back = mm(hits[...], jnp.concatenate([out, grad_local], 0)).astype(BF)
    back_ref[:, :16] = back.reshape(32, 16, FEAT)


def unpack_body(
    back_ref, rank_ref, gg_ref, feat_ref, prev_ref, next_ref, nbr_ref,
    block_ref, grad_ref, copies_ref, dense_ref,
):
    first, second = slot_hits(rank_ref[...])
    rows = back_ref[:, :16].reshape(SLOTS, FEAT)
    grad = t_mm(second, rows).astype(BF)
    gain = jnp.broadcast_to(gg_ref[...], (16, FEAT)).astype(BF)
    table = nbr_ref[...].astype(F32)
    table = jnp.concatenate([table, jnp.zeros((32 - OFFS, PTS), F32)], 0).astype(BF)
    grad_ref[...] = grad
    for x in range(NX):
        copies_ref[x, :AT_GAIN] = grad
        copies_ref[x, AT_GAIN:AT_EXT] = gain
        copies_ref[x, AT_EXT : AT_EXT + PTS] = feat_ref[...]
        copies_ref[x, AT_EXT + PTS : AT_EXT + PTS + RIM] = prev_ref[...]
        copies_ref[x, AT_EXT + PTS + RIM : AT_TAB] = next_ref[...]
        copies_ref[x, AT_TAB:, :PTS] = table[:16]
        copies_ref[x, AT_TAB:, PTS:] = table[16:]
    dense_ref[...] = jnp.sum(back_ref[:, 16:].astype(F32), 0).astype(BF)
    block_ref[...] = t_mm(first, rows).astype(BF)


def spread_body(grad_ref, nbr_ref, weight, own_ref, down_ref, up_ref, terms, acc):
    weight_ref, weight_here = weight
    grad = grad_ref[...]
    table = nbr_ref[...].astype(F32)
    points = iota((EXT, PTS), 0).astype(F32)
    for k in range(OFFS):
        hit = one_hot(points == table[k : k + 1])
        terms[k * EXT : (k + 1) * EXT] = mm(hit, grad).astype(BF)
    weight_here()
    acc[...] = jnp.zeros((EXT, FEAT), F32)
    for k in range(OFFS):
        acc[...] += mm_t(terms[k * EXT : (k + 1) * EXT], weight_ref[k * FEAT : (k + 1) * FEAT])
    own_ref[...] = acc[:PTS] + grad.astype(F32)
    down_ref[...] = acc[PTS : PTS + RIM].astype(BF)
    up_ref[...] = acc[PTS + RIM :].astype(BF)


def rim_body(own_ref, down_ref, up_ref, pick_ref, out_ref):
    rows = jnp.broadcast_to(pick_ref[...], (PTS, 2 * RIM))
    hit = one_hot(rows == iota((PTS, 2 * RIM), 0))
    rims = jnp.concatenate([down_ref[...], up_ref[...]], 0)
    out_ref[...] = (own_ref[...] + mm(hit, rims)).astype(BF)


def kernel_grad_body(p0_ref, p1_ref, p2_ref, p3_ref, near_ref, far_ref, out_ref, tab, exts, terms, total):
    x, core = position()
    base = x * 1728 + core * 108
    first_offset = jnp.minimum(lax.shift_right_logical(base, 8), OFFS - 8)
    first_row = base - first_offset * FEAT - core * 4
    dense = p0_ref[...].astype(F32) + p1_ref[...].astype(F32) + p2_ref[...].astype(F32) + p3_ref[...].astype(F32)
    dense = dense.astype(BF)
    gain = jnp.zeros((1, FEAT), F32)
    points = iota((EXT, PTS), 0).astype(F32)
    for s in range(NX * NC):
        held = near_ref if s < NX else far_ref
        rows = held[s % NX, AT_TAB:].astype(F32)
        tab[s * 32 : s * 32 + 16] = rows[:, :PTS]
        tab[s * 32 + 16 : s * 32 + 32] = rows[:, PTS:]
        exts[s * EXT : (s + 1) * EXT] = held[s % NX, AT_EXT:AT_TAB]
        gain += held[s % NX, AT_GAIN : AT_GAIN + 1].astype(F32)
        hits = [one_hot(points == tab[pl.ds(first_offset + (s * 32 + k), 1), :]) for k in range(8)]
        found = mm(jnp.concatenate(hits, 0), held[s % NX, :PTS]).astype(BF)
        for k in range(8):
            terms[k, s * EXT : (s + 1) * EXT] = found[k * EXT : (k + 1) * EXT]
    ext_t = jnp.transpose(exts[...])
    for k in range(8):
        total[k * FEAT : (k + 1) * FEAT] = mm(ext_t, terms[k])
    total[8 * FEAT :] = jnp.zeros((16, FEAT), F32)
    at = iota((112, FEAT), 0)
    for z in range(NZ):
        wide = total[pl.ds(pl.multiple_of(first_row + z * 216, 8), 120), :]
        rows = jnp.where(core == 1, wide[4:116], wide[:112])
        rows = jnp.where(at < 108, rows, jnp.where(at == 108, gain, 0.0))
        out_ref[z, :112] = rows.astype(BF)
        out_ref[z, 112:] = dense


def sum_body(got_ref, conv_ref, dense_ref):
    total = got_ref[0].astype(F32)
    for i in range(1, NZ):
        total += got_ref[i].astype(F32)
    conv_ref[...] = total[:112].astype(BF)
    for i in range(NZ):
        dense_ref[i * 16 : (i + 1) * 16] = got_ref[i, 112:]


def last_body(factor, *refs):
    groups, parts = refs[:4], refs[4 : 4 + NX * NC]
    conv_ref, gain_ref, qkv_ref, proj_ref, rows = refs[4 + NX * NC :]
    total = groups[0][...].astype(F32)
    for group in groups[1:]:
        total += group[...].astype(F32)
    conv_ref[...] = total[:108] * factor
    gain_ref[...] = total[108:109] * factor
    x, core = position()
    for s in range(NX * NC):
        source = ((x + NX - s % NX) & (NX - 1)) + NX * (core if s < NX else 1 - core)
        rows[source] = parts[s][...].astype(F32) * factor
    for b in range(NX * NC):
        part, at = b // 2, b % 2 * PTS
        if part < 3:
            qkv_ref[at : at + PTS, part * FEAT : (part + 1) * FEAT] = rows[b]
        else:
            proj_ref[at : at + PTS] = rows[b]


def shards(
    features,
    hilbert_rank,
    neighbours,
    halo_rows,
    cotangent,
    conv_weight,
    qkv_weight,
    proj_weight,
    norm_gain,
):
    factor = 1.0 / math.sqrt(PTS * NX * NZ * NC * lax.axis_size("grp"))
    rank_row = hilbert_rank.reshape(1, PTS)
    gain_row = norm_gain.reshape(1, FEAT)
    table = neighbours.T
    to_prev, to_next = call(
        pick_body, [sds((RIM, FEAT))] * 2, halo_rows, features, fetched=(0, 1), us=0.5, limit=8
    )
    from_prev = lax.ppermute(to_next, "gz", UP)
    from_next = lax.ppermute(to_prev, "gz", DOWN)
    send = call(
        conv_body,
        sds((SLOTS, FEAT + PTS)),
        features, from_prev, from_next, table, rank_row, cotangent, conv_weight,
        scratch=[pltpu.VMEM((FEAT, FEAT), BF), pltpu.VMEM((PTS, PTS), F32), pltpu.VMEM((PTS, OFFS * FEAT), BF)],
        fetched=(0, 3, 4, 5), late=(6,), us=3.0,
    )
    got = lax.all_to_all(
        send.reshape(32, 16, FEAT + PTS), "gz", split_axis=0, concat_axis=0,
        axis_index_groups=XZ_GROUPS, tiled=True,
    ).reshape(SLOTS, FEAT + PTS)
    other = lax.ppermute(got, "gz", SWAP)
    rows = 2 * HEADS * PTS
    back, grad_gain = call(
        patch_body,
        [sds((32, 32, FEAT)), sds((1, FEAT), F32)],
        got, other, qkv_weight, proj_weight, gain_row,
        scratch=[pltpu.VMEM((SLOTS, SLOTS), BF)]
        + [pltpu.VMEM((rows, FEAT), BF)] * 4
        + [pltpu.VMEM((rows, FEAT), F32)] * 2
        + [pltpu.VMEM((2 * FEAT, FEAT), BF)],
        us=6.0, limit=32,
    )
    returned = lax.all_to_all(
        back, "gz", split_axis=0, concat_axis=0, axis_index_groups=XZ_GROUPS, tiled=True
    )
    block_out, grad, grad_copies, dense = call(
        unpack_body,
        [sds((PTS, FEAT)), sds((PTS, FEAT)), sds((NX, PAY, FEAT)), sds((16, FEAT))],
        returned, rank_row, grad_gain, features, from_prev, from_next, table,
        fetched=(1, 3, 6), pinned=(1, 2, 3), us=1.5, limit=8,
    )
    near_grads, far_grads = by_chips(grad_copies)
    dense_groups = over_groups(dense)
    own_part, rim_down, rim_up = call(
        spread_body,
        [sds((PTS, FEAT), F32), sds((RIM, FEAT)), sds((RIM, FEAT))],
        grad, table, conv_weight,
        scratch=[pltpu.VMEM((OFFS * EXT, FEAT), BF), pltpu.VMEM((EXT, FEAT), F32)],
        fetched=(0, 1), late=(2,), pinned=(0, 1, 2), us=4.0,
    )
    got_down = lax.ppermute(rim_down, "gz", DOWN)
    got_up = lax.ppermute(rim_up, "gz", UP)
    parts = call(
        kernel_grad_body,
        sds((NZ, 128, FEAT)),
        *dense_groups, near_grads, far_grads, own_part,
        scratch=[
            pltpu.VMEM((NX * NC * 32, PTS), F32),
            pltpu.VMEM((NX * NC * EXT, FEAT), BF),
            pltpu.VMEM((8, NX * NC * EXT, FEAT), BF),
            pltpu.VMEM((8 * FEAT + 16, FEAT), F32),
        ],
        fetched=(0,), idle=(6,), pinned=(0,), us=5.0, limit=24,
    )
    grad_features = call(
        rim_body, sds((PTS, FEAT)), own_part, got_up, got_down, halo_rows,
        fetched=(0, 3), us=1.0, limit=8,
    )
    z_parts = lax.all_to_all(
        parts, "gz", split_axis=0, concat_axis=0, axis_index_groups=Z_GROUPS, tiled=True
    )
    conv_part, dense_sum = call(
        sum_body, [sds((112, FEAT)), sds((PTS, FEAT))], z_parts, grad_features,
        idle=(1,), us=1.0, limit=8,
    )
    grad_conv, gain_sum, grad_qkv, grad_proj = call(
        lambda *refs: last_body(factor, *refs),
        [sds((108, FEAT), F32), sds((1, FEAT), F32), sds((FEAT, 3 * FEAT), F32), sds((FEAT, FEAT), F32)],
        *over_groups(conv_part), *over_chips(dense_sum),
        scratch=[pltpu.VMEM((NX * NC, PTS, FEAT), F32)],
        limit=8,
    )
    return (block_out, grad_features, grad_conv, grad_qkv, grad_proj, gain_sum.reshape(FEAT))


def solution(mesh):
    return jax.shard_map(
        shards,
        mesh=mesh,
        in_specs=(
            P(("grp", "gz"), None),
            P(("grp", "gz")),
            P(("grp", "gz"), None),
            P(("grp", "gz"), None),
            P(("grp", "gz"), None),
            P(),
            P(),
            P(),
            P(),
        ),
        out_specs=(P(("grp", "gz"), None), P(("grp", "gz"), None), P("gz", None), P(), P(), P()),
        check_vma=False,
    )
```

```python
import math

import jax
import jax.numpy as jnp
from jax import lax
from jax.experimental import pallas as pl
from jax.experimental.pallas import tpu as pltpu
from jax.sharding import PartitionSpec as P

HEADS = 16
NORM_EPS = 1e-05
BF = jnp.bfloat16
F32 = jnp.float32
I32 = jnp.int32

PTS = 128
FEAT = 256
OFFS = 27
RIM = 16
EXT = PTS + 2 * RIM
SLOTS = 512
AT_GAIN, AT_EXT, AT_TAB, PAY = 128, 144, 304, 320
MIB = 1024 * 1024

NX, NZ, NC = 4, 8, 2
Z_GROUPS = [[x * 16 + z * 2 + c for z in range(NZ)] for x in range(NX) for c in range(NC)]
X_GROUPS = [[x * 16 + z * 2 + c for x in range(NX)] for z in range(NZ) for c in range(NC)]
XZ_GROUPS = [[x * 16 + z * 2 + c for x in range(NX) for z in range(NZ)] for c in range(NC)]
SWAP = [(i, i ^ 1) for i in range(NX * NZ * NC)]
UP = [(i, i + 1) for i in range(NX * NZ * NC - 1)]
DOWN = [(i + 1, i) for i in range(NX * NZ * NC - 1)]


def by_x(copies):
    return lax.all_to_all(copies, "gz", split_axis=0, concat_axis=0, axis_index_groups=X_GROUPS, tiled=True)


def flip(value, bit):
    return lax.ppermute(value, "gz", [(i, i ^ bit) for i in range(NX * NZ * NC)])


def over_groups(value):
    n = lax.axis_size("grp")
    return [value] + [lax.ppermute(value, "grp", [(i, (i + d) % n) for i in range(n)]) for d in range(1, n)]


def mm(a, b):
    return jnp.dot(a, b, preferred_element_type=F32)


def mm_t(a, b):
    return lax.dot_general(a, b, (((1,), (1,)), ((), ())), preferred_element_type=F32)


def t_mm(a, b):
    return lax.dot_general(a, b, (((0,), (0,)), ((), ())), preferred_element_type=F32)


def one_hot(cond):
    return jnp.where(cond, 1.0, 0.0).astype(BF)


def iota(shape, dim):
    return lax.broadcasted_iota(I32, shape, dim)


def call(body, out_shape, *args, scratch=(), us=1.0, fetched=(), late=(), idle=(), pinned=(), limit=16):
    fetched = tuple(fetched) + tuple(late)
    args = [pltpu.with_memory_space_constraint(a, pltpu.HBM) if i in fetched + tuple(idle) else a for i, a in enumerate(args)]
    specs = []
    for i in range(len(args)):
        space = pltpu.HBM if i in fetched + tuple(idle) else pltpu.VMEM
        specs.append(pl.BlockSpec(memory_space=space))
    single = not isinstance(out_shape, (list, tuple))
    outs = [out_shape] if single else list(out_shape)
    held = [pltpu.VMEM(args[i].shape, args[i].dtype) for i in fetched]
    held += [pltpu.VMEM(outs[i].shape, outs[i].dtype) for i in pinned]
    held += [pltpu.SemaphoreType.DMA] * (len(fetched) + len(pinned))
    shapes = [pltpu.HBM(o.shape, o.dtype) if i in pinned else o for i, o in enumerate(outs)]

    def outer(*refs):
        ins = list(refs[: len(args)])
        results = list(refs[len(args) : len(args) + len(outs)])
        first = len(args) + len(outs)
        extra = refs[first : first + len(scratch)]
        rest = refs[first + len(scratch) :]
        moved = len(fetched) + len(pinned)
        buffers, sems = rest[:moved], rest[moved:]
        copies = {}
        for n, i in enumerate(fetched):
            copies[i] = pltpu.make_async_copy(ins[i], buffers[n], sems[n])
            copies[i].start()
            ins[i] = buffers[n]
        for i in fetched:
            if i in late:
                ins[i] = (ins[i], copies[i].wait)
            else:
                copies[i].wait()
        leaving = []
        for n, i in enumerate(pinned):
            n += len(fetched)
            leaving.append(pltpu.make_async_copy(buffers[n], results[i], sems[n]))
            results[i] = buffers[n]
        body(*[v for i, v in enumerate(ins) if i not in idle], *results, *extra)
        for copy in leaving:
            copy.start()
        for copy in leaving:
            copy.wait()

    got = pl.pallas_call(
        outer,
        out_shape=shapes,
        in_specs=specs,
        out_specs=[pl.BlockSpec(memory_space=pltpu.HBM if i in pinned else pltpu.VMEM) for i in range(len(outs))],
        scratch_shapes=list(scratch) + held,
        compiler_params=pltpu.CompilerParams(vmem_limit_bytes=limit * MIB),
        cost_estimate=pl.CostEstimate(flops=int(us * 1.1e9), bytes_accessed=1 << 18, transcendentals=0),
    )(*args)
    return got[0] if single else got


def sds(shape, dtype=BF):
    return jax.ShapeDtypeStruct(shape, dtype)


def position():
    me = lax.axis_index("gz")
    return lax.shift_right_logical(me, 4), me & 1


def pick_body(pick_ref, feat_ref, down_ref, up_ref):
    rows = jnp.broadcast_to(pick_ref[...], (PTS, 2 * RIM))
    hit = one_hot(rows == iota((PTS, 2 * RIM), 0))
    got = t_mm(hit, feat_ref[...]).astype(BF)
    down_ref[...] = got[:RIM]
    up_ref[...] = got[RIM:]


def slot_hits(rank_row):
    owner = lax.shift_right_logical(rank_row, 7)
    wide = jnp.broadcast_to(owner, (PTS, PTS))
    tall = jnp.transpose(wide)
    earlier = (wide == tall) & (iota((PTS, PTS), 0) < iota((PTS, PTS), 1))
    slot = jnp.sum(jnp.where(earlier, 1, 0), axis=0, keepdims=True)
    target = owner * 8 + slot
    rows = iota((SLOTS, PTS), 0)
    return one_hot(rows == target), one_hot(rows == target + 4)


def conv_body(feat_ref, prev_ref, next_ref, nbr_ref, rank_ref, cot_ref, weight_ref, send_ref, ext, tab, wide):
    ext[:PTS] = feat_ref[...]
    ext[PTS : PTS + RIM] = prev_ref[...]
    ext[PTS + RIM : EXT] = next_ref[...]
    ext[EXT:] = jnp.zeros((FEAT - EXT, FEAT), BF)
    rows = ext[...]
    tab[:OFFS] = nbr_ref[...].astype(F32)
    tab[OFFS:] = jnp.zeros((PTS - OFFS, PTS), F32)
    table = jnp.transpose(tab[...])
    lanes = iota((PTS, FEAT), 1).astype(F32)
    for k in range(OFFS):
        hit = one_hot(table[:, k : k + 1] == lanes)
        wide[:, k * FEAT : (k + 1) * FEAT] = mm(hit, rows).astype(BF)
    mixed = (feat_ref[...].astype(F32) + mm(wide[...], weight_ref[...])).astype(BF)
    rank_row = rank_ref[...]
    first, second = slot_hits(rank_row)
    place = jnp.transpose(jnp.broadcast_to(rank_row & (PTS - 1), (PTS, PTS))).astype(F32)
    send_ref[:, :FEAT] = (mm(first, mixed) + mm(second, cot_ref[...])).astype(BF)
    marks = mm(first, (place + 1.0).astype(BF)) + mm(second, (place + (PTS + 1.0)).astype(BF))
    send_ref[:, FEAT:] = marks.astype(BF)


def patch_hits(marks):
    upper = lax.shift_right_logical(iota((SLOTS, PTS), 0), 3) & 1
    marks = marks.astype(F32) + jnp.where(upper == 1, 512.0, 0.0)
    lanes = iota((SLOTS, PTS), 1).astype(F32)
    return jnp.concatenate([one_hot(marks == lanes + (b + 1.0)) for b in (0, 512, 128, 640)], 1)


def layer_norm(hidden):
    centred = hidden - jnp.mean(hidden, -1, keepdims=True)
    inverse = lax.rsqrt(jnp.mean(centred * centred, -1, keepdims=True) + NORM_EPS)
    return centred * inverse, inverse


def patch_body(
    a_ref, b_ref, qkv_ref, proj_ref, gain_ref,
    back_ref, gg_ref,
    hits, qm, am, pr, ds, sc, gs, dense,
):
    x, core = position()
    whole = 2 * PTS
    head_dim = FEAT // HEADS
    scale = head_dim ** (-0.5)
    hits[...] = patch_hits(a_ref[:, FEAT:])
    rows = t_mm(hits[...], a_ref[:, :FEAT]) + t_mm(patch_hits(b_ref[:, FEAT:]), b_ref[:, :FEAT])
    hidden = rows[:whole]
    cot = rows[whole:].astype(BF)
    gain = gain_ref[...]
    normed, inverse = layer_norm(hidden)
    scaled = (normed * gain).astype(BF)
    projected = mm(scaled, qkv_ref[...]).astype(BF)
    query, keys, values = (projected[:, i * FEAT : (i + 1) * FEAT] for i in range(3))
    grad_att = mm_t(cot, proj_ref[...]).astype(BF)
    head_of = iota((PTS, FEAT), 1) // head_dim
    zero = jnp.zeros((PTS, FEAT), BF)
    halves = [slice(0, PTS), slice(PTS, whole)]
    spans = [[slice((s * HEADS + h) * PTS, (s * HEADS + h + 1) * PTS) for h in range(HEADS)] for s in range(2)]
    for s in range(2):
        for h in range(HEADS):
            qm[spans[s][h]] = jnp.where(head_of == h, query[halves[s]], zero)
            am[spans[s][h]] = jnp.where(head_of == h, grad_att[halves[s]], zero)
    sc[...] = mm_t(qm[...], keys)
    gs[...] = mm_t(am[...], values)
    for span in spans[0] + spans[1]:
        e = jnp.exp(sc[span] * scale)
        probs = (e * (1.0 / jnp.sum(e, -1, keepdims=True))).astype(BF)
        pr[span] = probs
        wide = probs.astype(F32)
        grad_probs = gs[span]
        delta = jnp.sum(wide * grad_probs, -1, keepdims=True)
        ds[span] = (wide * (grad_probs - delta) * scale).astype(BF)
    sc[...] = mm(pr[...], values)
    gs[...] = mm(ds[...], keys)
    att_parts, gq_parts, parts = [], [], []
    for s in range(2):
        att, gq = sc[spans[s][0]], gs[spans[s][0]]
        for h in range(1, HEADS):
            att = jnp.where(head_of == h, sc[spans[s][h]], att)
            gq = jnp.where(head_of == h, gs[spans[s][h]], gq)
        att_parts.append(att.astype(BF))
        gq_parts.append(gq.astype(BF))
        half = slice(s * HEADS * PTS, (s + 1) * HEADS * PTS)
        parts.append((t_mm(ds[half], qm[half]).astype(BF), t_mm(pr[half], am[half]).astype(BF)))
    attended = jnp.concatenate(att_parts, 0)
    gq = jnp.concatenate(gq_parts, 0)
    out = (hidden + mm(attended, proj_ref[...])).astype(BF)
    w_query, w_key, w_value = (qkv_ref[:, i * FEAT : (i + 1) * FEAT] for i in range(3))
    grad_scaled = mm_t(gq, w_query)
    for grad_key, grad_value in parts:
        grad_scaled += mm_t(grad_key, w_key) + mm_t(grad_value, w_value)

    @pl.when(core == 0)
    def _():
        dense[:FEAT] = t_mm(scaled, gq).astype(BF)
        dense[FEAT:] = (t_mm(scaled, parts[0][0]) + t_mm(scaled, parts[1][0])).astype(BF)

    @pl.when(core == 1)
    def _():
        dense[:FEAT] = (t_mm(scaled, parts[0][1]) + t_mm(scaled, parts[1][1])).astype(BF)
        dense[FEAT:] = t_mm(attended, cot).astype(BF)

    back_ref[:, 16:] = dense[...].reshape(32, 16, FEAT)
    gain_terms = grad_scaled * normed
    gg_ref[...] = jnp.sum(jnp.where(core == 0, gain_terms[:PTS], gain_terms[PTS:]), 0, keepdims=True)
    grad_normed = grad_scaled * gain
    grad_hidden = (
        grad_normed
        - jnp.mean(grad_normed, -1, keepdims=True)
        - normed * jnp.mean(grad_normed * normed, -1, keepdims=True)
    ) * inverse
    grad_local = (cot.astype(F32) + grad_hidden).astype(BF)
    back = mm(hits[...], jnp.concatenate([out, grad_local], 0)).astype(BF)
    back_ref[:, :16] = back.reshape(32, 16, FEAT)


def unpack_body(
    back_ref, rank_ref, gg_ref, feat_ref, prev_ref, next_ref, nbr_ref,
    block_ref, grad_ref, copies_ref, dense_ref,
):
    first, second = slot_hits(rank_ref[...])
    rows = back_ref[:, :16].reshape(SLOTS, FEAT)
    grad = t_mm(second, rows).astype(BF)
    gain = jnp.broadcast_to(gg_ref[...], (16, FEAT)).astype(BF)
    table = nbr_ref[...].astype(F32)
    table = jnp.concatenate([table, jnp.zeros((32 - OFFS, PTS), F32)], 0).astype(BF)
    grad_ref[...] = grad
    for x in range(NX):
        copies_ref[x, :AT_GAIN] = grad
        copies_ref[x, AT_GAIN:AT_EXT] = gain
        copies_ref[x, AT_EXT : AT_EXT + PTS] = feat_ref[...]
        copies_ref[x, AT_EXT + PTS : AT_EXT + PTS + RIM] = prev_ref[...]
        copies_ref[x, AT_EXT + PTS + RIM : AT_TAB] = next_ref[...]
        copies_ref[x, AT_TAB:, :PTS] = table[:16]
        copies_ref[x, AT_TAB:, PTS:] = table[16:]
    dense_ref[...] = jnp.sum(back_ref[:, 16:].astype(F32), 0).astype(BF)
    block_ref[...] = t_mm(first, rows).astype(BF)


def spread_body(grad_ref, nbr_ref, weight, own_ref, down_ref, up_ref, terms, acc):
    weight_ref, weight_here = weight
    grad = grad_ref[...]
    table = nbr_ref[...].astype(F32)
    points = iota((EXT, PTS), 0).astype(F32)
    for k in range(OFFS):
        hit = one_hot(points == table[k : k + 1])
        terms[k * EXT : (k + 1) * EXT] = mm(hit, grad).astype(BF)
    weight_here()
    acc[...] = jnp.zeros((EXT, FEAT), F32)
    for k in range(OFFS):
        acc[...] += mm_t(terms[k * EXT : (k + 1) * EXT], weight_ref[k * FEAT : (k + 1) * FEAT])
    own_ref[...] = acc[:PTS] + grad.astype(F32)
    down_ref[...] = acc[PTS : PTS + RIM].astype(BF)
    up_ref[...] = acc[PTS + RIM :].astype(BF)


def rim_body(own_ref, down_ref, up_ref, pick_ref, out_ref):
    rows = jnp.broadcast_to(pick_ref[...], (PTS, 2 * RIM))
    hit = one_hot(rows == iota((PTS, 2 * RIM), 0))
    rims = jnp.concatenate([down_ref[...], up_ref[...]], 0)
    out_ref[...] = (own_ref[...] + mm(hit, rims)).astype(BF)


def kernel_grad_body(p0, p1_ref, p2_ref, p3_ref, near_ref, far_ref, out_ref, tab, exts, terms, total):
    x, core = position()
    base = x * 1728 + core * 108
    first_offset = jnp.minimum(lax.shift_right_logical(base, 8), OFFS - 8)
    first_row = base - first_offset * FEAT - core * 4
    gain = jnp.zeros((1, FEAT), F32)
    points = iota((EXT, PTS), 0).astype(F32)
    for s in range(NX * NC):
        held = near_ref if s < NX else far_ref
        rows = held[s % NX, AT_TAB:].astype(F32)
        tab[s * 32 : s * 32 + 16] = rows[:, :PTS]
        tab[s * 32 + 16 : s * 32 + 32] = rows[:, PTS:]
        exts[s * EXT : (s + 1) * EXT] = held[s % NX, AT_EXT:AT_TAB]
        gain += held[s % NX, AT_GAIN : AT_GAIN + 1].astype(F32)
        hits = [one_hot(points == tab[pl.ds(first_offset + (s * 32 + k), 1), :]) for k in range(8)]
        found = mm(jnp.concatenate(hits, 0), held[s % NX, :PTS]).astype(BF)
        for k in range(8):
            terms[k, s * EXT : (s + 1) * EXT] = found[k * EXT : (k + 1) * EXT]
    ext_t = jnp.transpose(exts[...])
    for k in range(8):
        total[k * FEAT : (k + 1) * FEAT] = mm(ext_t, terms[k])
    total[8 * FEAT :] = jnp.zeros((16, FEAT), F32)
    p0_ref, p0_here = p0
    p0_here()
    dense = p0_ref[...].astype(F32) + p1_ref[...].astype(F32) + p2_ref[...].astype(F32) + p3_ref[...].astype(F32)
    dense = dense.astype(BF)
    at = iota((112, FEAT), 0)
    for z in range(NZ):
        wide = total[pl.ds(pl.multiple_of(first_row + z * 216, 8), 120), :]
        rows = jnp.where(core == 1, wide[4:116], wide[:112])
        rows = jnp.where(at < 108, rows, jnp.where(at == 108, gain, 0.0))
        out_ref[z, :112] = rows.astype(BF)
        out_ref[z, 112:] = dense


def sum_body(got_ref, conv_ref, dense_ref):
    total = got_ref[0].astype(F32)
    for i in range(1, NZ):
        total += got_ref[i].astype(F32)
    conv_ref[...] = total[:112].astype(BF)
    for i in range(NZ):
        dense_ref[i * 16 : (i + 1) * 16] = got_ref[i, 112:]


def middle_body(conv_ref, other_ref, dense_ref, across_ref, pair_ref, two_ref):
    pair_ref[...] = (conv_ref[...].astype(F32) + other_ref[...].astype(F32)).astype(BF)
    two_ref[0] = dense_ref[...]
    two_ref[1] = across_ref[...]


def last_body(factor, pair_ref, other_ref, *refs):
    parts, (conv_ref, gain_ref, qkv_ref, proj_ref, rows) = refs[:4], refs[4:]
    total = pair_ref[...].astype(F32) + other_ref[...].astype(F32)
    conv_ref[...] = total[:108] * factor
    gain_ref[...] = total[108:109] * factor
    x, core = position()
    for s in range(NX * NC):
        source = (x ^ (s % 2 * 2) ^ (s // 2 % 2)) + NX * (core ^ (s // 4))
        rows[source] = parts[s // 2][s % 2].astype(F32) * factor
    for b in range(NX * NC):
        part, at = b // 2, b % 2 * PTS
        if part < 3:
            qkv_ref[at : at + PTS, part * FEAT : (part + 1) * FEAT] = rows[b]
        else:
            proj_ref[at : at + PTS] = rows[b]


def shards(
    features,
    hilbert_rank,
    neighbours,
    halo_rows,
    cotangent,
    conv_weight,
    qkv_weight,
    proj_weight,
    norm_gain,
):
    factor = 1.0 / math.sqrt(PTS * NX * NZ * NC * lax.axis_size("grp"))
    rank_row = hilbert_rank.reshape(1, PTS)
    gain_row = norm_gain.reshape(1, FEAT)
    table = neighbours.T
    to_prev, to_next = call(
        pick_body, [sds((RIM, FEAT))] * 2, halo_rows, features, fetched=(0, 1), us=10.0, limit=8
    )
    from_prev = lax.ppermute(to_next, "gz", UP)
    from_next = lax.ppermute(to_prev, "gz", DOWN)
    send = call(
        conv_body,
        sds((SLOTS, FEAT + PTS)),
        features, from_prev, from_next, table, rank_row, cotangent, conv_weight,
        scratch=[pltpu.VMEM((FEAT, FEAT), BF), pltpu.VMEM((PTS, PTS), F32), pltpu.VMEM((PTS, OFFS * FEAT), BF)],
        us=3.0,
    )
    got = lax.all_to_all(
        send.reshape(32, 16, FEAT + PTS), "gz", split_axis=0, concat_axis=0,
        axis_index_groups=XZ_GROUPS, tiled=True,
    ).reshape(SLOTS, FEAT + PTS)
    other = lax.ppermute(got, "gz", SWAP)
    rows = 2 * HEADS * PTS
    back, grad_gain = call(
        patch_body,
        [sds((32, 32, FEAT)), sds((1, FEAT), F32)],
        got, other, qkv_weight, proj_weight, gain_row,
        scratch=[pltpu.VMEM((SLOTS, SLOTS), BF)]
        + [pltpu.VMEM((rows, FEAT), BF)] * 4
        + [pltpu.VMEM((rows, FEAT), F32)] * 2
        + [pltpu.VMEM((2 * FEAT, FEAT), BF)],
        us=6.0, limit=32,
    )
    returned = lax.all_to_all(
        back, "gz", split_axis=0, concat_axis=0, axis_index_groups=XZ_GROUPS, tiled=True
    )
    block_out, grad, grad_copies, dense = call(
        unpack_body,
        [sds((PTS, FEAT)), sds((PTS, FEAT)), sds((NX, PAY, FEAT)), sds((16, FEAT))],
        returned, rank_row, grad_gain, features, from_prev, from_next, table,
        pinned=(1, 2, 3), us=1.5, limit=8,
    )
    near_grads = by_x(grad_copies)
    dense_groups = over_groups(dense)
    own_part, rim_down, rim_up = call(
        spread_body,
        [sds((PTS, FEAT), F32), sds((RIM, FEAT)), sds((RIM, FEAT))],
        grad, table, conv_weight,
        scratch=[pltpu.VMEM((OFFS * EXT, FEAT), BF), pltpu.VMEM((EXT, FEAT), F32)],
        fetched=(0, 1), late=(2,), pinned=(0, 1, 2), us=4.0,
    )
    near_grads, own_part, dense_groups = lax.optimization_barrier((near_grads, own_part, dense_groups))
    far_grads = lax.ppermute(near_grads, "gz", SWAP)
    got_down = lax.ppermute(rim_down, "gz", DOWN)
    got_up = lax.ppermute(rim_up, "gz", UP)
    parts = call(
        kernel_grad_body,
        sds((NZ, 128, FEAT)),
        *dense_groups, near_grads, far_grads, own_part,
        scratch=[
            pltpu.VMEM((NX * NC * 32, PTS), F32),
            pltpu.VMEM((NX * NC * EXT, FEAT), BF),
            pltpu.VMEM((8, NX * NC * EXT, FEAT), BF),
            pltpu.VMEM((8 * FEAT + 16, FEAT), F32),
        ],
        late=(0,), idle=(6,), pinned=(0,), us=5.0, limit=24,
    )
    z_parts = lax.all_to_all(
        parts, "gz", split_axis=0, concat_axis=0, axis_index_groups=Z_GROUPS, tiled=True
    )
    z_parts, got_up, got_down = lax.optimization_barrier((z_parts, got_up, got_down))
    conv_part, dense_sum = call(
        sum_body, [sds((112, FEAT)), sds((PTS, FEAT))], z_parts, us=1.0, limit=8,
    )
    conv_pair, dense_two = call(
        middle_body, [sds((112, FEAT)), sds((2, PTS, FEAT))],
        conv_part, lax.ppermute(conv_part, "grp", [(i, i ^ 1) for i in range(4)]), dense_sum, flip(dense_sum, 32),
        us=0.5, limit=8,
    )
    conv_pair, dense_two, got_up, got_down = lax.optimization_barrier((conv_pair, dense_two, got_up, got_down))
    grad_features = call(
        rim_body, sds((PTS, FEAT)), own_part, got_up, got_down, halo_rows,
        fetched=(0, 3), us=3.0, limit=8,
    )
    conv_other = lax.ppermute(conv_pair, "grp", [(i, i ^ 2) for i in range(4)])
    dense_more = flip(dense_two, 16)
    grad_conv, gain_sum, grad_qkv, grad_proj = call(
        lambda *refs: last_body(factor, *refs),
        [sds((108, FEAT), F32), sds((1, FEAT), F32), sds((FEAT, 3 * FEAT), F32), sds((FEAT, FEAT), F32)],
        conv_pair, conv_other, dense_two, dense_more, flip(dense_two, 1), flip(dense_more, 1),
        scratch=[pltpu.VMEM((NX * NC, PTS, FEAT), F32)],
        limit=8,
    )
    return (block_out, grad_features, grad_conv, grad_qkv, grad_proj, gain_sum.reshape(FEAT))


def solution(mesh):
    return jax.shard_map(
        shards,
        mesh=mesh,
        in_specs=(
            P(("grp", "gz"), None),
            P(("grp", "gz")),
            P(("grp", "gz"), None),
            P(("grp", "gz"), None),
            P(("grp", "gz"), None),
            P(),
            P(),
            P(),
            P(),
        ),
        out_specs=(P(("grp", "gz"), None), P(("grp", "gz"), None), P("gz", None), P(), P(), P()),
        check_vma=False,
    )
```

```python
import math

import jax
import jax.numpy as jnp
from jax import lax
from jax.experimental import pallas as pl
from jax.experimental.pallas import tpu as pltpu
from jax.sharding import PartitionSpec as P

HEADS = 16
NORM_EPS = 1e-05
BF = jnp.bfloat16
F32 = jnp.float32
I32 = jnp.int32

PTS = 128
FEAT = 256
OFFS = 27
RIM = 16
EXT = PTS + 2 * RIM
SLOTS = 512
AT_GAIN, AT_EXT, AT_TAB, PAY = 128, 144, 304, 320
MIB = 1024 * 1024

NX, NZ, NC = 4, 8, 2
Z_GROUPS = [[x * 16 + z * 2 + c for z in range(NZ)] for x in range(NX) for c in range(NC)]
X_GROUPS = [[x * 16 + z * 2 + c for x in range(NX)] for z in range(NZ) for c in range(NC)]
XZ_GROUPS = [[x * 16 + z * 2 + c for x in range(NX) for z in range(NZ)] for c in range(NC)]
SWAP = [(i, i ^ 1) for i in range(NX * NZ * NC)]
UP = [(i, i + 1) for i in range(NX * NZ * NC - 1)]
DOWN = [(i + 1, i) for i in range(NX * NZ * NC - 1)]


def flip(value, bit):
    return lax.ppermute(value, "gz", [(i, i ^ bit) for i in range(NX * NZ * NC)])


def over_groups(value):
    n = lax.axis_size("grp")
    return [value] + [lax.ppermute(value, "grp", [(i, (i + d) % n) for i in range(n)]) for d in range(1, n)]


def mm(a, b):
    return jnp.dot(a, b, preferred_element_type=F32)


def mm_t(a, b):
    return lax.dot_general(a, b, (((1,), (1,)), ((), ())), preferred_element_type=F32)


def t_mm(a, b):
    return lax.dot_general(a, b, (((0,), (0,)), ((), ())), preferred_element_type=F32)


def one_hot(cond):
    return jnp.where(cond, 1.0, 0.0).astype(BF)


def iota(shape, dim):
    return lax.broadcasted_iota(I32, shape, dim)


def call(body, out_shape, *args, scratch=(), us=1.0, fetched=(), late=(), idle=(), pinned=(), limit=16):
    fetched = tuple(fetched) + tuple(late)
    args = [pltpu.with_memory_space_constraint(a, pltpu.HBM) if i in fetched + tuple(idle) else a for i, a in enumerate(args)]
    specs = []
    for i in range(len(args)):
        space = pltpu.HBM if i in fetched + tuple(idle) else pltpu.VMEM
        specs.append(pl.BlockSpec(memory_space=space))
    single = not isinstance(out_shape, (list, tuple))
    outs = [out_shape] if single else list(out_shape)
    held = [pltpu.VMEM(args[i].shape, args[i].dtype) for i in fetched]
    held += [pltpu.VMEM(outs[i].shape, outs[i].dtype) for i in pinned]
    held += [pltpu.SemaphoreType.DMA] * (len(fetched) + len(pinned))
    shapes = [pltpu.HBM(o.shape, o.dtype) if i in pinned else o for i, o in enumerate(outs)]

    def outer(*refs):
        ins = list(refs[: len(args)])
        results = list(refs[len(args) : len(args) + len(outs)])
        first = len(args) + len(outs)
        extra = refs[first : first + len(scratch)]
        rest = refs[first + len(scratch) :]
        moved = len(fetched) + len(pinned)
        buffers, sems = rest[:moved], rest[moved:]
        copies = {}
        for n, i in enumerate(fetched):
            copies[i] = pltpu.make_async_copy(ins[i], buffers[n], sems[n])
            copies[i].start()
            ins[i] = buffers[n]
        for i in fetched:
            if i in late:
                ins[i] = (ins[i], copies[i].wait)
            else:
                copies[i].wait()
        leaving = []
        for n, i in enumerate(pinned):
            n += len(fetched)
            leaving.append(pltpu.make_async_copy(buffers[n], results[i], sems[n]))
            results[i] = buffers[n]
        body(*[v for i, v in enumerate(ins) if i not in idle], *results, *extra)
        for copy in leaving:
            copy.start()
        for copy in leaving:
            copy.wait()

    got = pl.pallas_call(
        outer,
        out_shape=shapes,
        in_specs=specs,
        out_specs=[pl.BlockSpec(memory_space=pltpu.HBM if i in pinned else pltpu.VMEM) for i in range(len(outs))],
        scratch_shapes=list(scratch) + held,
        compiler_params=pltpu.CompilerParams(vmem_limit_bytes=limit * MIB),
        cost_estimate=pl.CostEstimate(flops=int(us * 1.1e9), bytes_accessed=1 << 18, transcendentals=0),
    )(*args)
    return got[0] if single else got


def sds(shape, dtype=BF):
    return jax.ShapeDtypeStruct(shape, dtype)


def position():
    me = lax.axis_index("gz")
    return lax.shift_right_logical(me, 4), me & 1


def pick_body(pick_ref, feat_ref, down_ref, up_ref):
    rows = jnp.broadcast_to(pick_ref[...], (PTS, 2 * RIM))
    hit = one_hot(rows == iota((PTS, 2 * RIM), 0))
    got = t_mm(hit, feat_ref[...]).astype(BF)
    down_ref[...] = got[:RIM]
    up_ref[...] = got[RIM:]


def slot_hits(rank_row):
    owner = lax.shift_right_logical(rank_row, 7)
    wide = jnp.broadcast_to(owner, (PTS, PTS))
    tall = jnp.transpose(wide)
    earlier = (wide == tall) & (iota((PTS, PTS), 0) < iota((PTS, PTS), 1))
    slot = jnp.sum(jnp.where(earlier, 1, 0), axis=0, keepdims=True)
    target = owner * 8 + slot
    rows = iota((SLOTS, PTS), 0)
    return one_hot(rows == target), one_hot(rows == target + 4)


def conv_body(feat_ref, prev_ref, next_ref, nbr_ref, rank_ref, cot_ref, weight_ref, send_ref, ext, tab, wide):
    ext[:PTS] = feat_ref[...]
    ext[PTS : PTS + RIM] = prev_ref[...]
    ext[PTS + RIM : EXT] = next_ref[...]
    ext[EXT:] = jnp.zeros((FEAT - EXT, FEAT), BF)
    rows = ext[...]
    tab[:OFFS] = nbr_ref[...].astype(F32)
    tab[OFFS:] = jnp.zeros((PTS - OFFS, PTS), F32)
    table = jnp.transpose(tab[...])
    lanes = iota((PTS, FEAT), 1).astype(F32)
    for k in range(OFFS):
        hit = one_hot(table[:, k : k + 1] == lanes)
        wide[:, k * FEAT : (k + 1) * FEAT] = mm(hit, rows).astype(BF)
    mixed = (feat_ref[...].astype(F32) + mm(wide[...], weight_ref[...])).astype(BF)
    rank_row = rank_ref[...]
    first, second = slot_hits(rank_row)
    place = jnp.transpose(jnp.broadcast_to(rank_row & (PTS - 1), (PTS, PTS))).astype(F32)
    send_ref[:, :FEAT] = (mm(first, mixed) + mm(second, cot_ref[...])).astype(BF)
    marks = mm(first, (place + 1.0).astype(BF)) + mm(second, (place + (PTS + 1.0)).astype(BF))
    send_ref[:, FEAT:] = marks.astype(BF)


def patch_hits(marks):
    upper = lax.shift_right_logical(iota((SLOTS, PTS), 0), 3) & 1
    marks = marks.astype(F32) + jnp.where(upper == 1, 512.0, 0.0)
    lanes = iota((SLOTS, PTS), 1).astype(F32)
    return jnp.concatenate([one_hot(marks == lanes + (b + 1.0)) for b in (0, 512, 128, 640)], 1)


def layer_norm(hidden):
    centred = hidden - jnp.mean(hidden, -1, keepdims=True)
    inverse = lax.rsqrt(jnp.mean(centred * centred, -1, keepdims=True) + NORM_EPS)
    return centred * inverse, inverse


def patch_body(
    a_ref, b_ref, qkv_ref, proj_ref, gain_ref,
    back_ref, gg_ref,
    hits, qm, am, pr, ds, sc, gs, dense,
):
    x, core = position()
    whole = 2 * PTS
    head_dim = FEAT // HEADS
    scale = head_dim ** (-0.5)
    hits[...] = patch_hits(a_ref[:, FEAT:])
    rows = t_mm(hits[...], a_ref[:, :FEAT]) + t_mm(patch_hits(b_ref[:, FEAT:]), b_ref[:, :FEAT])
    hidden = rows[:whole]
    cot = rows[whole:].astype(BF)
    gain = gain_ref[...]
    normed, inverse = layer_norm(hidden)
    scaled = (normed * gain).astype(BF)
    projected = mm(scaled, qkv_ref[...]).astype(BF)
    query, keys, values = (projected[:, i * FEAT : (i + 1) * FEAT] for i in range(3))
    grad_att = mm_t(cot, proj_ref[...]).astype(BF)
    head_of = iota((PTS, FEAT), 1) // head_dim
    zero = jnp.zeros((PTS, FEAT), BF)
    halves = [slice(0, PTS), slice(PTS, whole)]
    spans = [[slice((s * HEADS + h) * PTS, (s * HEADS + h + 1) * PTS) for h in range(HEADS)] for s in range(2)]
    for s in range(2):
        for h in range(HEADS):
            qm[spans[s][h]] = jnp.where(head_of == h, query[halves[s]], zero)
            am[spans[s][h]] = jnp.where(head_of == h, grad_att[halves[s]], zero)
    sc[...] = mm_t(qm[...], keys)
    gs[...] = mm_t(am[...], values)
    for span in spans[0] + spans[1]:
        e = jnp.exp(sc[span] * scale)
        probs = (e * (1.0 / jnp.sum(e, -1, keepdims=True))).astype(BF)
        pr[span] = probs
        wide = probs.astype(F32)
        grad_probs = gs[span]
        delta = jnp.sum(wide * grad_probs, -1, keepdims=True)
        ds[span] = (wide * (grad_probs - delta) * scale).astype(BF)
    sc[...] = mm(pr[...], values)
    gs[...] = mm(ds[...], keys)
    att_parts, gq_parts, parts = [], [], []
    for s in range(2):
        att, gq = sc[spans[s][0]], gs[spans[s][0]]
        for h in range(1, HEADS):
            att = jnp.where(head_of == h, sc[spans[s][h]], att)
            gq = jnp.where(head_of == h, gs[spans[s][h]], gq)
        att_parts.append(att.astype(BF))
        gq_parts.append(gq.astype(BF))
        half = slice(s * HEADS * PTS, (s + 1) * HEADS * PTS)
        parts.append((t_mm(ds[half], qm[half]).astype(BF), t_mm(pr[half], am[half]).astype(BF)))
    attended = jnp.concatenate(att_parts, 0)
    gq = jnp.concatenate(gq_parts, 0)
    out = (hidden + mm(attended, proj_ref[...])).astype(BF)
    w_query, w_key, w_value = (qkv_ref[:, i * FEAT : (i + 1) * FEAT] for i in range(3))
    grad_scaled = mm_t(gq, w_query)
    for grad_key, grad_value in parts:
        grad_scaled += mm_t(grad_key, w_key) + mm_t(grad_value, w_value)

    @pl.when(core == 0)
    def _():
        dense[:FEAT] = t_mm(scaled, gq).astype(BF)
        dense[FEAT:] = (t_mm(scaled, parts[0][0]) + t_mm(scaled, parts[1][0])).astype(BF)

    @pl.when(core == 1)
    def _():
        dense[:FEAT] = (t_mm(scaled, parts[0][1]) + t_mm(scaled, parts[1][1])).astype(BF)
        dense[FEAT:] = t_mm(attended, cot).astype(BF)

    back_ref[:, 16:] = dense[...].reshape(32, 16, FEAT)
    gain_terms = grad_scaled * normed
    gg_ref[...] = jnp.sum(jnp.where(core == 0, gain_terms[:PTS], gain_terms[PTS:]), 0, keepdims=True)
    grad_normed = grad_scaled * gain
    grad_hidden = (
        grad_normed
        - jnp.mean(grad_normed, -1, keepdims=True)
        - normed * jnp.mean(grad_normed * normed, -1, keepdims=True)
    ) * inverse
    grad_local = (cot.astype(F32) + grad_hidden).astype(BF)
    back = mm(hits[...], jnp.concatenate([out, grad_local], 0)).astype(BF)
    back_ref[:, :16] = back.reshape(32, 16, FEAT)


def unpack_body(
    back_ref, rank_ref, gg_ref, feat_ref, prev_ref, next_ref, nbr_ref,
    block_ref, grad_ref, copies_ref, dense_ref,
):
    first, second = slot_hits(rank_ref[...])
    rows = back_ref[:, :16].reshape(SLOTS, FEAT)
    grad = t_mm(second, rows).astype(BF)
    gain = jnp.broadcast_to(gg_ref[...], (16, FEAT)).astype(BF)
    table = nbr_ref[...].astype(F32)
    table = jnp.concatenate([table, jnp.zeros((32 - OFFS, PTS), F32)], 0).astype(BF)
    grad_ref[...] = grad
    copies_ref[:AT_GAIN] = grad
    copies_ref[AT_GAIN:AT_EXT] = gain
    copies_ref[AT_EXT : AT_EXT + PTS] = feat_ref[...]
    copies_ref[AT_EXT + PTS : AT_EXT + PTS + RIM] = prev_ref[...]
    copies_ref[AT_EXT + PTS + RIM : AT_TAB] = next_ref[...]
    copies_ref[AT_TAB:, :PTS] = table[:16]
    copies_ref[AT_TAB:, PTS:] = table[16:]
    dense_ref[...] = jnp.sum(back_ref[:, 16:].astype(F32), 0).astype(BF)
    block_ref[...] = t_mm(first, rows).astype(BF)


def spread_body(grad_ref, nbr_ref, weight_ref, own_ref, down_ref, up_ref, terms, acc):
    grad = grad_ref[...]
    table = nbr_ref[...].astype(F32)
    points = iota((EXT, PTS), 0).astype(F32)
    for k in range(OFFS):
        hit = one_hot(points == table[k : k + 1])
        terms[k * EXT : (k + 1) * EXT] = mm(hit, grad).astype(BF)
    acc[...] = jnp.zeros((EXT, FEAT), F32)
    for k in range(OFFS):
        acc[...] += mm_t(terms[k * EXT : (k + 1) * EXT], weight_ref[k * FEAT : (k + 1) * FEAT])
    own_ref[...] = acc[:PTS] + grad.astype(F32)
    down_ref[...] = acc[PTS : PTS + RIM].astype(BF)
    up_ref[...] = acc[PTS + RIM :].astype(BF)


def rim_body(own_ref, down_ref, up_ref, pick_ref, out_ref):
    rows = jnp.broadcast_to(pick_ref[...], (PTS, 2 * RIM))
    hit = one_hot(rows == iota((PTS, 2 * RIM), 0))
    rims = jnp.concatenate([down_ref[...], up_ref[...]], 0)
    out_ref[...] = (own_ref[...] + mm(hit, rims)).astype(BF)


def corner():
    x, core = position()
    base = x * 1728 + core * 108
    first_offset = jnp.minimum(lax.shift_right_logical(base, 8), OFFS - 8)
    return first_offset, base - first_offset * FEAT - core * 4, core


def chip_terms(held, first_offset, tab, exts, terms):
    gain = jnp.zeros((1, FEAT), F32)
    points = iota((EXT, PTS), 0).astype(F32)
    for s in range(NX):
        rows = held[s][AT_TAB:].astype(F32)
        tab[s * 32 : s * 32 + 16] = rows[:, :PTS]
        tab[s * 32 + 16 : s * 32 + 32] = rows[:, PTS:]
        exts[s * EXT : (s + 1) * EXT] = held[s][AT_EXT:AT_TAB]
        gain += held[s][AT_GAIN : AT_GAIN + 1].astype(F32)
        hits = [one_hot(points == tab[pl.ds(first_offset + (s * 32 + k), 1), :]) for k in range(8)]
        found = mm(jnp.concatenate(hits, 0), held[s][:PTS]).astype(BF)
        for k in range(8):
            terms[k, s * EXT : (s + 1) * EXT] = found[k * EXT : (k + 1) * EXT]
    return gain, jnp.transpose(exts[...])


def near_grad_body(h0, h1, h2, h3, total_ref, gain_ref, tab, exts, terms):
    held = (h0, h1, h2, h3)
    first_offset, _, _ = corner()
    gain, ext_t = chip_terms(held, first_offset, tab, exts, terms)
    gain_ref[...] = gain
    for k in range(8):
        total_ref[k * FEAT : (k + 1) * FEAT] = mm(ext_t, terms[k])
    total_ref[8 * FEAT :] = jnp.zeros((16, FEAT), F32)


def kernel_grad_body(p0_ref, p1_ref, p2_ref, p3_ref, near_ref, gain_ref, h0, h1, h2, h3, out_ref, tab, exts, terms, total):
    held = (h0, h1, h2, h3)
    first_offset, first_row, core = corner()
    gain, ext_t = chip_terms(held, first_offset, tab, exts, terms)
    gain = gain + gain_ref[...]
    for k in range(8):
        span = slice(k * FEAT, (k + 1) * FEAT)
        total[span] = near_ref[span] + mm(ext_t, terms[k])
    total[8 * FEAT :] = jnp.zeros((16, FEAT), F32)
    dense = p0_ref[...].astype(F32) + p1_ref[...].astype(F32) + p2_ref[...].astype(F32) + p3_ref[...].astype(F32)
    dense = dense.astype(BF)
    at = iota((112, FEAT), 0)
    for z in range(NZ):
        wide = total[pl.ds(pl.multiple_of(first_row + z * 216, 8), 120), :]
        rows = jnp.where(core == 1, wide[4:116], wide[:112])
        rows = jnp.where(at < 108, rows, jnp.where(at == 108, gain, 0.0))
        out_ref[z, :112] = rows.astype(BF)
        out_ref[z, 112:] = dense


def sum_body(got_ref, conv_ref, dense_ref):
    total = got_ref[0].astype(F32)
    for i in range(1, NZ):
        total += got_ref[i].astype(F32)
    conv_ref[...] = total[:112].astype(BF)
    for i in range(NZ):
        dense_ref[i * 16 : (i + 1) * 16] = got_ref[i, 112:]


def middle_body(conv_ref, other_ref, dense_ref, across_ref, pair_ref, two_ref):
    pair_ref[...] = (conv_ref[...].astype(F32) + other_ref[...].astype(F32)).astype(BF)
    two_ref[0] = dense_ref[...]
    two_ref[1] = across_ref[...]


def last_body(factor, pair_ref, other_ref, *refs):
    parts, (conv_ref, gain_ref, qkv_ref, proj_ref, rows) = refs[:4], refs[4:]
    total = pair_ref[...].astype(F32) + other_ref[...].astype(F32)
    conv_ref[...] = total[:108] * factor
    gain_ref[...] = total[108:109] * factor
    x, core = position()
    for s in range(NX * NC):
        source = (x ^ (s % 2 * 2) ^ (s // 2 % 2)) + NX * (core ^ (s // 4))
        rows[source] = parts[s // 2][s % 2].astype(F32) * factor
    for b in range(NX * NC):
        part, at = b // 2, b % 2 * PTS
        if part < 3:
            qkv_ref[at : at + PTS, part * FEAT : (part + 1) * FEAT] = rows[b]
        else:
            proj_ref[at : at + PTS] = rows[b]


def shards(
    features,
    hilbert_rank,
    neighbours,
    halo_rows,
    cotangent,
    conv_weight,
    qkv_weight,
    proj_weight,
    norm_gain,
):
    factor = 1.0 / math.sqrt(PTS * NX * NZ * NC * lax.axis_size("grp"))
    rank_row = hilbert_rank.reshape(1, PTS)
    gain_row = norm_gain.reshape(1, FEAT)
    table = neighbours.T
    to_prev, to_next = call(
        pick_body, [sds((RIM, FEAT))] * 2, halo_rows, features, fetched=(0, 1), us=10.0, limit=8
    )
    from_prev = lax.ppermute(to_next, "gz", UP)
    from_next = lax.ppermute(to_prev, "gz", DOWN)
    send = call(
        conv_body,
        sds((SLOTS, FEAT + PTS)),
        features, from_prev, from_next, table, rank_row, cotangent, conv_weight,
        scratch=[pltpu.VMEM((FEAT, FEAT), BF), pltpu.VMEM((PTS, PTS), F32), pltpu.VMEM((PTS, OFFS * FEAT), BF)],
        us=3.0,
    )
    got = lax.all_to_all(
        send.reshape(32, 16, FEAT + PTS), "gz", split_axis=0, concat_axis=0,
        axis_index_groups=XZ_GROUPS, tiled=True,
    ).reshape(SLOTS, FEAT + PTS)
    other = lax.ppermute(got, "gz", SWAP)
    rows = 2 * HEADS * PTS
    back, grad_gain = call(
        patch_body,
        [sds((32, 32, FEAT)), sds((1, FEAT), F32)],
        got, other, qkv_weight, proj_weight, gain_row,
        scratch=[pltpu.VMEM((SLOTS, SLOTS), BF)]
        + [pltpu.VMEM((rows, FEAT), BF)] * 4
        + [pltpu.VMEM((rows, FEAT), F32)] * 2
        + [pltpu.VMEM((2 * FEAT, FEAT), BF)],
        us=6.0, limit=32,
    )
    returned = lax.all_to_all(
        back, "gz", split_axis=0, concat_axis=0, axis_index_groups=XZ_GROUPS, tiled=True
    )
    block_out, grad, grad_copies, dense = call(
        unpack_body,
        [sds((PTS, FEAT)), sds((PTS, FEAT)), sds((PAY, FEAT)), sds((16, FEAT))],
        returned, rank_row, grad_gain, features, from_prev, from_next, table,
        us=1.5, limit=8,
    )
    near_grads = [grad_copies] + [flip(grad_copies, 16 * d) for d in (1, 3, 2)]
    dense_groups = over_groups(dense)
    own_part, rim_down, rim_up = call(
        spread_body,
        [sds((PTS, FEAT), F32), sds((RIM, FEAT)), sds((RIM, FEAT))],
        grad, table, conv_weight,
        scratch=[pltpu.VMEM((OFFS * EXT, FEAT), BF), pltpu.VMEM((EXT, FEAT), F32)],
        pinned=(0, 1, 2), us=3.0,
    )
    near_grads, own_part, dense_groups = lax.optimization_barrier((near_grads, own_part, dense_groups))
    far_grads = [flip(v, 1) for v in near_grads]
    got_down = lax.ppermute(rim_down, "gz", DOWN)
    got_up = lax.ppermute(rim_up, "gz", UP)
    held_scratch = [
        pltpu.VMEM((NX * 32, PTS), F32),
        pltpu.VMEM((NX * EXT, FEAT), BF),
        pltpu.VMEM((8, NX * EXT, FEAT), BF),
    ]
    total_rows = 8 * FEAT + 16
    near_total, near_gain = call(
        near_grad_body, [sds((total_rows, FEAT), F32), sds((1, FEAT), F32)], *near_grads,
        scratch=held_scratch, us=3.0, limit=16,
    )
    parts = call(
        kernel_grad_body,
        sds((NZ, 128, FEAT)),
        *dense_groups, near_total, near_gain, *far_grads, own_part,
        scratch=held_scratch + [pltpu.VMEM((total_rows, FEAT), F32)],
        idle=(10,), pinned=(0,), us=5.0, limit=24,
    )
    z_parts = lax.all_to_all(
        parts, "gz", split_axis=0, concat_axis=0, axis_index_groups=Z_GROUPS, tiled=True
    )
    z_parts, got_up, got_down = lax.optimization_barrier((z_parts, got_up, got_down))
    conv_part, dense_sum = call(
        sum_body, [sds((112, FEAT)), sds((PTS, FEAT))], z_parts, us=1.0, limit=8,
    )
    conv_pair, dense_two = call(
        middle_body, [sds((112, FEAT)), sds((2, PTS, FEAT))],
        conv_part, lax.ppermute(conv_part, "grp", [(i, i ^ 1) for i in range(4)]), dense_sum, flip(dense_sum, 32),
        us=0.5, limit=8,
    )
    conv_pair, dense_two, got_up, got_down = lax.optimization_barrier((conv_pair, dense_two, got_up, got_down))
    grad_features = call(
        rim_body, sds((PTS, FEAT)), own_part, got_up, got_down, halo_rows,
        fetched=(0, 3), us=3.0, limit=8,
    )
    conv_other = lax.ppermute(conv_pair, "grp", [(i, i ^ 2) for i in range(4)])
    dense_more = flip(dense_two, 16)
    grad_conv, gain_sum, grad_qkv, grad_proj = call(
        lambda *refs: last_body(factor, *refs),
        [sds((108, FEAT), F32), sds((1, FEAT), F32), sds((FEAT, 3 * FEAT), F32), sds((FEAT, FEAT), F32)],
        conv_pair, conv_other, dense_two, dense_more, flip(dense_two, 1), flip(dense_more, 1),
        scratch=[pltpu.VMEM((NX * NC, PTS, FEAT), F32)],
        limit=8,
    )
    return (block_out, grad_features, grad_conv, grad_qkv, grad_proj, gain_sum.reshape(FEAT))


def solution(mesh):
    return jax.shard_map(
        shards,
        mesh=mesh,
        in_specs=(
            P(("grp", "gz"), None),
            P(("grp", "gz")),
            P(("grp", "gz"), None),
            P(("grp", "gz"), None),
            P(("grp", "gz"), None),
            P(),
            P(),
            P(),
            P(),
        ),
        out_specs=(P(("grp", "gz"), None), P(("grp", "gz"), None), P("gz", None), P(), P(), P()),
        check_vma=False,
    )
```

```python
import math

import jax
import jax.numpy as jnp
from jax import lax
from jax.experimental import pallas as pl
from jax.experimental.pallas import tpu as pltpu
from jax.sharding import PartitionSpec as P

HEADS = 16
NORM_EPS = 1e-05
BF = jnp.bfloat16
F32 = jnp.float32
I32 = jnp.int32

PTS = 128
FEAT = 256
OFFS = 27
RIM = 16
EXT = PTS + 2 * RIM
SLOTS = 512
AT_EXT, AT_TAB, PAY = 128, 288, 304
MIB = 1024 * 1024

NX, NZ, NC = 4, 8, 2
Z_GROUPS = [[x * 16 + z * 2 + c for z in range(NZ)] for x in range(NX) for c in range(NC)]
X_GROUPS = [[x * 16 + z * 2 + c for x in range(NX)] for z in range(NZ) for c in range(NC)]
XZ_GROUPS = [[x * 16 + z * 2 + c for x in range(NX) for z in range(NZ)] for c in range(NC)]
SWAP = [(i, i ^ 1) for i in range(NX * NZ * NC)]
UP = [(i, i + 1) for i in range(NX * NZ * NC - 1)]
DOWN = [(i + 1, i) for i in range(NX * NZ * NC - 1)]


def flip(value, bit):
    return lax.ppermute(value, "gz", [(i, i ^ bit) for i in range(NX * NZ * NC)])


def over_groups(value):
    n = lax.axis_size("grp")
    return [value] + [lax.ppermute(value, "grp", [(i, (i + d) % n) for i in range(n)]) for d in range(1, n)]


def mm(a, b):
    return jnp.dot(a, b, preferred_element_type=F32)


def mm_t(a, b):
    return lax.dot_general(a, b, (((1,), (1,)), ((), ())), preferred_element_type=F32)


def t_mm(a, b):
    return lax.dot_general(a, b, (((0,), (0,)), ((), ())), preferred_element_type=F32)


def one_hot(cond):
    return jnp.where(cond, 1.0, 0.0).astype(BF)


def iota(shape, dim):
    return lax.broadcasted_iota(I32, shape, dim)


def call(body, out_shape, *args, scratch=(), us=1.0, fetched=(), late=(), idle=(), pinned=(), limit=16):
    fetched = tuple(fetched) + tuple(late)
    args = [pltpu.with_memory_space_constraint(a, pltpu.HBM) if i in fetched + tuple(idle) else a for i, a in enumerate(args)]
    specs = []
    for i in range(len(args)):
        space = pltpu.HBM if i in fetched + tuple(idle) else pltpu.VMEM
        specs.append(pl.BlockSpec(memory_space=space))
    single = not isinstance(out_shape, (list, tuple))
    outs = [out_shape] if single else list(out_shape)
    held = [pltpu.VMEM(args[i].shape, args[i].dtype) for i in fetched]
    held += [pltpu.VMEM(outs[i].shape, outs[i].dtype) for i in pinned]
    held += [pltpu.SemaphoreType.DMA] * (len(fetched) + len(pinned))
    shapes = [pltpu.HBM(o.shape, o.dtype) if i in pinned else o for i, o in enumerate(outs)]

    def outer(*refs):
        ins = list(refs[: len(args)])
        results = list(refs[len(args) : len(args) + len(outs)])
        first = len(args) + len(outs)
        extra = refs[first : first + len(scratch)]
        rest = refs[first + len(scratch) :]
        moved = len(fetched) + len(pinned)
        buffers, sems = rest[:moved], rest[moved:]
        copies = {}
        for n, i in enumerate(fetched):
            copies[i] = pltpu.make_async_copy(ins[i], buffers[n], sems[n])
            copies[i].start()
            ins[i] = buffers[n]
        for i in fetched:
            if i in late:
                ins[i] = (ins[i], copies[i].wait)
            else:
                copies[i].wait()
        leaving = []
        for n, i in enumerate(pinned):
            n += len(fetched)
            leaving.append(pltpu.make_async_copy(buffers[n], results[i], sems[n]))
            results[i] = buffers[n]
        body(*[v for i, v in enumerate(ins) if i not in idle], *results, *extra)
        for copy in leaving:
            copy.start()
        for copy in leaving:
            copy.wait()

    got = pl.pallas_call(
        outer,
        out_shape=shapes,
        in_specs=specs,
        out_specs=[pl.BlockSpec(memory_space=pltpu.HBM if i in pinned else pltpu.VMEM) for i in range(len(outs))],
        scratch_shapes=list(scratch) + held,
        compiler_params=pltpu.CompilerParams(vmem_limit_bytes=limit * MIB),
        cost_estimate=pl.CostEstimate(flops=int(us * 1.1e9), bytes_accessed=1 << 18, transcendentals=0),
    )(*args)
    return got[0] if single else got


def sds(shape, dtype=BF):
    return jax.ShapeDtypeStruct(shape, dtype)


def position():
    me = lax.axis_index("gz")
    return lax.shift_right_logical(me, 4), me & 1


def pick_body(pick_ref, feat_ref, down_ref, up_ref):
    rows = jnp.broadcast_to(pick_ref[...], (PTS, 2 * RIM))
    hit = one_hot(rows == iota((PTS, 2 * RIM), 0))
    got = t_mm(hit, feat_ref[...]).astype(BF)
    down_ref[...] = got[:RIM]
    up_ref[...] = got[RIM:]


def slot_hits(rank_row):
    owner = lax.shift_right_logical(rank_row, 7)
    wide = jnp.broadcast_to(owner, (PTS, PTS))
    tall = jnp.transpose(wide)
    earlier = (wide == tall) & (iota((PTS, PTS), 0) < iota((PTS, PTS), 1))
    slot = jnp.sum(jnp.where(earlier, 1, 0), axis=0, keepdims=True)
    target = owner * 8 + slot
    rows = iota((SLOTS, PTS), 0)
    return one_hot(rows == target), one_hot(rows == target + 4)


def conv_body(feat_ref, prev_ref, next_ref, nbr_ref, rank_ref, cot_ref, weight_ref, send_ref, ext, tab, wide):
    ext[:PTS] = feat_ref[...]
    ext[PTS : PTS + RIM] = prev_ref[...]
    ext[PTS + RIM : EXT] = next_ref[...]
    ext[EXT:] = jnp.zeros((FEAT - EXT, FEAT), BF)
    rows = ext[...]
    tab[:OFFS] = nbr_ref[...].astype(F32)
    tab[OFFS:] = jnp.zeros((PTS - OFFS, PTS), F32)
    table = jnp.transpose(tab[...])
    lanes = iota((PTS, FEAT), 1).astype(F32)
    for k in range(OFFS):
        hit = one_hot(table[:, k : k + 1] == lanes)
        wide[:, k * FEAT : (k + 1) * FEAT] = mm(hit, rows).astype(BF)
    mixed = (feat_ref[...].astype(F32) + mm(wide[...], weight_ref[...])).astype(BF)
    rank_row = rank_ref[...]
    first, second = slot_hits(rank_row)
    place = jnp.transpose(jnp.broadcast_to(rank_row & (PTS - 1), (PTS, PTS))).astype(F32)
    send_ref[:, :FEAT] = (mm(first, mixed) + mm(second, cot_ref[...])).astype(BF)
    marks = mm(first, (place + 1.0).astype(BF)) + mm(second, (place + (PTS + 1.0)).astype(BF))
    send_ref[:, FEAT:] = marks.astype(BF)


def patch_hits(marks):
    upper = lax.shift_right_logical(iota((SLOTS, PTS), 0), 3) & 1
    marks = marks.astype(F32) + jnp.where(upper == 1, 512.0, 0.0)
    lanes = iota((SLOTS, PTS), 1).astype(F32)
    return jnp.concatenate([one_hot(marks == lanes + (b + 1.0)) for b in (0, 512, 128, 640)], 1)


def layer_norm(hidden):
    centred = hidden - jnp.mean(hidden, -1, keepdims=True)
    inverse = lax.rsqrt(jnp.mean(centred * centred, -1, keepdims=True) + NORM_EPS)
    return centred * inverse, inverse


def patch_body(
    a_ref, b_ref, qkv_ref, proj_ref, gain_ref,
    back_ref, gg_ref,
    hits, qm, am, pr, ds, sc, gs, dense,
):
    x, core = position()
    whole = 2 * PTS
    head_dim = FEAT // HEADS
    scale = head_dim ** (-0.5)
    hits[...] = patch_hits(a_ref[:, FEAT:])
    rows = t_mm(hits[...], a_ref[:, :FEAT]) + t_mm(patch_hits(b_ref[:, FEAT:]), b_ref[:, :FEAT])
    hidden = rows[:whole]
    cot = rows[whole:].astype(BF)
    gain = gain_ref[...]
    normed, inverse = layer_norm(hidden)
    scaled = (normed * gain).astype(BF)
    projected = mm(scaled, qkv_ref[...]).astype(BF)
    query, keys, values = (projected[:, i * FEAT : (i + 1) * FEAT] for i in range(3))
    grad_att = mm_t(cot, proj_ref[...]).astype(BF)
    head_of = iota((PTS, FEAT), 1) // head_dim
    zero = jnp.zeros((PTS, FEAT), BF)
    halves = [slice(0, PTS), slice(PTS, whole)]
    spans = [[slice((s * HEADS + h) * PTS, (s * HEADS + h + 1) * PTS) for h in range(HEADS)] for s in range(2)]
    for s in range(2):
        for h in range(HEADS):
            qm[spans[s][h]] = jnp.where(head_of == h, query[halves[s]], zero)
            am[spans[s][h]] = jnp.where(head_of == h, grad_att[halves[s]], zero)
    sc[...] = mm_t(qm[...], keys)
    gs[...] = mm_t(am[...], values)
    for span in spans[0] + spans[1]:
        e = jnp.exp(sc[span] * scale)
        probs = (e * (1.0 / jnp.sum(e, -1, keepdims=True))).astype(BF)
        pr[span] = probs
        wide = probs.astype(F32)
        grad_probs = gs[span]
        delta = jnp.sum(wide * grad_probs, -1, keepdims=True)
        ds[span] = (wide * (grad_probs - delta) * scale).astype(BF)
    sc[...] = mm(pr[...], values)
    gs[...] = mm(ds[...], keys)
    att_parts, gq_parts, parts = [], [], []
    for s in range(2):
        att, gq = sc[spans[s][0]], gs[spans[s][0]]
        for h in range(1, HEADS):
            att = jnp.where(head_of == h, sc[spans[s][h]], att)
            gq = jnp.where(head_of == h, gs[spans[s][h]], gq)
        att_parts.append(att.astype(BF))
        gq_parts.append(gq.astype(BF))
        half = slice(s * HEADS * PTS, (s + 1) * HEADS * PTS)
        parts.append((t_mm(ds[half], qm[half]).astype(BF), t_mm(pr[half], am[half]).astype(BF)))
    attended = jnp.concatenate(att_parts, 0)
    gq = jnp.concatenate(gq_parts, 0)
    out = (hidden + mm(attended, proj_ref[...])).astype(BF)
    w_query, w_key, w_value = (qkv_ref[:, i * FEAT : (i + 1) * FEAT] for i in range(3))
    grad_scaled = mm_t(gq, w_query)
    for grad_key, grad_value in parts:
        grad_scaled += mm_t(grad_key, w_key) + mm_t(grad_value, w_value)

    @pl.when(core == 0)
    def _():
        dense[:FEAT] = t_mm(scaled, gq).astype(BF)
        dense[FEAT:] = (t_mm(scaled, parts[0][0]) + t_mm(scaled, parts[1][0])).astype(BF)

    @pl.when(core == 1)
    def _():
        dense[:FEAT] = (t_mm(scaled, parts[0][1]) + t_mm(scaled, parts[1][1])).astype(BF)
        dense[FEAT:] = t_mm(attended, cot).astype(BF)

    back_ref[:, 16:] = dense[...].reshape(32, 16, FEAT)
    gain_terms = grad_scaled * normed
    gg_ref[...] = jnp.sum(jnp.where(core == 0, gain_terms[:PTS], gain_terms[PTS:]), 0, keepdims=True)
    grad_normed = grad_scaled * gain
    grad_hidden = (
        grad_normed
        - jnp.mean(grad_normed, -1, keepdims=True)
        - normed * jnp.mean(grad_normed * normed, -1, keepdims=True)
    ) * inverse
    grad_local = (cot.astype(F32) + grad_hidden).astype(BF)
    back = mm(hits[...], jnp.concatenate([out, grad_local], 0)).astype(BF)
    back_ref[:, :16] = back.reshape(32, 16, FEAT)


def unpack_body(
    back_ref, rank_ref, gg_ref, feat_ref, prev_ref, next_ref, nbr_ref,
    block_ref, grad_ref, copies_ref, dense_ref,
):
    first, second = slot_hits(rank_ref[...])
    rows = back_ref[:, :16].reshape(SLOTS, FEAT)
    grad = t_mm(second, rows).astype(BF)
    table = nbr_ref[...].astype(F32)
    low = jnp.concatenate([table[16:], jnp.zeros((32 - OFFS, PTS), F32)], 0)
    at = iota((16, PTS), 0)
    gain = gg_ref[...]
    low = jnp.where(at == 12, gain[:, :PTS], jnp.where(at == 14, gain[:, PTS:], low))
    grad_ref[...] = grad
    copies_ref[:PTS] = grad
    copies_ref[AT_EXT : AT_EXT + PTS] = feat_ref[...]
    copies_ref[AT_EXT + PTS : AT_EXT + PTS + RIM] = prev_ref[...]
    copies_ref[AT_EXT + PTS + RIM : AT_TAB] = next_ref[...]
    copies_ref[AT_TAB:, :PTS] = table[:16].astype(BF)
    copies_ref[AT_TAB:, PTS:] = low.astype(BF)
    dense_ref[...] = jnp.sum(back_ref[:, 16:].astype(F32), 0).astype(BF)
    block_ref[...] = t_mm(first, rows).astype(BF)


def spread_body(grad_ref, nbr_ref, weight_ref, own_ref, down_ref, up_ref, terms, acc):
    grad = grad_ref[...]
    table = nbr_ref[...].astype(F32)
    points = iota((EXT, PTS), 0).astype(F32)
    for k in range(OFFS):
        hit = one_hot(points == table[k : k + 1])
        terms[k * EXT : (k + 1) * EXT] = mm(hit, grad).astype(BF)
    acc[...] = jnp.zeros((EXT, FEAT), F32)
    for k in range(OFFS):
        acc[...] += mm_t(terms[k * EXT : (k + 1) * EXT], weight_ref[k * FEAT : (k + 1) * FEAT])
    own_ref[...] = acc[:PTS] + grad.astype(F32)
    down_ref[...] = acc[PTS : PTS + RIM].astype(BF)
    up_ref[...] = acc[PTS + RIM :].astype(BF)


def rim_body(own_ref, down_ref, up_ref, pick_ref, out_ref):
    rows = jnp.broadcast_to(pick_ref[...], (PTS, 2 * RIM))
    hit = one_hot(rows == iota((PTS, 2 * RIM), 0))
    rims = jnp.concatenate([down_ref[...], up_ref[...]], 0)
    out_ref[...] = (own_ref[...] + mm(hit, rims)).astype(BF)


def corner():
    x, core = position()
    base = x * 1728 + core * 108
    first_offset = jnp.minimum(lax.shift_right_logical(base, 8), OFFS - 8)
    return first_offset, base - first_offset * FEAT - core * 4, core


def chip_terms(held, first_offset, tab, exts, terms):
    gain = jnp.zeros((1, FEAT), F32)
    points = iota((EXT, PTS), 0).astype(F32)
    for s in range(NX):
        rows = held[s][AT_TAB:].astype(F32)
        tab[s * 32 : s * 32 + 16] = rows[:, :PTS]
        tab[s * 32 + 16 : s * 32 + 32] = rows[:, PTS:]
        exts[s * EXT : (s + 1) * EXT] = held[s][AT_EXT:AT_TAB]
        gain += jnp.concatenate([rows[12:13, PTS:], rows[14:15, PTS:]], 1)
        hits = [one_hot(points == tab[pl.ds(first_offset + (s * 32 + k), 1), :]) for k in range(8)]
        found = mm(jnp.concatenate(hits, 0), held[s][:PTS]).astype(BF)
        for k in range(8):
            terms[k, s * EXT : (s + 1) * EXT] = found[k * EXT : (k + 1) * EXT]
    return gain, jnp.transpose(exts[...])


def near_grad_body(h0, h1, h2, h3, total_ref, gain_ref, tab, exts, terms):
    held = (h0, h1, h2, h3)
    first_offset, _, _ = corner()
    gain, ext_t = chip_terms(held, first_offset, tab, exts, terms)
    gain_ref[...] = gain
    for k in range(8):
        total_ref[k * FEAT : (k + 1) * FEAT] = mm(ext_t, terms[k])
    total_ref[8 * FEAT :] = jnp.zeros((16, FEAT), F32)


def kernel_grad_body(p0_ref, p1_ref, p2_ref, p3_ref, near_ref, gain_ref, h0, h1, h2, h3, out_ref, tab, exts, terms, total):
    held = (h0, h1, h2, h3)
    first_offset, first_row, core = corner()
    gain, ext_t = chip_terms(held, first_offset, tab, exts, terms)
    gain = gain + gain_ref[...]
    for k in range(8):
        span = slice(k * FEAT, (k + 1) * FEAT)
        total[span] = near_ref[span] + mm(ext_t, terms[k])
    total[8 * FEAT :] = jnp.zeros((16, FEAT), F32)
    dense = p0_ref[...].astype(F32) + p1_ref[...].astype(F32) + p2_ref[...].astype(F32) + p3_ref[...].astype(F32)
    dense = dense.astype(BF)
    at = iota((112, FEAT), 0)
    for z in range(NZ):
        wide = total[pl.ds(pl.multiple_of(first_row + z * 216, 8), 120), :]
        rows = jnp.where(core == 1, wide[4:116], wide[:112])
        rows = jnp.where(at < 108, rows, jnp.where(at == 108, gain, 0.0))
        out_ref[z, :112] = rows.astype(BF)
        out_ref[z, 112:] = dense


def sum_body(got_ref, conv_ref, dense_ref):
    total = got_ref[0].astype(F32)
    for i in range(1, NZ):
        total += got_ref[i].astype(F32)
    conv_ref[...] = total[:112].astype(BF)
    for i in range(NZ):
        dense_ref[i * 16 : (i + 1) * 16] = got_ref[i, 112:]


def middle_body(conv_ref, other_ref, dense_ref, across_ref, pair_ref, two_ref):
    pair_ref[...] = (conv_ref[...].astype(F32) + other_ref[...].astype(F32)).astype(BF)
    two_ref[0] = dense_ref[...]
    two_ref[1] = across_ref[...]


def last_body(factor, pair_ref, other_ref, *refs):
    parts, (conv_ref, gain_ref, qkv_ref, proj_ref, rows) = refs[:4], refs[4:]
    total = pair_ref[...].astype(F32) + other_ref[...].astype(F32)
    conv_ref[...] = total[:108] * factor
    gain_ref[...] = total[108:109] * factor
    x, core = position()
    for s in range(NX * NC):
        source = (x ^ (s % 2 * 2) ^ (s // 2 % 2)) + NX * (core ^ (s // 4))
        rows[source] = parts[s // 2][s % 2].astype(F32) * factor
    for b in range(NX * NC):
        part, at = b // 2, b % 2 * PTS
        if part < 3:
            qkv_ref[at : at + PTS, part * FEAT : (part + 1) * FEAT] = rows[b]
        else:
            proj_ref[at : at + PTS] = rows[b]


def shards(
    features,
    hilbert_rank,
    neighbours,
    halo_rows,
    cotangent,
    conv_weight,
    qkv_weight,
    proj_weight,
    norm_gain,
):
    factor = 1.0 / math.sqrt(PTS * NX * NZ * NC * lax.axis_size("grp"))
    rank_row = hilbert_rank.reshape(1, PTS)
    gain_row = norm_gain.reshape(1, FEAT)
    table = neighbours.T
    to_prev, to_next = call(
        pick_body, [sds((RIM, FEAT))] * 2, halo_rows, features, fetched=(0, 1), us=10.0, limit=8
    )
    from_prev = lax.ppermute(to_next, "gz", UP)
    from_next = lax.ppermute(to_prev, "gz", DOWN)
    send = call(
        conv_body,
        sds((SLOTS, FEAT + PTS)),
        features, from_prev, from_next, table, rank_row, cotangent, conv_weight,
        scratch=[pltpu.VMEM((FEAT, FEAT), BF), pltpu.VMEM((PTS, PTS), F32), pltpu.VMEM((PTS, OFFS * FEAT), BF)],
        us=3.0,
    )
    got = lax.all_to_all(
        send.reshape(32, 16, FEAT + PTS), "gz", split_axis=0, concat_axis=0,
        axis_index_groups=XZ_GROUPS, tiled=True,
    ).reshape(SLOTS, FEAT + PTS)
    other = lax.ppermute(got, "gz", SWAP)
    rows = 2 * HEADS * PTS
    back, grad_gain = call(
        patch_body,
        [sds((32, 32, FEAT)), sds((1, FEAT), F32)],
        got, other, qkv_weight, proj_weight, gain_row,
        scratch=[pltpu.VMEM((SLOTS, SLOTS), BF)]
        + [pltpu.VMEM((rows, FEAT), BF)] * 4
        + [pltpu.VMEM((rows, FEAT), F32)] * 2
        + [pltpu.VMEM((2 * FEAT, FEAT), BF)],
        us=6.0, limit=32,
    )
    returned = lax.all_to_all(
        back, "gz", split_axis=0, concat_axis=0, axis_index_groups=XZ_GROUPS, tiled=True
    )
    block_out, grad, grad_copies, dense = call(
        unpack_body,
        [sds((PTS, FEAT)), sds((PTS, FEAT)), sds((PAY, FEAT)), sds((16, FEAT))],
        returned, rank_row, grad_gain, features, from_prev, from_next, table,
        us=1.5, limit=8,
    )
    near_grads = [grad_copies] + [flip(grad_copies, 16 * d) for d in (1, 3, 2)]
    dense_groups = over_groups(dense)
    own_part, rim_down, rim_up = call(
        spread_body,
        [sds((PTS, FEAT), F32), sds((RIM, FEAT)), sds((RIM, FEAT))],
        grad, table, conv_weight,
        scratch=[pltpu.VMEM((OFFS * EXT, FEAT), BF), pltpu.VMEM((EXT, FEAT), F32)],
        pinned=(0, 1, 2), us=3.0,
    )
    near_grads, own_part, dense_groups = lax.optimization_barrier((near_grads, own_part, dense_groups))
    far_grads = [flip(v, 1) for v in near_grads]
    got_down = lax.ppermute(rim_down, "gz", DOWN)
    got_up = lax.ppermute(rim_up, "gz", UP)
    held_scratch = [
        pltpu.VMEM((NX * 32, PTS), F32),
        pltpu.VMEM((NX * EXT, FEAT), BF),
        pltpu.VMEM((8, NX * EXT, FEAT), BF),
    ]
    total_rows = 8 * FEAT + 16
    near_total, near_gain = call(
        near_grad_body, [sds((total_rows, FEAT), F32), sds((1, FEAT), F32)], *near_grads,
        scratch=held_scratch, us=3.0, limit=16,
    )
    parts = call(
        kernel_grad_body,
        sds((NZ, 128, FEAT)),
        *dense_groups, near_total, near_gain, *far_grads, own_part,
        scratch=held_scratch + [pltpu.VMEM((total_rows, FEAT), F32)],
        idle=(10,), pinned=(0,), us=5.0, limit=24,
    )
    z_parts = lax.all_to_all(
        parts, "gz", split_axis=0, concat_axis=0, axis_index_groups=Z_GROUPS, tiled=True
    )
    z_parts, got_up, got_down = lax.optimization_barrier((z_parts, got_up, got_down))
    conv_part, dense_sum = call(
        sum_body, [sds((112, FEAT)), sds((PTS, FEAT))], z_parts, us=1.0, limit=8,
    )
    conv_pair, dense_two = call(
        middle_body, [sds((112, FEAT)), sds((2, PTS, FEAT))],
        conv_part, lax.ppermute(conv_part, "grp", [(i, i ^ 1) for i in range(4)]), dense_sum, flip(dense_sum, 32),
        us=0.5, limit=8,
    )
    conv_pair, dense_two, got_up, got_down = lax.optimization_barrier((conv_pair, dense_two, got_up, got_down))
    grad_features = call(
        rim_body, sds((PTS, FEAT)), own_part, got_up, got_down, halo_rows,
        us=3.0, limit=8,
    )
    conv_other = lax.ppermute(conv_pair, "grp", [(i, i ^ 2) for i in range(4)])
    dense_more = flip(dense_two, 16)
    grad_conv, gain_sum, grad_qkv, grad_proj = call(
        lambda *refs: last_body(factor, *refs),
        [sds((108, FEAT), F32), sds((1, FEAT), F32), sds((FEAT, 3 * FEAT), F32), sds((FEAT, FEAT), F32)],
        conv_pair, conv_other, dense_two, dense_more, flip(dense_two, 1), flip(dense_more, 1),
        scratch=[pltpu.VMEM((NX * NC, PTS, FEAT), F32)],
        limit=8,
    )
    return (block_out, grad_features, grad_conv, grad_qkv, grad_proj, gain_sum.reshape(FEAT))


def solution(mesh):
    return jax.shard_map(
        shards,
        mesh=mesh,
        in_specs=(
            P(("grp", "gz"), None),
            P(("grp", "gz")),
            P(("grp", "gz"), None),
            P(("grp", "gz"), None),
            P(("grp", "gz"), None),
            P(),
            P(),
            P(),
            P(),
        ),
        out_specs=(P(("grp", "gz"), None), P(("grp", "gz"), None), P("gz", None), P(), P(), P()),
        check_vma=False,
    )
```

```python
import math

import jax
import jax.numpy as jnp
from jax import lax
from jax.experimental import pallas as pl
from jax.experimental.pallas import tpu as pltpu
from jax.sharding import PartitionSpec as P

HEADS = 16
NORM_EPS = 1e-05
BF = jnp.bfloat16
F32 = jnp.float32
I32 = jnp.int32

PTS = 128
FEAT = 256
OFFS = 27
RIM = 16
EXT = PTS + 2 * RIM
SLOTS = 512
AT_EXT, AT_TAB, PAY = 128, 288, 304
MIB = 1024 * 1024

NX, NZ, NC = 4, 8, 2
Z_GROUPS = [[x * 16 + z * 2 + c for z in range(NZ)] for x in range(NX) for c in range(NC)]
X_GROUPS = [[x * 16 + z * 2 + c for x in range(NX)] for z in range(NZ) for c in range(NC)]
XZ_GROUPS = [[x * 16 + z * 2 + c for x in range(NX) for z in range(NZ)] for c in range(NC)]
SWAP = [(i, i ^ 1) for i in range(NX * NZ * NC)]
UP = [(i, i + 1) for i in range(NX * NZ * NC - 1)]
DOWN = [(i + 1, i) for i in range(NX * NZ * NC - 1)]


def flip(value, bit):
    return lax.ppermute(value, "gz", [(i, i ^ bit) for i in range(NX * NZ * NC)])


def over_groups(value):
    n = lax.axis_size("grp")
    return [value] + [lax.ppermute(value, "grp", [(i, (i + d) % n) for i in range(n)]) for d in range(1, n)]


def mm(a, b):
    return jnp.dot(a, b, preferred_element_type=F32)


def mm_t(a, b):
    return lax.dot_general(a, b, (((1,), (1,)), ((), ())), preferred_element_type=F32)


def t_mm(a, b):
    return lax.dot_general(a, b, (((0,), (0,)), ((), ())), preferred_element_type=F32)


def one_hot(cond):
    return jnp.where(cond, 1.0, 0.0).astype(BF)


def iota(shape, dim):
    return lax.broadcasted_iota(I32, shape, dim)


def call(body, out_shape, *args, scratch=(), us=1.0, fetched=(), late=(), idle=(), pinned=(), limit=16):
    fetched = tuple(fetched) + tuple(late)
    args = [pltpu.with_memory_space_constraint(a, pltpu.HBM) if i in fetched + tuple(idle) else a for i, a in enumerate(args)]
    specs = []
    for i in range(len(args)):
        space = pltpu.HBM if i in fetched + tuple(idle) else pltpu.VMEM
        specs.append(pl.BlockSpec(memory_space=space))
    single = not isinstance(out_shape, (list, tuple))
    outs = [out_shape] if single else list(out_shape)
    held = [pltpu.VMEM(args[i].shape, args[i].dtype) for i in fetched]
    held += [pltpu.VMEM(outs[i].shape, outs[i].dtype) for i in pinned]
    held += [pltpu.SemaphoreType.DMA] * (len(fetched) + len(pinned))
    shapes = [pltpu.HBM(o.shape, o.dtype) if i in pinned else o for i, o in enumerate(outs)]

    def outer(*refs):
        ins = list(refs[: len(args)])
        results = list(refs[len(args) : len(args) + len(outs)])
        first = len(args) + len(outs)
        extra = refs[first : first + len(scratch)]
        rest = refs[first + len(scratch) :]
        moved = len(fetched) + len(pinned)
        buffers, sems = rest[:moved], rest[moved:]
        copies = {}
        for n, i in enumerate(fetched):
            copies[i] = pltpu.make_async_copy(ins[i], buffers[n], sems[n])
            copies[i].start()
            ins[i] = buffers[n]
        for i in fetched:
            if i in late:
                ins[i] = (ins[i], copies[i].wait)
            else:
                copies[i].wait()
        leaving = []
        for n, i in enumerate(pinned):
            n += len(fetched)
            leaving.append(pltpu.make_async_copy(buffers[n], results[i], sems[n]))
            results[i] = buffers[n]
        body(*[v for i, v in enumerate(ins) if i not in idle], *results, *extra)
        for copy in leaving:
            copy.start()
        for copy in leaving:
            copy.wait()

    got = pl.pallas_call(
        outer,
        out_shape=shapes,
        in_specs=specs,
        out_specs=[pl.BlockSpec(memory_space=pltpu.HBM if i in pinned else pltpu.VMEM) for i in range(len(outs))],
        scratch_shapes=list(scratch) + held,
        compiler_params=pltpu.CompilerParams(vmem_limit_bytes=limit * MIB),
        cost_estimate=pl.CostEstimate(flops=int(us * 1.1e9), bytes_accessed=1 << 18, transcendentals=0),
    )(*args)
    return got[0] if single else got


def sds(shape, dtype=BF):
    return jax.ShapeDtypeStruct(shape, dtype)


def position():
    me = lax.axis_index("gz")
    return lax.shift_right_logical(me, 4), me & 1


def pick_body(pick_ref, feat_ref, down_ref, up_ref):
    rows = jnp.broadcast_to(pick_ref[...], (PTS, 2 * RIM))
    hit = one_hot(rows == iota((PTS, 2 * RIM), 0))
    got = t_mm(hit, feat_ref[...]).astype(BF)
    down_ref[...] = got[:RIM]
    up_ref[...] = got[RIM:]


def slot_hits(rank_row):
    owner = lax.shift_right_logical(rank_row, 7)
    wide = jnp.broadcast_to(owner, (PTS, PTS))
    tall = jnp.transpose(wide)
    earlier = (wide == tall) & (iota((PTS, PTS), 0) < iota((PTS, PTS), 1))
    slot = jnp.sum(jnp.where(earlier, 1, 0), axis=0, keepdims=True)
    target = owner * 8 + slot
    rows = iota((SLOTS, PTS), 0)
    return one_hot(rows == target), one_hot(rows == target + 4)


def conv_body(feat_ref, prev_ref, next_ref, nbr_ref, rank_ref, cot_ref, weight_ref, send_ref, ext, tab, wide):
    ext[:PTS] = feat_ref[...]
    ext[PTS : PTS + RIM] = prev_ref[...]
    ext[PTS + RIM : EXT] = next_ref[...]
    ext[EXT:] = jnp.zeros((FEAT - EXT, FEAT), BF)
    rows = ext[...]
    tab[:OFFS] = nbr_ref[...].astype(F32)
    tab[OFFS:] = jnp.zeros((PTS - OFFS, PTS), F32)
    table = jnp.transpose(tab[...])
    lanes = iota((PTS, FEAT), 1).astype(F32)
    for k in range(OFFS):
        hit = one_hot(table[:, k : k + 1] == lanes)
        wide[:, k * FEAT : (k + 1) * FEAT] = mm(hit, rows).astype(BF)
    mixed = (feat_ref[...].astype(F32) + mm(wide[...], weight_ref[...])).astype(BF)
    rank_row = rank_ref[...]
    first, second = slot_hits(rank_row)
    place = jnp.transpose(jnp.broadcast_to(rank_row & (PTS - 1), (PTS, PTS))).astype(F32)
    send_ref[:, :FEAT] = (mm(first, mixed) + mm(second, cot_ref[...])).astype(BF)
    marks = mm(first, (place + 1.0).astype(BF)) + mm(second, (place + (PTS + 1.0)).astype(BF))
    send_ref[:, FEAT:] = marks.astype(BF)


def patch_hits(marks):
    upper = lax.shift_right_logical(iota((SLOTS, PTS), 0), 3) & 1
    marks = marks.astype(F32) + jnp.where(upper == 1, 512.0, 0.0)
    lanes = iota((SLOTS, PTS), 1).astype(F32)
    return jnp.concatenate([one_hot(marks == lanes + (b + 1.0)) for b in (0, 512, 128, 640)], 1)


def layer_norm(hidden):
    centred = hidden - jnp.mean(hidden, -1, keepdims=True)
    inverse = lax.rsqrt(jnp.mean(centred * centred, -1, keepdims=True) + NORM_EPS)
    return centred * inverse, inverse


def patch_body(
    a_ref, b_ref, qkv_ref, proj_ref, gain_ref,
    back_ref, gg_ref,
    hits, qm, am, pr, ds, sc, gs, dense,
):
    x, core = position()
    whole = 2 * PTS
    head_dim = FEAT // HEADS
    scale = head_dim ** (-0.5)
    hits[...] = patch_hits(a_ref[:, FEAT:])
    rows = t_mm(hits[...], a_ref[:, :FEAT]) + t_mm(patch_hits(b_ref[:, FEAT:]), b_ref[:, :FEAT])
    hidden = rows[:whole]
    cot = rows[whole:].astype(BF)
    gain = gain_ref[...]
    normed, inverse = layer_norm(hidden)
    scaled = (normed * gain).astype(BF)
    projected = mm(scaled, qkv_ref[...]).astype(BF)
    query, keys, values = (projected[:, i * FEAT : (i + 1) * FEAT] for i in range(3))
    grad_att = mm_t(cot, proj_ref[...]).astype(BF)
    head_of = iota((PTS, FEAT), 1) // head_dim
    zero = jnp.zeros((PTS, FEAT), BF)
    halves = [slice(0, PTS), slice(PTS, whole)]
    spans = [[slice((s * HEADS + h) * PTS, (s * HEADS + h + 1) * PTS) for h in range(HEADS)] for s in range(2)]
    for s in range(2):
        for h in range(HEADS):
            qm[spans[s][h]] = jnp.where(head_of == h, query[halves[s]], zero)
            am[spans[s][h]] = jnp.where(head_of == h, grad_att[halves[s]], zero)
    sc[...] = mm_t(qm[...], keys)
    gs[...] = mm_t(am[...], values)
    for span in spans[0] + spans[1]:
        e = jnp.exp(sc[span] * scale)
        probs = (e * (1.0 / jnp.sum(e, -1, keepdims=True))).astype(BF)
        pr[span] = probs
        wide = probs.astype(F32)
        grad_probs = gs[span]
        delta = jnp.sum(wide * grad_probs, -1, keepdims=True)
        ds[span] = (wide * (grad_probs - delta) * scale).astype(BF)
    sc[...] = mm(pr[...], values)
    gs[...] = mm(ds[...], keys)
    att_parts, gq_parts, parts = [], [], []
    for s in range(2):
        att, gq = sc[spans[s][0]], gs[spans[s][0]]
        for h in range(1, HEADS):
            att = jnp.where(head_of == h, sc[spans[s][h]], att)
            gq = jnp.where(head_of == h, gs[spans[s][h]], gq)
        att_parts.append(att.astype(BF))
        gq_parts.append(gq.astype(BF))
        half = slice(s * HEADS * PTS, (s + 1) * HEADS * PTS)
        parts.append((t_mm(ds[half], qm[half]).astype(BF), t_mm(pr[half], am[half]).astype(BF)))
    attended = jnp.concatenate(att_parts, 0)
    gq = jnp.concatenate(gq_parts, 0)
    out = (hidden + mm(attended, proj_ref[...])).astype(BF)
    w_query, w_key, w_value = (qkv_ref[:, i * FEAT : (i + 1) * FEAT] for i in range(3))
    grad_scaled = mm_t(gq, w_query)
    for grad_key, grad_value in parts:
        grad_scaled += mm_t(grad_key, w_key) + mm_t(grad_value, w_value)

    @pl.when(core == 0)
    def _():
        dense[:FEAT] = t_mm(scaled, gq).astype(BF)
        dense[FEAT:] = (t_mm(scaled, parts[0][0]) + t_mm(scaled, parts[1][0])).astype(BF)

    @pl.when(core == 1)
    def _():
        dense[:FEAT] = (t_mm(scaled, parts[0][1]) + t_mm(scaled, parts[1][1])).astype(BF)
        dense[FEAT:] = t_mm(attended, cot).astype(BF)

    back_ref[:, 16:] = dense[...].reshape(32, 16, FEAT)
    gain_terms = grad_scaled * normed
    gg_ref[...] = jnp.sum(jnp.where(core == 0, gain_terms[:PTS], gain_terms[PTS:]), 0, keepdims=True)
    grad_normed = grad_scaled * gain
    grad_hidden = (
        grad_normed
        - jnp.mean(grad_normed, -1, keepdims=True)
        - normed * jnp.mean(grad_normed * normed, -1, keepdims=True)
    ) * inverse
    grad_local = (cot.astype(F32) + grad_hidden).astype(BF)
    back = mm(hits[...], jnp.concatenate([out, grad_local], 0)).astype(BF)
    back_ref[:, :16] = back.reshape(32, 16, FEAT)


def unpack_body(
    back_ref, rank_ref, gg_ref, feat_ref, prev_ref, next_ref, nbr_ref,
    block_ref, grad_ref, copies_ref, dense_ref,
):
    first, second = slot_hits(rank_ref[...])
    rows = back_ref[:, :16].reshape(SLOTS, FEAT)
    grad = t_mm(second, rows).astype(BF)
    table = nbr_ref[...].astype(F32)
    low = jnp.concatenate([table[16:], jnp.zeros((32 - OFFS, PTS), F32)], 0)
    at = iota((16, PTS), 0)
    gain = gg_ref[...]
    low = jnp.where(at == 12, gain[:, :PTS], jnp.where(at == 14, gain[:, PTS:], low))
    grad_ref[...] = grad
    copies_ref[:PTS] = grad
    copies_ref[AT_EXT : AT_EXT + PTS] = feat_ref[...]
    copies_ref[AT_EXT + PTS : AT_EXT + PTS + RIM] = prev_ref[...]
    copies_ref[AT_EXT + PTS + RIM : AT_TAB] = next_ref[...]
    copies_ref[AT_TAB:, :PTS] = table[:16].astype(BF)
    copies_ref[AT_TAB:, PTS:] = low.astype(BF)
    dense_ref[...] = jnp.sum(back_ref[:, 16:].astype(F32), 0).astype(BF)
    block_ref[...] = t_mm(first, rows).astype(BF)


def spread_body(grad_ref, nbr_ref, weight_ref, own_ref, down_ref, up_ref, terms, acc):
    grad = grad_ref[...]
    table = nbr_ref[...].astype(F32)
    points = iota((EXT, PTS), 0).astype(F32)
    for k in range(OFFS):
        hit = one_hot(points == table[k : k + 1])
        terms[k * EXT : (k + 1) * EXT] = mm(hit, grad).astype(BF)
    acc[...] = jnp.zeros((EXT, FEAT), F32)
    for k in range(OFFS):
        acc[...] += mm_t(terms[k * EXT : (k + 1) * EXT], weight_ref[k * FEAT : (k + 1) * FEAT])
    own_ref[...] = acc[:PTS] + grad.astype(F32)
    down_ref[...] = acc[PTS : PTS + RIM].astype(BF)
    up_ref[...] = acc[PTS + RIM :].astype(BF)


def rim_body(own_ref, down_ref, up_ref, pick_ref, out_ref):
    rows = jnp.broadcast_to(pick_ref[...], (PTS, 2 * RIM))
    hit = one_hot(rows == iota((PTS, 2 * RIM), 0))
    rims = jnp.concatenate([down_ref[...], up_ref[...]], 0)
    out_ref[...] = (own_ref[...] + mm(hit, rims)).astype(BF)


def corner():
    x, core = position()
    base = x * 1728 + core * 108
    first_offset = jnp.minimum(lax.shift_right_logical(base, 8), OFFS - 8)
    return first_offset, base - first_offset * FEAT - core * 4, core


def chip_terms(held, first_offset, tab, exts, terms):
    gain = jnp.zeros((1, FEAT), F32)
    points = iota((EXT, PTS), 0).astype(F32)
    for s in range(NX):
        rows = held[s][AT_TAB:].astype(F32)
        tab[s * 32 : s * 32 + 16] = rows[:, :PTS]
        tab[s * 32 + 16 : s * 32 + 32] = rows[:, PTS:]
        exts[s * EXT : (s + 1) * EXT] = held[s][AT_EXT:AT_TAB]
        gain += jnp.concatenate([rows[12:13, PTS:], rows[14:15, PTS:]], 1)
        hits = [one_hot(points == tab[pl.ds(first_offset + (s * 32 + k), 1), :]) for k in range(8)]
        found = mm(jnp.concatenate(hits, 0), held[s][:PTS]).astype(BF)
        for k in range(8):
            terms[k, s * EXT : (s + 1) * EXT] = found[k * EXT : (k + 1) * EXT]
    return gain, jnp.transpose(exts[...])


def near_grad_body(h0, h1, h2, h3, total_ref, gain_ref, tab, exts, terms):
    held = (h0, h1, h2, h3)
    first_offset, _, _ = corner()
    gain, ext_t = chip_terms(held, first_offset, tab, exts, terms)
    gain_ref[...] = gain
    for k in range(8):
        total_ref[k * FEAT : (k + 1) * FEAT] = mm(ext_t, terms[k])
    total_ref[8 * FEAT :] = jnp.zeros((16, FEAT), F32)


def kernel_grad_body(p0_ref, p1_ref, p2_ref, p3_ref, near_ref, gain_ref, h0, h1, h2, h3, out_ref, tab, exts, terms, total):
    held = (h0, h1, h2, h3)
    first_offset, first_row, core = corner()
    gain, ext_t = chip_terms(held, first_offset, tab, exts, terms)
    gain = gain + gain_ref[...]
    for k in range(8):
        span = slice(k * FEAT, (k + 1) * FEAT)
        total[span] = near_ref[span] + mm(ext_t, terms[k])
    total[8 * FEAT :] = jnp.zeros((16, FEAT), F32)
    dense = p0_ref[...].astype(F32) + p1_ref[...].astype(F32) + p2_ref[...].astype(F32) + p3_ref[...].astype(F32)
    dense = dense.astype(BF)
    at = iota((112, FEAT), 0)
    for z in range(NZ):
        wide = total[pl.ds(pl.multiple_of(first_row + z * 216, 8), 120), :]
        rows = jnp.where(core == 1, wide[4:116], wide[:112])
        rows = jnp.where(at < 108, rows, jnp.where(at == 108, gain, 0.0))
        out_ref[z, :112] = rows.astype(BF)
        out_ref[z, 112:] = dense


def sum_body(got_ref, conv_ref, dense_ref):
    total = got_ref[0].astype(F32)
    for i in range(1, NZ):
        total += got_ref[i].astype(F32)
    conv_ref[...] = total[:112].astype(BF)
    for i in range(NZ):
        dense_ref[i * 16 : (i + 1) * 16] = got_ref[i, 112:]


def middle_body(conv_ref, other_ref, dense_ref, across_ref, pair_ref, two_ref):
    pair_ref[...] = (conv_ref[...].astype(F32) + other_ref[...].astype(F32)).astype(BF)
    two_ref[0] = dense_ref[...]
    two_ref[1] = across_ref[...]


def last_body(factor, pair_ref, other_ref, *refs):
    parts, (conv_ref, gain_ref, qkv_ref, proj_ref) = refs[:4], refs[4:]
    total = pair_ref[...].astype(F32) + other_ref[...].astype(F32)
    conv_ref[...] = total[:108] * factor
    gain_ref[...] = total[108:109] * factor
    x, core = position()

    def fill(low_parts, high_parts):
        for s in range(NX):
            source = x ^ (s % 2 * 2) ^ (s // 2)
            row = pl.ds(pl.multiple_of((source & 1) * PTS, PTS), PTS)
            column = pl.multiple_of(lax.shift_right_logical(source, 1) * FEAT, FEAT)
            qkv_ref[row, pl.ds(column, FEAT)] = low_parts[s // 2][s % 2].astype(F32) * factor
            block = high_parts[s // 2][s % 2].astype(F32) * factor

            @pl.when(source < 2)
            def _():
                qkv_ref[row, 2 * FEAT :] = block

            @pl.when(source >= 2)
            def _():
                proj_ref[row, :] = block

    @pl.when(core == 0)
    def _():
        fill(parts[:2], parts[2:])

    @pl.when(core == 1)
    def _():
        fill(parts[2:], parts[:2])


def shards(
    features,
    hilbert_rank,
    neighbours,
    halo_rows,
    cotangent,
    conv_weight,
    qkv_weight,
    proj_weight,
    norm_gain,
):
    factor = 1.0 / math.sqrt(PTS * NX * NZ * NC * lax.axis_size("grp"))
    rank_row = hilbert_rank.reshape(1, PTS)
    gain_row = norm_gain.reshape(1, FEAT)
    table = neighbours.T
    to_prev, to_next = call(
        pick_body, [sds((RIM, FEAT))] * 2, halo_rows, features, fetched=(0, 1), us=10.0, limit=8
    )
    from_prev = lax.ppermute(to_next, "gz", UP)
    from_next = lax.ppermute(to_prev, "gz", DOWN)
    send = call(
        conv_body,
        sds((SLOTS, FEAT + PTS)),
        features, from_prev, from_next, table, rank_row, cotangent, conv_weight,
        scratch=[pltpu.VMEM((FEAT, FEAT), BF), pltpu.VMEM((PTS, PTS), F32), pltpu.VMEM((PTS, OFFS * FEAT), BF)],
        us=3.0,
    )
    got = lax.all_to_all(
        send.reshape(32, 16, FEAT + PTS), "gz", split_axis=0, concat_axis=0,
        axis_index_groups=XZ_GROUPS, tiled=True,
    ).reshape(SLOTS, FEAT + PTS)
    other = lax.ppermute(got, "gz", SWAP)
    rows = 2 * HEADS * PTS
    back, grad_gain = call(
        patch_body,
        [sds((32, 32, FEAT)), sds((1, FEAT), F32)],
        got, other, qkv_weight, proj_weight, gain_row,
        scratch=[pltpu.VMEM((SLOTS, SLOTS), BF)]
        + [pltpu.VMEM((rows, FEAT), BF)] * 4
        + [pltpu.VMEM((rows, FEAT), F32)] * 2
        + [pltpu.VMEM((2 * FEAT, FEAT), BF)],
        us=6.0, limit=32,
    )
    returned = lax.all_to_all(
        back, "gz", split_axis=0, concat_axis=0, axis_index_groups=XZ_GROUPS, tiled=True
    )
    block_out, grad, grad_copies, dense = call(
        unpack_body,
        [sds((PTS, FEAT)), sds((PTS, FEAT)), sds((PAY, FEAT)), sds((16, FEAT))],
        returned, rank_row, grad_gain, features, from_prev, from_next, table,
        us=1.5, limit=8,
    )
    near_grads = [grad_copies] + [flip(grad_copies, 16 * d) for d in (1, 3, 2)]
    dense_groups = over_groups(dense)
    own_part, rim_down, rim_up = call(
        spread_body,
        [sds((PTS, FEAT), F32), sds((RIM, FEAT)), sds((RIM, FEAT))],
        grad, table, conv_weight,
        scratch=[pltpu.VMEM((OFFS * EXT, FEAT), BF), pltpu.VMEM((EXT, FEAT), F32)],
        pinned=(0, 1, 2), us=3.0,
    )
    near_grads, own_part, dense_groups = lax.optimization_barrier((near_grads, own_part, dense_groups))
    far_grads = [flip(v, 1) for v in near_grads]
    got_down = lax.ppermute(rim_down, "gz", DOWN)
    got_up = lax.ppermute(rim_up, "gz", UP)
    held_scratch = [
        pltpu.VMEM((NX * 32, PTS), F32),
        pltpu.VMEM((NX * EXT, FEAT), BF),
        pltpu.VMEM((8, NX * EXT, FEAT), BF),
    ]
    total_rows = 8 * FEAT + 16
    near_total, near_gain = call(
        near_grad_body, [sds((total_rows, FEAT), F32), sds((1, FEAT), F32)], *near_grads,
        scratch=held_scratch, us=3.0, limit=16,
    )
    parts = call(
        kernel_grad_body,
        sds((NZ, 128, FEAT)),
        *dense_groups, near_total, near_gain, *far_grads, own_part,
        scratch=held_scratch + [pltpu.VMEM((total_rows, FEAT), F32)],
        idle=(10,), pinned=(0,), us=5.0, limit=24,
    )
    z_parts = lax.all_to_all(
        parts, "gz", split_axis=0, concat_axis=0, axis_index_groups=Z_GROUPS, tiled=True
    )
    z_parts, got_up, got_down = lax.optimization_barrier((z_parts, got_up, got_down))
    conv_part, dense_sum = call(
        sum_body, [sds((112, FEAT)), sds((PTS, FEAT))], z_parts, us=1.0, limit=8,
    )
    conv_pair, dense_two = call(
        middle_body, [sds((112, FEAT)), sds((2, PTS, FEAT))],
        conv_part, lax.ppermute(conv_part, "grp", [(i, i ^ 1) for i in range(4)]), dense_sum, flip(dense_sum, 32),
        us=0.5, limit=8,
    )
    conv_pair, dense_two, got_up, got_down = lax.optimization_barrier((conv_pair, dense_two, got_up, got_down))
    grad_features = call(
        rim_body, sds((PTS, FEAT)), own_part, got_up, got_down, halo_rows,
        us=3.0, limit=8,
    )
    conv_other = lax.ppermute(conv_pair, "grp", [(i, i ^ 2) for i in range(4)])
    dense_more = flip(dense_two, 16)
    grad_conv, gain_sum, grad_qkv, grad_proj = call(
        lambda *refs: last_body(factor, *refs),
        [sds((108, FEAT), F32), sds((1, FEAT), F32), sds((FEAT, 3 * FEAT), F32), sds((FEAT, FEAT), F32)],
        conv_pair, conv_other, dense_two, dense_more, flip(dense_two, 1), flip(dense_more, 1),
        limit=8,
    )
    return (block_out, grad_features, grad_conv, grad_qkv, grad_proj, gain_sum.reshape(FEAT))


def solution(mesh):
    return jax.shard_map(
        shards,
        mesh=mesh,
        in_specs=(
            P(("grp", "gz"), None),
            P(("grp", "gz")),
            P(("grp", "gz"), None),
            P(("grp", "gz"), None),
            P(("grp", "gz"), None),
            P(),
            P(),
            P(),
            P(),
        ),
        out_specs=(P(("grp", "gz"), None), P(("grp", "gz"), None), P("gz", None), P(), P(), P()),
        check_vma=False,
    )
```

```python
import math

import jax
import jax.numpy as jnp
from jax import lax
from jax.experimental import pallas as pl
from jax.experimental.pallas import tpu as pltpu
from jax.sharding import PartitionSpec as P

HEADS = 16
NORM_EPS = 1e-05
BF = jnp.bfloat16
F32 = jnp.float32
I32 = jnp.int32

PTS = 128
FEAT = 256
OFFS = 27
RIM = 16
EXT = PTS + 2 * RIM
SLOTS = 512
AT_EXT, AT_TAB, PAY = 128, 288, 304
MIB = 1024 * 1024

NX, NZ, NC = 4, 8, 2
Z_GROUPS = [[x * 16 + z * 2 + c for z in range(NZ)] for x in range(NX) for c in range(NC)]
X_GROUPS = [[x * 16 + z * 2 + c for x in range(NX)] for z in range(NZ) for c in range(NC)]
XZ_GROUPS = [[x * 16 + z * 2 + c for x in range(NX) for z in range(NZ)] for c in range(NC)]
SWAP = [(i, i ^ 1) for i in range(NX * NZ * NC)]
UP = [(i, i + 1) for i in range(NX * NZ * NC - 1)]
DOWN = [(i + 1, i) for i in range(NX * NZ * NC - 1)]


def flip(value, bit):
    return lax.ppermute(value, "gz", [(i, i ^ bit) for i in range(NX * NZ * NC)])


def over_groups(value):
    n = lax.axis_size("grp")
    return [value] + [lax.ppermute(value, "grp", [(i, (i + d) % n) for i in range(n)]) for d in range(1, n)]


def mm(a, b):
    return jnp.dot(a, b, preferred_element_type=F32)


def mm_t(a, b):
    return lax.dot_general(a, b, (((1,), (1,)), ((), ())), preferred_element_type=F32)


def t_mm(a, b):
    return lax.dot_general(a, b, (((0,), (0,)), ((), ())), preferred_element_type=F32)


def one_hot(cond):
    return jnp.where(cond, 1.0, 0.0).astype(BF)


def iota(shape, dim):
    return lax.broadcasted_iota(I32, shape, dim)


def call(body, out_shape, *args, scratch=(), us=1.0, fetched=(), late=(), idle=(), pinned=(), limit=16):
    fetched = tuple(fetched) + tuple(late)
    args = [pltpu.with_memory_space_constraint(a, pltpu.HBM) if i in fetched + tuple(idle) else a for i, a in enumerate(args)]
    specs = []
    for i in range(len(args)):
        space = pltpu.HBM if i in fetched + tuple(idle) else pltpu.VMEM
        specs.append(pl.BlockSpec(memory_space=space))
    single = not isinstance(out_shape, (list, tuple))
    outs = [out_shape] if single else list(out_shape)
    held = [pltpu.VMEM(args[i].shape, args[i].dtype) for i in fetched]
    held += [pltpu.VMEM(outs[i].shape, outs[i].dtype) for i in pinned]
    held += [pltpu.SemaphoreType.DMA] * (len(fetched) + len(pinned))
    shapes = [pltpu.HBM(o.shape, o.dtype) if i in pinned else o for i, o in enumerate(outs)]

    def outer(*refs):
        ins = list(refs[: len(args)])
        results = list(refs[len(args) : len(args) + len(outs)])
        first = len(args) + len(outs)
        extra = refs[first : first + len(scratch)]
        rest = refs[first + len(scratch) :]
        moved = len(fetched) + len(pinned)
        buffers, sems = rest[:moved], rest[moved:]
        copies = {}
        for n, i in enumerate(fetched):
            copies[i] = pltpu.make_async_copy(ins[i], buffers[n], sems[n])
            copies[i].start()
            ins[i] = buffers[n]
        for i in fetched:
            if i in late:
                ins[i] = (ins[i], copies[i].wait)
            else:
                copies[i].wait()
        leaving = []
        for n, i in enumerate(pinned):
            n += len(fetched)
            leaving.append(pltpu.make_async_copy(buffers[n], results[i], sems[n]))
            results[i] = buffers[n]
        body(*[v for i, v in enumerate(ins) if i not in idle], *results, *extra)
        for copy in leaving:
            copy.start()
        for copy in leaving:
            copy.wait()

    got = pl.pallas_call(
        outer,
        out_shape=shapes,
        in_specs=specs,
        out_specs=[pl.BlockSpec(memory_space=pltpu.HBM if i in pinned else pltpu.VMEM) for i in range(len(outs))],
        scratch_shapes=list(scratch) + held,
        compiler_params=pltpu.CompilerParams(vmem_limit_bytes=limit * MIB),
        cost_estimate=pl.CostEstimate(flops=int(us * 1.1e9), bytes_accessed=1 << 18, transcendentals=0),
    )(*args)
    return got[0] if single else got


def sds(shape, dtype=BF):
    return jax.ShapeDtypeStruct(shape, dtype)


def position():
    me = lax.axis_index("gz")
    return lax.shift_right_logical(me, 4), me & 1


def pick_body(pick_ref, feat_ref, down_ref, up_ref):
    rows = jnp.broadcast_to(pick_ref[...], (PTS, 2 * RIM))
    hit = one_hot(rows == iota((PTS, 2 * RIM), 0))
    got = t_mm(hit, feat_ref[...]).astype(BF)
    down_ref[...] = got[:RIM]
    up_ref[...] = got[RIM:]


def slot_hits(rank_row):
    owner = lax.shift_right_logical(rank_row, 7)
    wide = jnp.broadcast_to(owner, (PTS, PTS))
    tall = jnp.transpose(wide)
    earlier = (wide == tall) & (iota((PTS, PTS), 0) < iota((PTS, PTS), 1))
    slot = jnp.sum(jnp.where(earlier, 1, 0), axis=0, keepdims=True)
    target = owner * 8 + slot
    rows = iota((SLOTS, PTS), 0)
    return one_hot(rows == target), one_hot(rows == target + 4)


def conv_body(feat_ref, prev_ref, next_ref, nbr_ref, rank_ref, cot_ref, weight_ref, send_ref, ext, tab, wide):
    ext[:PTS] = feat_ref[...]
    ext[PTS : PTS + RIM] = prev_ref[...]
    ext[PTS + RIM : EXT] = next_ref[...]
    ext[EXT:] = jnp.zeros((FEAT - EXT, FEAT), BF)
    rows = ext[...]
    tab[:OFFS] = nbr_ref[...].astype(F32)
    tab[OFFS:] = jnp.zeros((PTS - OFFS, PTS), F32)
    table = jnp.transpose(tab[...])
    lanes = iota((PTS, FEAT), 1).astype(F32)
    for k in range(OFFS):
        hit = one_hot(table[:, k : k + 1] == lanes)
        wide[:, k * FEAT : (k + 1) * FEAT] = mm(hit, rows).astype(BF)
    mixed = (feat_ref[...].astype(F32) + mm(wide[...], weight_ref[...])).astype(BF)
    rank_row = rank_ref[...]
    first, second = slot_hits(rank_row)
    place = jnp.transpose(jnp.broadcast_to(rank_row & (PTS - 1), (PTS, PTS))).astype(F32)
    send_ref[:, :FEAT] = (mm(first, mixed) + mm(second, cot_ref[...])).astype(BF)
    marks = mm(first, (place + 1.0).astype(BF)) + mm(second, (place + (PTS + 1.0)).astype(BF))
    send_ref[:, FEAT:] = marks.astype(BF)


def patch_hits(marks):
    upper = lax.shift_right_logical(iota((SLOTS, PTS), 0), 3) & 1
    marks = marks.astype(F32) + jnp.where(upper == 1, 512.0, 0.0)
    lanes = iota((SLOTS, PTS), 1).astype(F32)
    return jnp.concatenate([one_hot(marks == lanes + (b + 1.0)) for b in (0, 512, 128, 640)], 1)


def layer_norm(hidden):
    centred = hidden - jnp.mean(hidden, -1, keepdims=True)
    inverse = lax.rsqrt(jnp.mean(centred * centred, -1, keepdims=True) + NORM_EPS)
    return centred * inverse, inverse


def patch_body(
    a_ref, b_ref, qkv_ref, proj_ref, gain_ref,
    back_ref, gg_ref,
    hits, qm, am, pr, ds, sc, gs, dense,
):
    x, core = position()
    whole = 2 * PTS
    head_dim = FEAT // HEADS
    scale = head_dim ** (-0.5)
    hits[...] = patch_hits(a_ref[:, FEAT:])
    rows = t_mm(hits[...], a_ref[:, :FEAT]) + t_mm(patch_hits(b_ref[:, FEAT:]), b_ref[:, :FEAT])
    hidden = rows[:whole]
    cot = rows[whole:].astype(BF)
    gain = gain_ref[...]
    normed, inverse = layer_norm(hidden)
    scaled = (normed * gain).astype(BF)
    projected = mm(scaled, qkv_ref[...]).astype(BF)
    query, keys, values = (projected[:, i * FEAT : (i + 1) * FEAT] for i in range(3))
    grad_att = mm_t(cot, proj_ref[...]).astype(BF)
    head_of = iota((PTS, FEAT), 1) // head_dim
    zero = jnp.zeros((PTS, FEAT), BF)
    halves = [slice(0, PTS), slice(PTS, whole)]
    spans = [[slice((s * HEADS + h) * PTS, (s * HEADS + h + 1) * PTS) for h in range(HEADS)] for s in range(2)]
    for s in range(2):
        for h in range(HEADS):
            qm[spans[s][h]] = jnp.where(head_of == h, query[halves[s]], zero)
            am[spans[s][h]] = jnp.where(head_of == h, grad_att[halves[s]], zero)
    sc[...] = mm_t(qm[...], keys)
    gs[...] = mm_t(am[...], values)
    for span in spans[0] + spans[1]:
        e = jnp.exp(sc[span] * scale)
        probs = (e * (1.0 / jnp.sum(e, -1, keepdims=True))).astype(BF)
        pr[span] = probs
        wide = probs.astype(F32)
        grad_probs = gs[span]
        delta = jnp.sum(wide * grad_probs, -1, keepdims=True)
        ds[span] = (wide * (grad_probs - delta) * scale).astype(BF)
    sc[...] = mm(pr[...], values)
    gs[...] = mm(ds[...], keys)
    att_parts, gq_parts, parts = [], [], []
    for s in range(2):
        att, gq = sc[spans[s][0]], gs[spans[s][0]]
        for h in range(1, HEADS):
            att = jnp.where(head_of == h, sc[spans[s][h]], att)
            gq = jnp.where(head_of == h, gs[spans[s][h]], gq)
        att_parts.append(att.astype(BF))
        gq_parts.append(gq.astype(BF))
        half = slice(s * HEADS * PTS, (s + 1) * HEADS * PTS)
        parts.append((t_mm(ds[half], qm[half]).astype(BF), t_mm(pr[half], am[half]).astype(BF)))
    attended = jnp.concatenate(att_parts, 0)
    gq = jnp.concatenate(gq_parts, 0)
    out = (hidden + mm(attended, proj_ref[...])).astype(BF)
    w_query, w_key, w_value = (qkv_ref[:, i * FEAT : (i + 1) * FEAT] for i in range(3))
    grad_scaled = mm_t(gq, w_query)
    for grad_key, grad_value in parts:
        grad_scaled += mm_t(grad_key, w_key) + mm_t(grad_value, w_value)

    @pl.when(core == 0)
    def _():
        dense[:FEAT] = t_mm(scaled, gq).astype(BF)
        dense[FEAT:] = (t_mm(scaled, parts[0][0]) + t_mm(scaled, parts[1][0])).astype(BF)

    @pl.when(core == 1)
    def _():
        dense[:FEAT] = (t_mm(scaled, parts[0][1]) + t_mm(scaled, parts[1][1])).astype(BF)
        dense[FEAT:] = t_mm(attended, cot).astype(BF)

    back_ref[:, 16:] = dense[...].reshape(32, 16, FEAT)
    gain_terms = grad_scaled * normed
    gg_ref[...] = jnp.sum(jnp.where(core == 0, gain_terms[:PTS], gain_terms[PTS:]), 0, keepdims=True)
    grad_normed = grad_scaled * gain
    grad_hidden = (
        grad_normed
        - jnp.mean(grad_normed, -1, keepdims=True)
        - normed * jnp.mean(grad_normed * normed, -1, keepdims=True)
    ) * inverse
    grad_local = (cot.astype(F32) + grad_hidden).astype(BF)
    back = mm(hits[...], jnp.concatenate([out, grad_local], 0)).astype(BF)
    back_ref[:, :16] = back.reshape(32, 16, FEAT)


def unpack_body(
    back_ref, rank_ref, gg_ref, feat_ref, prev_ref, next_ref, nbr_ref,
    block_ref, grad_ref, copies_ref, dense_ref,
):
    first, second = slot_hits(rank_ref[...])
    rows = back_ref[:, :16].reshape(SLOTS, FEAT)
    grad = t_mm(second, rows).astype(BF)
    table = nbr_ref[...].astype(F32)
    low = jnp.concatenate([table[16:], jnp.zeros((32 - OFFS, PTS), F32)], 0)
    at = iota((16, PTS), 0)
    gain = gg_ref[...]
    low = jnp.where(at == 12, gain[:, :PTS], jnp.where(at == 14, gain[:, PTS:], low))
    grad_ref[...] = grad
    copies_ref[:PTS] = grad
    copies_ref[AT_EXT : AT_EXT + PTS] = feat_ref[...]
    copies_ref[AT_EXT + PTS : AT_EXT + PTS + RIM] = prev_ref[...]
    copies_ref[AT_EXT + PTS + RIM : AT_TAB] = next_ref[...]
    copies_ref[AT_TAB:, :PTS] = table[:16].astype(BF)
    copies_ref[AT_TAB:, PTS:] = low.astype(BF)
    dense_ref[...] = jnp.sum(back_ref[:, 16:].astype(F32), 0).astype(BF)
    block_ref[...] = t_mm(first, rows).astype(BF)


def spread_body(grad_ref, nbr_ref, weight_ref, own_ref, down_ref, up_ref, terms, acc):
    grad = grad_ref[...]
    table = nbr_ref[...].astype(F32)
    points = iota((EXT, PTS), 0).astype(F32)
    for k in range(OFFS):
        hit = one_hot(points == table[k : k + 1])
        terms[k * EXT : (k + 1) * EXT] = mm(hit, grad).astype(BF)
    acc[...] = jnp.zeros((EXT, FEAT), F32)
    for k in range(OFFS):
        acc[...] += mm_t(terms[k * EXT : (k + 1) * EXT], weight_ref[k * FEAT : (k + 1) * FEAT])
    own_ref[...] = acc[:PTS] + grad.astype(F32)
    down_ref[...] = acc[PTS : PTS + RIM].astype(BF)
    up_ref[...] = acc[PTS + RIM :].astype(BF)


def rim_body(own_ref, down_ref, up_ref, pick_ref, out_ref):
    rows = jnp.broadcast_to(pick_ref[...], (PTS, 2 * RIM))
    hit = one_hot(rows == iota((PTS, 2 * RIM), 0))
    rims = jnp.concatenate([down_ref[...], up_ref[...]], 0)
    out_ref[...] = (own_ref[...] + mm(hit, rims)).astype(BF)


def corner():
    x, core = position()
    base = x * 1728 + core * 108
    first_offset = jnp.minimum(lax.shift_right_logical(base, 8), OFFS - 8)
    return first_offset, base - first_offset * FEAT - core * 4, core


def chip_terms(held, first_offset, tab, exts, terms):
    gain = jnp.zeros((1, FEAT), F32)
    points = iota((EXT, PTS), 0).astype(F32)
    for s in range(NX):
        rows = held[s][AT_TAB:].astype(F32)
        tab[s * 32 : s * 32 + 16] = rows[:, :PTS]
        tab[s * 32 + 16 : s * 32 + 32] = rows[:, PTS:]
        exts[s * EXT : (s + 1) * EXT] = held[s][AT_EXT:AT_TAB]
        gain += jnp.concatenate([rows[12:13, PTS:], rows[14:15, PTS:]], 1)
        hits = [one_hot(points == tab[pl.ds(first_offset + (s * 32 + k), 1), :]) for k in range(8)]
        found = mm(jnp.concatenate(hits, 0), held[s][:PTS]).astype(BF)
        for k in range(8):
            terms[k, s * EXT : (s + 1) * EXT] = found[k * EXT : (k + 1) * EXT]
    return gain, jnp.transpose(exts[...])


def near_grad_body(h0, h1, h2, h3, total_ref, gain_ref, tab, exts, terms):
    held = (h0, h1, h2, h3)
    first_offset, _, _ = corner()
    gain, ext_t = chip_terms(held, first_offset, tab, exts, terms)
    gain_ref[...] = gain
    for k in range(8):
        total_ref[k * FEAT : (k + 1) * FEAT] = mm(ext_t, terms[k])
    total_ref[8 * FEAT :] = jnp.zeros((16, FEAT), F32)


def kernel_grad_body(p0_ref, p1_ref, p2_ref, p3_ref, near_ref, gain_ref, h0, h1, h2, h3, out_ref, tab, exts, terms, total):
    held = (h0, h1, h2, h3)
    first_offset, first_row, core = corner()
    gain, ext_t = chip_terms(held, first_offset, tab, exts, terms)
    gain = gain + gain_ref[...]
    for k in range(8):
        span = slice(k * FEAT, (k + 1) * FEAT)
        total[span] = near_ref[span] + mm(ext_t, terms[k])
    total[8 * FEAT :] = jnp.zeros((16, FEAT), F32)
    dense = p0_ref[...].astype(F32) + p1_ref[...].astype(F32) + p2_ref[...].astype(F32) + p3_ref[...].astype(F32)
    dense = dense.astype(BF)
    at = iota((112, FEAT), 0)
    for z in range(NZ):
        wide = total[pl.ds(pl.multiple_of(first_row + z * 216, 8), 120), :]
        rows = jnp.where(core == 1, wide[4:116], wide[:112])
        rows = jnp.where(at < 108, rows, jnp.where(at == 108, gain, 0.0))
        out_ref[z, :112] = rows.astype(BF)
        out_ref[z, 112:] = dense


def sum_body(got_ref, conv_ref, dense_ref):
    total = got_ref[0].astype(F32)
    for i in range(1, NZ):
        total += got_ref[i].astype(F32)
    conv_ref[...] = total[:112].astype(BF)
    for i in range(NZ):
        dense_ref[i * 16 : (i + 1) * 16] = got_ref[i, 112:]


def middle_body(conv_ref, other_ref, dense_ref, across_ref, pair_ref, two_ref):
    pair_ref[...] = (conv_ref[...].astype(F32) + other_ref[...].astype(F32)).astype(BF)
    two_ref[0] = dense_ref[...]
    two_ref[1] = across_ref[...]


def last_body(factor, pair_ref, other_ref, *refs):
    parts, (conv_ref, gain_ref, qkv_ref, proj_ref) = refs[:4], refs[4:]
    total = pair_ref[...].astype(F32) + other_ref[...].astype(F32)
    conv_ref[...] = total[:108] * factor
    gain_ref[...] = total[108:109] * factor
    x, core = position()

    def fill(low_parts, high_parts):
        for s in range(NX):
            source = x ^ (s % 2 * 2) ^ (s // 2)
            row = pl.ds(pl.multiple_of((source & 1) * PTS, PTS), PTS)
            column = pl.multiple_of(lax.shift_right_logical(source, 1) * FEAT, FEAT)
            qkv_ref[row, pl.ds(column, FEAT)] = low_parts[s // 2][s % 2].astype(F32) * factor
            block = high_parts[s // 2][s % 2].astype(F32) * factor

            @pl.when(source < 2)
            def _():
                qkv_ref[row, 2 * FEAT :] = block

            @pl.when(source >= 2)
            def _():
                proj_ref[row, :] = block

    @pl.when(core == 0)
    def _():
        fill(parts[:2], parts[2:])

    @pl.when(core == 1)
    def _():
        fill(parts[2:], parts[:2])


def shards(
    features,
    hilbert_rank,
    neighbours,
    halo_rows,
    cotangent,
    conv_weight,
    qkv_weight,
    proj_weight,
    norm_gain,
):
    factor = 1.0 / math.sqrt(PTS * NX * NZ * NC * lax.axis_size("grp"))
    rank_row = hilbert_rank.reshape(1, PTS)
    gain_row = norm_gain.reshape(1, FEAT)
    table = neighbours.T
    to_prev, to_next = call(
        pick_body, [sds((RIM, FEAT))] * 2, halo_rows, features, fetched=(0, 1), us=10.0, limit=8
    )
    from_prev = lax.ppermute(to_next, "gz", UP)
    from_next = lax.ppermute(to_prev, "gz", DOWN)
    send = call(
        conv_body,
        sds((SLOTS, FEAT + PTS)),
        features, from_prev, from_next, table, rank_row, cotangent, conv_weight,
        scratch=[pltpu.VMEM((FEAT, FEAT), BF), pltpu.VMEM((PTS, PTS), F32), pltpu.VMEM((PTS, OFFS * FEAT), BF)],
        us=3.0,
    )
    got = lax.all_to_all(
        send.reshape(32, 16, FEAT + PTS), "gz", split_axis=0, concat_axis=0,
        axis_index_groups=XZ_GROUPS, tiled=True,
    ).reshape(SLOTS, FEAT + PTS)
    other = lax.ppermute(got, "gz", SWAP)
    rows = 2 * HEADS * PTS
    back, grad_gain = call(
        patch_body,
        [sds((32, 32, FEAT)), sds((1, FEAT), F32)],
        got, other, qkv_weight, proj_weight, gain_row,
        scratch=[pltpu.VMEM((SLOTS, SLOTS), BF)]
        + [pltpu.VMEM((rows, FEAT), BF)] * 4
        + [pltpu.VMEM((rows, FEAT), F32)] * 2
        + [pltpu.VMEM((2 * FEAT, FEAT), BF)],
        us=6.0, limit=32,
    )
    returned = lax.all_to_all(
        back, "gz", split_axis=0, concat_axis=0, axis_index_groups=XZ_GROUPS, tiled=True
    )
    block_out, grad, grad_copies, dense = call(
        unpack_body,
        [sds((PTS, FEAT)), sds((PTS, FEAT)), sds((PAY, FEAT)), sds((16, FEAT))],
        returned, rank_row, grad_gain, features, from_prev, from_next, table,
        us=1.5, limit=8,
    )
    near_grads = [grad_copies] + [flip(grad_copies, 16 * d) for d in (1, 3, 2)]
    own_part, rim_down, rim_up = call(
        spread_body,
        [sds((PTS, FEAT), F32), sds((RIM, FEAT)), sds((RIM, FEAT))],
        grad, table, conv_weight,
        scratch=[pltpu.VMEM((OFFS * EXT, FEAT), BF), pltpu.VMEM((EXT, FEAT), F32)],
        pinned=(0, 1, 2), us=3.0,
    )
    dense, own_part = lax.optimization_barrier((dense, own_part))
    dense_groups = over_groups(dense)
    near_grads, own_part = lax.optimization_barrier((near_grads, own_part))
    far_grads = [flip(v, 1) for v in near_grads]
    got_down = lax.ppermute(rim_down, "gz", DOWN)
    got_up = lax.ppermute(rim_up, "gz", UP)
    held_scratch = [
        pltpu.VMEM((NX * 32, PTS), F32),
        pltpu.VMEM((NX * EXT, FEAT), BF),
        pltpu.VMEM((8, NX * EXT, FEAT), BF),
    ]
    total_rows = 8 * FEAT + 16
    near_total, near_gain = call(
        near_grad_body, [sds((total_rows, FEAT), F32), sds((1, FEAT), F32)], *near_grads,
        scratch=held_scratch, us=3.0, limit=16,
    )
    parts = call(
        kernel_grad_body,
        sds((NZ, 128, FEAT)),
        *dense_groups, near_total, near_gain, *far_grads, own_part,
        scratch=held_scratch + [pltpu.VMEM((total_rows, FEAT), F32)],
        idle=(10,), pinned=(0,), us=5.0, limit=24,
    )
    z_parts = lax.all_to_all(
        parts, "gz", split_axis=0, concat_axis=0, axis_index_groups=Z_GROUPS, tiled=True
    )
    z_parts, got_up, got_down = lax.optimization_barrier((z_parts, got_up, got_down))
    conv_part, dense_sum = call(
        sum_body, [sds((112, FEAT)), sds((PTS, FEAT))], z_parts, us=1.0, limit=8,
    )
    conv_pair, dense_two = call(
        middle_body, [sds((112, FEAT)), sds((2, PTS, FEAT))],
        conv_part, lax.ppermute(conv_part, "grp", [(i, i ^ 1) for i in range(4)]), dense_sum, flip(dense_sum, 32),
        us=0.5, limit=8,
    )
    conv_pair, dense_two, got_up, got_down = lax.optimization_barrier((conv_pair, dense_two, got_up, got_down))
    grad_features = call(
        rim_body, sds((PTS, FEAT)), own_part, got_up, got_down, halo_rows,
        us=3.0, limit=8,
    )
    conv_other = lax.ppermute(conv_pair, "grp", [(i, i ^ 2) for i in range(4)])
    dense_more = flip(dense_two, 16)
    grad_conv, gain_sum, grad_qkv, grad_proj = call(
        lambda *refs: last_body(factor, *refs),
        [sds((108, FEAT), F32), sds((1, FEAT), F32), sds((FEAT, 3 * FEAT), F32), sds((FEAT, FEAT), F32)],
        conv_pair, conv_other, dense_two, dense_more, flip(dense_two, 1), flip(dense_more, 1),
        limit=8,
    )
    return (block_out, grad_features, grad_conv, grad_qkv, grad_proj, gain_sum.reshape(FEAT))


def solution(mesh):
    return jax.shard_map(
        shards,
        mesh=mesh,
        in_specs=(
            P(("grp", "gz"), None),
            P(("grp", "gz")),
            P(("grp", "gz"), None),
            P(("grp", "gz"), None),
            P(("grp", "gz"), None),
            P(),
            P(),
            P(),
            P(),
        ),
        out_specs=(P(("grp", "gz"), None), P(("grp", "gz"), None), P("gz", None), P(), P(), P()),
        check_vma=False,
    )
```
